32 devices in a mesh: dp: 8 (over z, y), seq: 4 (over x, core).
Axes of the slice: x: 2, y: 2, z: 4, core: 2. Of those that a mesh axis runs over, the one named last changes fastest.
Arguments:
- inputs: bfloat16 [16, 1024, 1280], P('dp', 'seq'), may hold values from -6 to 6
- w_query: bfloat16 [1280, 1280], P(('dp', 'seq')), may hold values from -0.15625 to 0.15625
- w_key: bfloat16 [1280, 1280], P(('dp', 'seq')), may hold values from -0.15625 to 0.15625
- w_value: bfloat16 [1280, 1280], P(('dp', 'seq')), may hold values from -0.15625 to 0.15625
- w_out: bfloat16 [1280, 1280], P(('dp', 'seq')), may hold values from -0.625 to 0.625
- w_up: bfloat16 [1280, 1280], P(('dp', 'seq')), may hold values from -0.15625 to 0.15625
- w_down: bfloat16 [1280, 1280], P(('dp', 'seq')), may hold values from -0.3125 to 0.3125
- gain_attn: bfloat16 [1280], P(('dp', 'seq')), may hold values from 0.099609375 to 1.8984375
- gain_mlp: bfloat16 [1280], P(('dp', 'seq')), may hold values from 0.099609375 to 1.8984375
- pad_patches: int32 [16], P('dp'), may hold values from 0 to 1023, as said below
- cotangent: bfloat16 [16, 1024, 1280], P('dp', 'seq'), may hold values from -6 to 6
Outputs:
- layer_out: bfloat16 [16, 1024, 1280], P('dp', 'seq')
- grad_input: float32 [16, 1024, 1280], P('dp', 'seq')
- grad_query: float32 [1280, 1280], P(('dp', 'seq'))
- grad_key: float32 [1280, 1280], P(('dp', 'seq'))
- grad_value: float32 [1280, 1280], P(('dp', 'seq'))
- grad_outproj: float32 [1280, 1280], P(('dp', 'seq'))
- grad_upproj: float32 [1280, 1280], P(('dp', 'seq'))
- grad_downproj: float32 [1280, 1280], P(('dp', 'seq'))
- grad_gain_attn: float32 [1280], P(('dp', 'seq'))
- grad_gain_mlp: float32 [1280], P(('dp', 'seq'))
The draws below stay inside these ranges and needn't reach their ends.
Inputs may be any that keep to these rules, and one draw needn't show every extreme that they name: `pad_patches`: in each group of 2 contexts held by one index of dp, one context has fewer than 256 padding patches. Some context has no padding and some has 1023 padding patches.
All inputs are finite; a program needn't handle non-finite values.
Results may differ from the reference program's by a relative error of at most 0.03.
Values may be sent and summed in bfloat16 or wider, within the bound.
A program may use at most 256 MiB of HBM per device.

```python
import math
import jax
import jax.numpy as jnp
from jax import lax

D = 1280
HEADS = 16
HEAD_DIM = 80
FF = 1280
LEN = 1024
SEQS = 2
PART = 256
CONTEXTS = 16
N_SEQ = 4


def draw_pad_patches(key, part):
    key = jax.random.fold_in(key, 7)
    key_base, key_slot, key_span, key_zero, key_most = jax.random.split(key, 5)
    group_count = CONTEXTS // SEQS
    base = jax.random.randint(key_base, (group_count, SEQS), 0, LEN)
    span_slot = jax.random.randint(key_slot, (group_count, 1), 0, SEQS)
    span_pad = jax.random.randint(key_span, (group_count, 1), 0, PART)
    zero_group = jax.random.randint(key_zero, (), 0, group_count)
    most_group = jax.random.randint(key_most, (), 0, group_count)
    column = jnp.arange(SEQS, dtype=jnp.int32)[None, :]
    row = jnp.arange(group_count, dtype=jnp.int32)[:, None]
    padded = jnp.where(column == span_slot, span_pad, base)
    padded = jnp.where((row == zero_group) & (column == span_slot), 0, padded)
    other_slot = (span_slot + 1) % SEQS
    padded = jnp.where((row == most_group) & (column == other_slot), LEN - 1, padded)
    return padded.reshape(CONTEXTS).astype(jnp.int32)


def block_scale(rng, shape, pieces, smallest, largest):
    factor_of = 1.0
    for dim, blocks in pieces:
        heights = jax.random.uniform(jax.random.fold_in(jax.random.fold_in(rng, 6), dim), (blocks,), jnp.float32, smallest / len(pieces), largest / len(pieces))
        factor_of = factor_of * jnp.repeat(jnp.exp(heights), shape[dim] // blocks).reshape((-1,) + (1,) * (len(shape) - 1 - dim))
    return factor_of


def gaussian(own_key, dims, spread, bound, cuts=(), held_as=jnp.bfloat16):
    entries = jax.random.normal(own_key, dims, jnp.float32) * spread
    if len(cuts) > 0:
        entries = block_scale(own_key, dims, cuts, -0.22, 0.18) * entries
    return jnp.clip(entries, min=-bound, max=bound).astype(held_as)


def setup_inputs(seed: int = 0) -> dict:
    splits = jax.random.split(jax.random.key(seed), 12)
    return {
        "inputs": gaussian(splits[0], (CONTEXTS, LEN, D), 1.0, 6.0, ((0, 8), (1, 4))),
        "w_query": gaussian(splits[1], (D, D), D ** -0.5, 0.15625, ((0, 32),)),
        "w_key": gaussian(splits[2], (D, D), D ** -0.5, 0.15625, ((0, 32),)),
        "w_value": gaussian(splits[3], (D, D), D ** -0.5, 0.15625, ((0, 32),)),
        "w_out": gaussian(splits[4], (D, D), (D // 16) ** -0.5, 0.625, ((0, 32),)),
        "w_up": gaussian(splits[5], (D, FF), D ** -0.5, 0.15625, ((0, 32),)),
        "w_down": gaussian(splits[6], (FF, D), (FF // 4) ** -0.5, 0.3125, ((0, 32),)),
        "gain_attn": jnp.clip(1.0 + 0.18 * jax.random.normal(splits[7], (D,), jnp.float32), 0.099609375, 1.8984375).astype(jnp.bfloat16),
        "gain_mlp": jnp.clip(1.0 + 0.18 * jax.random.normal(splits[8], (D,), jnp.float32), 0.099609375, 1.8984375).astype(jnp.bfloat16),
        "pad_patches": draw_pad_patches(jax.random.fold_in(splits[11], 71), 0),
        "cotangent": gaussian(splits[10], (CONTEXTS, LEN, D), 1.0, 6.0, ((0, 8), (1, 4))),
    }


@jax.custom_vjp
def low(v):
    return lax.optimization_barrier(v.astype(jnp.bfloat16)).astype(jnp.float32)

@jax.custom_vjp
def low_back(v):
    return v

def low_keep(v):
    return (low(v), None)

def low_pass(kept, grad):
    return (grad,)

def back_keep(v):
    return (v, None)

def back_low(kept, grad):
    return (low(grad),)
low.defvjp(low_keep, low_pass)
low_back.defvjp(back_keep, back_low)

def matmul_high(left, right):
    return jnp.dot(left, right, precision=lax.Precision.HIGHEST)

def rms_norm(values, gain):
    return values * lax.rsqrt(lax.optimization_barrier(jnp.mean(values * values, axis=-1, keepdims=True)) + 1e-06) * gain

def rope_tables(positions, half):
    freqs = 10000.0 ** (-jnp.arange(half, dtype=jnp.float32) / half)
    angles = positions[:, None].astype(jnp.float32) * freqs[None, :]
    return (jnp.cos(angles), jnp.sin(angles))

def rotate_pairs(tensor, cosine, sine):
    half = tensor.shape[-1] // 2
    first = tensor[..., :half]
    second = tensor[..., half:]
    cos_b = cosine[None, :, None, :]
    sin_b = sine[None, :, None, :]
    return jnp.concatenate([first * cos_b - second * sin_b, first * sin_b + second * cos_b], axis=-1)

def forward(inputs, w_query, w_key, w_value, w_out, w_up, w_down, gain_attn, gain_mlp, pad_group):
    groups = inputs.shape[0]
    blocks = N_SEQ
    patches = LEN // N_SEQ
    norm_attn = low(rms_norm(inputs, gain_attn))
    flat_attn = norm_attn.reshape(-1, D)
    shape_heads = (groups, LEN, HEADS, HEAD_DIM)
    query_lin = low_back(matmul_high(flat_attn, w_query)).reshape(shape_heads)
    key_lin = low_back(matmul_high(flat_attn, w_key)).reshape(shape_heads)
    value_heads = low(low_back(matmul_high(flat_attn, w_value))).reshape(shape_heads)
    positions = jnp.arange(LEN, dtype=jnp.int32)
    cosine, sine = rope_tables(positions, HEAD_DIM // 2)
    queries = low(rotate_pairs(query_lin, cosine, sine))
    key_heads = low(rotate_pairs(key_lin, cosine, sine))
    key_blocks = key_heads.reshape(groups, blocks, patches, HEADS, HEAD_DIM)
    value_blocks = value_heads.reshape(groups, blocks, patches, HEADS, HEAD_DIM)
    scale_factor = HEAD_DIM ** (-0.5)
    scores = low_back(scale_factor * jnp.einsum('gqhd,gbkhd->ghqbk', queries, key_blocks, precision=lax.Precision.HIGHEST))
    key_pos = positions.reshape(blocks, patches)
    query_grid = positions[None, :, None, None]
    key_grid = key_pos[None, None, :, :]
    allowed = (key_grid <= query_grid) & ((key_grid >= pad_group[:, None, None, None]) | (key_grid == query_grid))
    allowed = allowed[:, None]
    masked = jnp.where(allowed, scores, -1e+30)
    peaks = lax.optimization_barrier(jnp.max(masked, axis=-1))
    expo = jnp.exp(masked - peaks[..., None]) * allowed.astype(jnp.float32)
    masses = lax.optimization_barrier(jnp.sum(expo, axis=-1))
    partials = low_back(jnp.einsum('ghqbk,gbkhd->gqbhd', low(expo), value_blocks, precision=lax.Precision.HIGHEST))
    summit = lax.optimization_barrier(jnp.max(peaks, axis=-1))
    weights_blk = jnp.exp(peaks - summit[..., None])
    total = lax.optimization_barrier(jnp.sum(weights_blk * masses, axis=-1))
    weights_tok = jnp.transpose(weights_blk, (0, 2, 3, 1))[..., None]
    attended = lax.optimization_barrier(jnp.sum(weights_tok * partials, axis=2)) / jnp.transpose(total, (0, 2, 1))[..., None]
    attn_low = low(low_back(attended)).reshape(-1, D)
    branch = low_back(matmul_high(attn_low, w_out)).reshape(groups, LEN, D)
    hidden = inputs + branch
    norm_mlp = low(rms_norm(hidden, gain_mlp)).reshape(-1, D)
    upper = low_back(matmul_high(norm_mlp, w_up))
    active = low(jax.nn.silu(upper))
    mlp_out = low_back(matmul_high(active, w_down)).reshape(groups, LEN, D)
    return hidden + mlp_out

def reference(inputs, w_query, w_key, w_value, w_out, w_up, w_down, gain_attn, gain_mlp, pad_patches, cotangent):
    params = (w_query.astype(jnp.float32), w_key.astype(jnp.float32), w_value.astype(jnp.float32), w_out.astype(jnp.float32), w_up.astype(jnp.float32), w_down.astype(jnp.float32), gain_attn.astype(jnp.float32), gain_mlp.astype(jnp.float32))
    group_size = math.gcd(CONTEXTS, max(1, 2048 // LEN))
    group_count = CONTEXTS // group_size
    input_groups = inputs.astype(jnp.float32).reshape(group_count, group_size, LEN, D)
    cot_groups = cotangent.astype(jnp.float32).reshape(group_count, group_size, LEN, D)
    pad_groups = pad_patches.reshape(group_count, group_size)

    def group_step(carry, item):
        input_group, cot_group, pad_group = item

        def layer_of(input_value, *weights):
            return forward(input_value, *weights, pad_group)
        output_value, pullback = jax.vjp(layer_of, input_group, *params)
        grads = pullback(cot_group)
        summed = tuple((left + right for left, right in zip(carry, grads[1:])))
        return (summed, (output_value, grads[0]))
    init = tuple((jnp.zeros(weight.shape, jnp.float32) for weight in params))
    final, (outputs, grad_inputs) = lax.scan(group_step, init, (input_groups, cot_groups, pad_groups))
    layer_out = outputs.reshape(CONTEXTS, LEN, D).astype(jnp.bfloat16)
    grad_input = grad_inputs.reshape(CONTEXTS, LEN, D)
    return (layer_out, grad_input, final[0], final[1], final[2], final[3], final[4], final[5], final[6], final[7])
```

```python
import jax
import jax.numpy as jnp
from jax import lax
from jax.experimental import pallas as pl
from jax.experimental.pallas import tpu as pltpu
from jax.sharding import PartitionSpec as P

HEADS = 16
HEAD_DIM = 80


def shifted(value, axis, steps):
    count = lax.axis_size(axis)
    initial, last = (max(0, -steps), min(count, count - steps))
    return lax.ppermute(value, axis, [(source, source + steps) for source in range(initial, last)])


def rms_scale(values):
    return lax.rsqrt(jnp.mean(values * values, axis=-1, keepdims=True) + 1e-06)


def rms_back(values, scale, gain, grad_norm):
    scaled_grad = grad_norm * gain
    grad_gain = jnp.sum(grad_norm * values * scale, axis=0)
    grad_values = scale * scaled_grad - values * (scale * scale * scale) * jnp.mean(
        scaled_grad * values, axis=-1, keepdims=True
    )
    return (grad_values, grad_gain)


def rope_tables(positions, half):
    freqs = 10000.0 ** (-jnp.arange(half, dtype=jnp.float32) / half)
    angles = positions[:, None].astype(jnp.float32) * freqs[None, :]
    return (jnp.cos(angles), jnp.sin(angles))


def rotate_pairs(tensor, cosine, sine):
    half = tensor.shape[-1] // 2
    first = tensor[..., :half]
    second = tensor[..., half:]
    cos_b = cosine[None, :, None, :]
    sin_b = sine[None, :, None, :]
    return jnp.concatenate(
        [first * cos_b - second * sin_b, first * sin_b + second * cos_b], axis=-1
    )


def rotate_back(tensor, cosine, sine):
    half = tensor.shape[-1] // 2
    first = tensor[..., :half]
    second = tensor[..., half:]
    cos_b = cosine[None, :, None, :]
    sin_b = sine[None, :, None, :]
    return jnp.concatenate(
        [first * cos_b + second * sin_b, second * cos_b - first * sin_b], axis=-1
    )


def block_weights(queries, key_block, source, positions, pad_patches, patches):
    scale_factor = queries.shape[-1] ** (-0.5)
    scores = scale_factor * jnp.einsum(
        "sqhd,skhd->shqk", queries, key_block, preferred_element_type=jnp.float32
    )
    key_pos = source * patches + jnp.arange(patches, dtype=jnp.int32)
    key_grid = key_pos[None, None, :]
    query_grid = positions[None, :, None]
    allowed = (
        (key_grid <= query_grid)
        & ((key_grid >= pad_patches[:, None, None]) | (key_grid == query_grid))
        & (source >= 0)
    )
    allowed = allowed[:, None]
    masked = jnp.where(allowed, scores, -1e30)
    peaks = jnp.max(masked, axis=-1)
    expo = jnp.exp(masked - peaks[..., None]) * allowed.astype(jnp.float32)
    return (expo, peaks)


def block_forward(queries, key_block, value_block, source, positions, pad_patches, patches):
    expo, peaks = block_weights(queries, key_block, source, positions, pad_patches, patches)
    masses = jnp.sum(expo, axis=-1)
    partials = jnp.einsum(
        "shqk,skhd->sqhd",
        expo.astype(jnp.bfloat16),
        value_block,
        preferred_element_type=jnp.float32,
    )
    return (peaks, masses, partials)


def block_backward(
    queries,
    key_block,
    value_block,
    source,
    positions,
    pad_patches,
    patches,
    summit,
    total,
    delta,
    grad_attn,
):
    expo, peaks = block_weights(queries, key_block, source, positions, pad_patches, patches)
    share = jnp.exp(peaks - summit) / total
    share_tok = jnp.swapaxes(share, 1, 2)[..., None]
    grad_part = (share_tok * grad_attn).astype(jnp.bfloat16)
    grad_vblock = jnp.einsum(
        "shqk,sqhd->skhd", expo.astype(jnp.bfloat16), grad_part, preferred_element_type=jnp.float32
    )
    grad_prob = jnp.einsum(
        "sqhd,skhd->shqk", grad_part, value_block, preferred_element_type=jnp.float32
    )
    grad_scores = (expo * (grad_prob - (share * delta)[..., None])).astype(jnp.bfloat16)
    grad_qblock = jnp.einsum(
        "shqk,skhd->sqhd", grad_scores, key_block, preferred_element_type=jnp.float32
    )
    grad_kblock = jnp.einsum(
        "shqk,sqhd->skhd", grad_scores, queries, preferred_element_type=jnp.float32
    )
    return (grad_qblock, grad_kblock, grad_vblock)


MESH_ID = pl.DeviceIdType.MESH
CUT = 256


def coordinates():
    dp = lax.axis_index("dp")
    seq = lax.axis_index("seq")
    return (dp // 2, lax.rem(dp, 2), seq // 2, lax.rem(seq, 2))


def device(z, y, x, c):
    return (z * 2 + y, x * 2 + c)


def peers_of(z, y, x, c):
    along = [device(lax.rem(z + k, 4), y, x, c) for k in (1, 2, 3)]
    return along + [device(z, 1 - y, x, c), device(z, y, 1 - x, c), device(z, y, x, 1 - c)]


def greet(peers):
    barrier = pltpu.get_barrier_semaphore()
    for peer in peers:
        pl.semaphore_signal(barrier, inc=1, device_id=peer, device_id_type=MESH_ID)
    pl.semaphore_wait(barrier, len(peers))


def send(src, dst, sems, peer):
    copy = pltpu.make_async_remote_copy(
        src_ref=src,
        dst_ref=dst,
        send_sem=sems[0],
        recv_sem=sems[1],
        device_id=peer,
        device_id_type=MESH_ID,
    )
    copy.start()
    return copy


class Gather:
    def __init__(self, ref, cut, sems, where):
        self.ref, self.cut, self.sems, self.where = ref, cut, sems, where
        self.copies = [[], [], []]
        self.phase = 0

    def sem(self, i):
        return (self.sems[0].at[i], self.sems[1].at[i])

    def start(self):
        z, y, x, c = self.where
        ref, low, high = self.ref, pl.ds(0, self.cut), pl.ds(self.cut, self.ref.shape[-1] - self.cut)
        phase = self.phase
        made = []
        if phase == 0:
            blocks = [ref.at[z, y, x, :, low]] * 3 + [ref.at[z, y, x, :, high]]
            for k in (1, 2, 3):
                made.append(send(blocks[0], blocks[0], self.sem(k - 1), device(lax.rem(z + k, 4), y, x, c)))
            made.append(send(blocks[3], blocks[3], self.sem(3), device(z, y, 1 - x, c)))
        elif phase == 1:
            block = ref.at[:, y, x, :, low]
            made.append(send(block, block, self.sem(4), device(z, 1 - y, x, c)))
            block = ref.at[z, y, :, :, high]
            for k in (1, 2, 3):
                made.append(send(block, block, self.sem(4 + k), device(lax.rem(z + k, 4), y, x, c)))
        else:
            block = ref.at[:, :, x, :, low]
            made.append(send(block, block, self.sem(8), device(z, y, 1 - x, c)))
            block = ref.at[:, y, :, :, high]
            made.append(send(block, block, self.sem(9), device(z, 1 - y, x, c)))
        self.copies[phase] = made
        self.phase = phase + 1

    def arrive(self, phase):
        for copy in self.copies[phase]:
            copy.wait_recv()

    def sent(self):
        for made in self.copies:
            for copy in made:
                copy.wait_send()


class Scatter:
    def __init__(self, cut, bufs, sems, where):
        self.cut, self.bufs, self.sems, self.where = cut, bufs, sems, where
        self.copies = []

    def sem(self, i):
        return (self.sems[0].at[i], self.sems[1].at[i])

    def start(self, total):
        z, y, x, c = self.where
        b, cut = self.bufs, self.cut

        def fill(i, _):
            zi, yi = i // 2, lax.rem(i, 2)
            b["sa1"][zi, yi] = total[zi, yi, 1 - x, :, :cut].astype(jnp.bfloat16)
            b["sb1"][zi, yi] = total[zi, 1 - y, yi, :, cut:].astype(jnp.bfloat16)
            return 0

        lax.fori_loop(0, 8, fill, 0)
        self.first = [
            send(b["sa1"], b["ra1"], self.sem(0), device(z, y, 1 - x, c)),
            send(b["sb1"], b["rb1"], self.sem(1), device(z, 1 - y, x, c)),
        ]
        self.copies += self.first
        self.total = total

    def second(self):
        z, y, x, c = self.where
        b, cut, total = self.bufs, self.cut, self.total
        for copy in self.first:
            copy.wait_recv()

        def fill(zi, _):
            b["sa2"][zi] = (total[zi, 1 - y, x, :, :cut] + b["ra1"][zi, 1 - y].astype(jnp.float32)).astype(jnp.bfloat16)
            b["ka2"][zi] = total[zi, y, x, :, :cut] + b["ra1"][zi, y].astype(jnp.float32)
            for xi in range(2):
                value = total[zi, y, xi, :, cut:] + b["rb1"][zi, xi].astype(jnp.float32)
                b["sb2"][zi, xi] = value.astype(jnp.bfloat16)
                b["kb2"][zi, xi] = value
            return 0

        lax.fori_loop(0, 4, fill, 0)
        self.next = [send(b["sa2"], b["ra2"], self.sem(2), device(z, 1 - y, x, c))]
        for k in (1, 2, 3):
            other = lax.rem(z + k, 4)
            self.next.append(send(b["sb2"].at[other], b["rb2"].at[k - 1], self.sem(2 + k), device(other, y, x, c)))
        self.copies += self.next

    def third(self):
        z, y, x, c = self.where
        b = self.bufs
        for copy in self.next:
            copy.wait_recv()

        def fill(zi, _):
            value = b["ka2"][zi] + b["ra2"][zi].astype(jnp.float32)
            b["ka2"][zi] = value
            b["sa3"][zi] = value.astype(jnp.bfloat16)
            return 0

        lax.fori_loop(0, 4, fill, 0)

        def value_of(xi):
            value = b["kb2"][z, xi]
            for k in range(3):
                value = value + b["rb2"][k, xi].astype(jnp.float32)
            return value

        b["sb3"][...] = value_of(1 - x).astype(jnp.bfloat16)
        b["kb3"][...] = value_of(x)
        self.next = [send(b["sb3"], b["rb3"], self.sem(6), device(z, y, 1 - x, c))]
        for k in (1, 2, 3):
            other = lax.rem(z + k, 4)
            self.next.append(send(b["sa3"].at[other], b["ra3"].at[k - 1], self.sem(6 + k), device(other, y, x, c)))
        self.copies += self.next

    def finish(self, out):
        z, y, x, c = self.where
        b, cut = self.bufs, self.cut
        for copy in self.next:
            copy.wait_recv()
        left = b["ka2"][z]
        for k in range(3):
            left = left + b["ra3"][k].astype(jnp.float32)
        right = b["kb3"][...] + b["rb3"][...].astype(jnp.float32)
        half = left.shape[0] // 2
        for part in range(2):
            rows = slice(part * half, part * half + half)
            out[part, :, :cut] = left[rows]
            out[part, :, cut:] = right[rows]

    def sent(self):
        for copy in self.copies:
            copy.wait_send()


def scatter_buffers(rows, columns, cut, low):
    wide, rest = cut, columns - cut
    f32 = jnp.float32
    return {
        "sa1": pltpu.VMEM((4, 2, rows, wide), low),
        "ra1": pltpu.VMEM((4, 2, rows, wide), low),
        "sa2": pltpu.VMEM((4, rows, wide), low),
        "ra2": pltpu.VMEM((4, rows, wide), low),
        "ka2": pltpu.VMEM((4, rows, wide), f32),
        "sa3": pltpu.VMEM((4, rows, wide), low),
        "ra3": pltpu.VMEM((3, rows, wide), low),
        "sb1": pltpu.VMEM((4, 2, rows, rest), low),
        "rb1": pltpu.VMEM((4, 2, rows, rest), low),
        "sb2": pltpu.VMEM((4, 2, rows, rest), low),
        "rb2": pltpu.VMEM((3, 2, rows, rest), low),
        "kb2": pltpu.VMEM((4, 2, rows, rest), f32),
        "sb3": pltpu.VMEM((rows, rest), low),
        "rb3": pltpu.VMEM((rows, rest), low),
        "kb3": pltpu.VMEM((rows, rest), f32),
    }


def gather_kernel(*refs):
    weights, tile = refs[:6], refs[6]
    out, tiles = refs[7], refs[8]
    full, own, other, ssem, rsem, gs, gr, xs, osem = refs[9:]
    where = coordinates()
    z, y, x, c = where
    greet(peers_of(*where))
    for w in range(6):
        for h in range(2):
            own[h, w] = weights[w][:, 640 * h : 640 * h + 640].astype(jnp.float32)
    tiles[z, y, x, c] = tile[...]
    sibling = device(z, y, x, 1 - c)
    pair = send(own.at[1 - c], other, (xs.at[0], xs.at[1]), sibling)
    pair_tile = send(tiles.at[z, y, x, c], tiles.at[z, y, x, c], (xs.at[2], xs.at[3]), sibling)
    pair.wait_recv()
    pair_tile.wait_recv()
    steps = []
    for w in range(6):
        mine, theirs = own[c, w], other[w]
        first = c == 0
        block = jnp.concatenate([jnp.where(first, mine, theirs), jnp.where(first, theirs, mine)], axis=0)
        full[w, c, z, y, x] = block.astype(jnp.bfloat16)
        steps.append(Gather(full.at[w, c], CUT, (ssem.at[w], rsem.at[w]), where))
    shares = []
    stores = []
    sends = []

    def tile_step(i, block, peers):
        made = []
        for j, peer in enumerate(peers):
            made.append(send(block, block, (gs.at[i + j], gr.at[i + j]), peer))
        return made

    made = tile_step(0, tiles.at[z, y, x], [device(lax.rem(z + k, 4), y, x, c) for k in (1, 2, 3)])
    for t in range(6 + 4):
        if t < 6:
            steps[t].start()
        if 0 <= t - 1 < 6:
            steps[t - 1].arrive(0)
            steps[t - 1].start()
        if t == 1:
            for m in made:
                m.wait_recv()
            sends += made
            made = tile_step(3, tiles.at[:, y, x], [device(z, 1 - y, x, c)])
        if t == 2:
            for m in made:
                m.wait_recv()
            sends += made
            made = tile_step(4, tiles.at[:, :, x], [device(z, y, 1 - x, c)])
        if 0 <= t - 2 < 6:
            steps[t - 2].arrive(1)
            steps[t - 2].start()
        if 0 <= t - 3 < 6:
            w = t - 3
            steps[w].arrive(2)
            shares.append(send(full.at[w, c], full.at[w, c], (gs.at[5 + w], gr.at[5 + w]), sibling))
        if 0 <= t - 4 < 6:
            w = t - 4
            shares[w].wait_recv()
            store = pltpu.make_async_copy(full.at[w], out.at[w], osem.at[w])
            store.start()
            stores.append(store)
    for m in made:
        m.wait_recv()
    sends += made
    for item in steps:
        item.sent()
    for copy in shares + sends + [pair, pair_tile]:
        copy.wait_send()
    for store in stores:
        store.wait()


def gather_all(weights, tile):
    dma = pltpu.SemaphoreType.DMA
    return pl.pallas_call(
        gather_kernel,
        name="gather_weights",
        out_shape=(
            jax.ShapeDtypeStruct((6, 2, 4, 2, 2, 80, 640), jnp.bfloat16),
            jax.ShapeDtypeStruct((4, 2, 2, 2, 8, 128), jnp.float32),
        ),
        in_specs=[pl.BlockSpec(memory_space=pltpu.VMEM)] * 7,
        out_specs=(pl.BlockSpec(memory_space=pl.ANY), pl.BlockSpec(memory_space=pltpu.VMEM)),
        scratch_shapes=[
            pltpu.VMEM((6, 2, 4, 2, 2, 80, 640), jnp.bfloat16),
            pltpu.VMEM((2, 6, 40, 640), jnp.float32),
            pltpu.VMEM((6, 40, 640), jnp.float32),
            dma((6, 10)),
            dma((6, 10)),
            dma((11,)),
            dma((11,)),
            dma((4,)),
            dma((6,)),
        ],
        compiler_params=pltpu.CompilerParams(
            collective_id=0, has_side_effects=True, vmem_limit_bytes=56 << 20
        ),
    )(*weights, tile)


SEND = ("sa1", "sa2", "sa3", "sb1", "sb2", "sb3", "ka2", "kb2", "kb3")


def scatter_kernel(*refs):
    grads, tile = refs[:6], refs[6]
    outs, out_tile = refs[7], refs[8]
    big, low_send, low_recv, totals, fins, finr, lsem, ds, dr, ssem, rsem, fs, fr, tot, trecv, gs, gr = refs[9:26]
    names = list(scatter_buffers(8, 640, CUT, jnp.bfloat16))
    bufs = dict(zip(names, refs[26:]))
    where = coordinates()
    z, y, x, c = where
    greet(peers_of(*where))
    sibling = device(z, y, x, 1 - c)
    loads = [
        pltpu.make_async_copy(grads[i // 2].at[pl.ds(640 * (i % 2), 640)], big.at[i % 2], lsem.at[i])
        for i in range(12)
    ]
    loads[0].start()
    shared, fin, sends = [None] * 6, [], []
    parts = []
    for w in range(6):
        mine = {k: v.at[w % 4 if k in SEND else w] for k, v in bufs.items()}
        parts.append(Scatter(CUT, mine, (ssem.at[w], rsem.at[w]), where))
    def tile_pass(i):
        if i == 0:
            return [send(tile, trecv.at[0], (gs.at[0], gr.at[0]), sibling)]
        if i == 1:
            tot[...] = tile[...] + trecv[0]
            return [send(tot.at[:, :, 1 - x], trecv.at[1, :, :, 0], (gs.at[1], gr.at[1]), device(z, y, 1 - x, c))]
        if i == 2:
            tot[:, :, x] = tot[:, :, x] + trecv[1, :, :, 0]
            return [send(tot.at[:, 1 - y, x], trecv.at[2, :, 0, 0], (gs.at[2], gr.at[2]), device(z, 1 - y, x, c))]
        if i == 3:
            tot[:, y, x] = tot[:, y, x] + trecv[2, :, 0, 0]
            made = []
            for k in (1, 2, 3):
                other = lax.rem(z + k, 4)
                made.append(send(tot.at[other, y, x], trecv.at[3, k, 0, 0], (gs.at[2 + k], gr.at[2 + k]), device(other, y, x, c)))
            return made
        out_tile[...] = tot[z, y, x] + trecv[3, 1, 0, 0] + trecv[3, 2, 0, 0] + trecv[3, 3, 0, 0]
        return []

    made = []
    for t in range(6 + 5):
        if t < 5:
            for m in made:
                m.wait_recv()
            sends += made
            made = tile_pass(t)
        if t < 6:
            w, slot = t, t % 2
            if w >= 2:
                shared[w - 2].wait_send()
            if w >= 4:
                parts[w - 4].sent()
            for half in range(2):
                i = 2 * w + half
                if i + 1 < 12:
                    loads[i + 1].start()
                loads[i].wait()

                def fill(j, _):
                    rows = pl.ds(pl.multiple_of(j * 80, 80), 80)
                    left, right = big[half, rows, :640], big[half, rows, 640:]
                    first = c == 0
                    totals[w % 3, half * 8 + j] = jnp.where(first, left, right)
                    low_send[slot, half * 8 + j] = jnp.where(first, right, left).astype(jnp.bfloat16)
                    return 0

                lax.fori_loop(0, 8, fill, 0)
            shared[w] = send(low_send.at[slot], low_recv.at[w], (ds.at[w], dr.at[w]), sibling)
        if 0 <= t - 1 < 6:
            w = t - 1
            shared[w].wait_recv()

            def add(i, _):
                totals[w % 3, i] = totals[w % 3, i] + low_recv[w, i].astype(jnp.float32)
                return 0

            lax.fori_loop(0, 16, add, 0)
            parts[w].start(totals.at[w % 3].reshape(4, 2, 2, 80, 640))
        if 0 <= t - 2 < 6:
            parts[t - 2].second()
        if 0 <= t - 3 < 6:
            parts[t - 3].third()
        if 0 <= t - 4 < 6:
            w = t - 4
            parts[w].finish(fins.at[w])
            fin.append(send(fins.at[w, 1 - c], finr.at[w], (fs.at[w], fr.at[w]), sibling))
        if 0 <= t - 5 < 6:
            w = t - 5
            fin[w].wait_recv()
            mine, theirs = fins[w, c], finr[w]
            first = c == 0
            outs[w, :, :640] = jnp.where(first, mine, theirs)
            outs[w, :, 640:] = jnp.where(first, theirs, mine)
    for part in parts[2:]:
        part.sent()
    for copy in shared[4:] + fin + sends:
        copy.wait_send()


def scatter_all(grads, tile):
    dma = pltpu.SemaphoreType.DMA
    low, f32 = jnp.bfloat16, jnp.float32
    bufs = {}
    for k, v in scatter_buffers(80, 640, CUT, low).items():
        bufs[k] = pltpu.VMEM((4 if k in SEND else 6,) + v.shape, v.dtype)
    return pl.pallas_call(
        scatter_kernel,
        name="scatter_grads",
        out_shape=(
            jax.ShapeDtypeStruct((6, 40, 1280), f32),
            jax.ShapeDtypeStruct((8, 128), f32),
        ),
        in_specs=[pl.BlockSpec(memory_space=pl.ANY)] * 6 + [pl.BlockSpec(memory_space=pltpu.VMEM)],
        out_specs=(pl.BlockSpec(memory_space=pltpu.VMEM), pl.BlockSpec(memory_space=pltpu.VMEM)),
        scratch_shapes=[
            pltpu.VMEM((2, 640, 1280), f32),
            pltpu.VMEM((2, 16, 80, 640), low),
            pltpu.VMEM((6, 16, 80, 640), low),
            pltpu.VMEM((3, 16, 80, 640), f32),
            pltpu.VMEM((6, 2, 40, 640), f32),
            pltpu.VMEM((6, 40, 640), f32),
            dma((12,)), dma((6,)), dma((6,)), dma((6, 10)), dma((6, 10)), dma((6,)), dma((6,)),
            pltpu.VMEM((4, 2, 2, 8, 128), f32),
            pltpu.VMEM((4, 4, 2, 2, 8, 128), f32),
            dma((6,)), dma((6,)),
        ] + list(bufs.values()),
        compiler_params=pltpu.CompilerParams(
            collective_id=1, has_side_effects=True, vmem_limit_bytes=60 << 20
        ),
    )(*grads, tile)


def body(
    inputs,
    w_query,
    w_key,
    w_value,
    w_out,
    w_up,
    w_down,
    gain_attn,
    gain_mlp,
    pad_patches,
    cotangent,
):
    contexts, patches, model_width = inputs.shape
    head_count = HEADS
    head_size = HEAD_DIM
    seq_count = lax.axis_size("seq")
    seq_rank = lax.axis_index("seq")
    token_rows = contexts * patches
    shape_heads = (contexts, patches, head_count, head_size)
    shape_flat = (contexts, patches, model_width)
    shards = (w_query, w_key, w_value, w_out, w_up, w_down, gain_attn, gain_mlp)
    gathered = (
        lax.all_gather(shards[0], ("dp", "seq"), axis=0, tiled=True),
        lax.all_gather(shards[1], ("dp", "seq"), axis=0, tiled=True),
        lax.all_gather(shards[2], ("dp", "seq"), axis=0, tiled=True),
        lax.all_gather(shards[3], ("dp", "seq"), axis=0, tiled=True),
        lax.all_gather(shards[4], ("dp", "seq"), axis=0, tiled=True),
        lax.all_gather(shards[5], ("dp", "seq"), axis=0, tiled=True),
        lax.all_gather(shards[6], ("dp", "seq"), axis=0, tiled=True),
        lax.all_gather(shards[7], ("dp", "seq"), axis=0, tiled=True),
    )
    full_q, full_k, full_v, full_o, full_up, full_down, full_ga, full_gm = gathered
    positions = seq_rank * patches + jnp.arange(patches, dtype=jnp.int32)
    cosine, sine = rope_tables(positions, head_size // 2)
    inputs_f = inputs.astype(jnp.float32).reshape(token_rows, model_width)
    gain_one = full_ga.astype(jnp.float32)
    scale_one = rms_scale(inputs_f)
    flat_attn = (inputs_f * scale_one * gain_one).astype(jnp.bfloat16)
    query_lin = jnp.dot(flat_attn, full_q, preferred_element_type=jnp.float32).reshape(shape_heads)
    key_lin = jnp.dot(flat_attn, full_k, preferred_element_type=jnp.float32).reshape(shape_heads)
    value_flat = jnp.dot(flat_attn, full_v, preferred_element_type=jnp.float32).astype(jnp.bfloat16)
    queries = rotate_pairs(query_lin, cosine, sine).astype(jnp.bfloat16)
    key_flat = rotate_pairs(key_lin, cosine, sine).astype(jnp.bfloat16)
    own_blocks = (key_flat.reshape(shape_flat), value_flat.reshape(shape_flat))
    kept = []
    sources = []
    current = own_blocks
    for offset in range(seq_count):
        if offset > 0:
            current = shifted((current[0], current[1]), "seq", 1)
        kept.append(current)
        sources.append(seq_rank - offset)
    stats = []
    for block_pair, source_idx in zip(kept, sources):
        stats.append(
            block_forward(
                queries,
                block_pair[0].reshape(shape_heads),
                block_pair[1].reshape(shape_heads),
                source_idx,
                positions,
                pad_patches,
                patches,
            )
        )
    peaks = jnp.stack([entry[0] for entry in stats])
    masses = jnp.stack([entry[1] for entry in stats])
    partials = jnp.stack([entry[2] for entry in stats])
    summit = jnp.max(peaks, axis=0)
    weights_blk = jnp.exp(peaks - summit[None])
    total = jnp.sum(weights_blk * masses, axis=0)
    attended = (
        jnp.sum(jnp.swapaxes(weights_blk, 2, 3)[..., None] * partials, axis=0)
        / jnp.swapaxes(total, 1, 2)[..., None]
    )
    attn_low = attended.astype(jnp.bfloat16).reshape(token_rows, model_width)
    branch = jnp.dot(attn_low, full_o, preferred_element_type=jnp.float32)
    hidden = inputs_f + branch
    gain_two = full_gm.astype(jnp.float32)
    scale_two = rms_scale(hidden)
    norm_mlp = (hidden * scale_two * gain_two).astype(jnp.bfloat16)
    upper = jnp.dot(norm_mlp, full_up, preferred_element_type=jnp.float32)
    active = jax.nn.silu(upper).astype(jnp.bfloat16)
    mlp_out = jnp.dot(active, full_down, preferred_element_type=jnp.float32)
    layer_out = (hidden + mlp_out).astype(jnp.bfloat16).reshape(shape_flat)
    back_q, back_k, back_v, back_o, back_up, back_down, back_ga, back_gm = gathered
    cot_low = cotangent.reshape(token_rows, model_width)
    cot_full = cot_low.astype(jnp.float32)
    grad_downw = jnp.dot(active.T, cot_low, preferred_element_type=jnp.float32)
    grad_active = jnp.dot(cot_low, back_down.T, preferred_element_type=jnp.float32)
    sigmoid_up = jax.nn.sigmoid(upper)
    grad_upper = (grad_active * sigmoid_up * (1.0 + upper * (1.0 - sigmoid_up))).astype(
        jnp.bfloat16
    )
    grad_upw = jnp.dot(norm_mlp.T, grad_upper, preferred_element_type=jnp.float32)
    grad_norm_mlp = jnp.dot(grad_upper, back_up.T, preferred_element_type=jnp.float32)
    grad_from_mlp, grad_gain_two = rms_back(
        hidden, scale_two, back_gm.astype(jnp.float32), grad_norm_mlp
    )
    grad_hidden = cot_full + grad_from_mlp
    hid_low = grad_hidden.astype(jnp.bfloat16)
    grad_outw = jnp.dot(attn_low.T, hid_low, preferred_element_type=jnp.float32)
    grad_attn = jnp.dot(hid_low, back_o.T, preferred_element_type=jnp.float32).astype(jnp.bfloat16)
    grad_attn_f = grad_attn.astype(jnp.float32).reshape(shape_heads)
    delta = jnp.swapaxes(jnp.sum(grad_attn_f * attended, axis=-1), 1, 2)
    grad_queries = jnp.zeros(shape_heads, jnp.float32)
    carried = (jnp.zeros(shape_flat, jnp.float32), jnp.zeros(shape_flat, jnp.float32))
    for offset in reversed(range(seq_count)):
        block_pair = kept[offset]
        part_q, part_k, part_v = block_backward(
            queries,
            block_pair[0].reshape(shape_heads),
            block_pair[1].reshape(shape_heads),
            sources[offset],
            positions,
            pad_patches,
            patches,
            summit,
            total,
            delta,
            grad_attn_f,
        )
        grad_queries = grad_queries + part_q
        carried = (carried[0] + part_k.reshape(shape_flat), carried[1] + part_v.reshape(shape_flat))
        if offset > 0:
            carried = (
                shifted(carried[0].astype(jnp.bfloat16), "seq", -1).astype(jnp.float32),
                shifted(carried[1].astype(jnp.bfloat16), "seq", -1).astype(jnp.float32),
            )
    grad_keys, grad_values = carried
    scale_factor = head_size ** (-0.5)
    grad_qlin = (
        rotate_back(grad_queries * scale_factor, cosine, sine)
        .astype(jnp.bfloat16)
        .reshape(token_rows, model_width)
    )
    grad_klin = (
        rotate_back(grad_keys.reshape(shape_heads) * scale_factor, cosine, sine)
        .astype(jnp.bfloat16)
        .reshape(token_rows, model_width)
    )
    grad_vlin = grad_values.astype(jnp.bfloat16).reshape(token_rows, model_width)
    grad_qw = jnp.dot(flat_attn.T, grad_qlin, preferred_element_type=jnp.float32)
    grad_kw = jnp.dot(flat_attn.T, grad_klin, preferred_element_type=jnp.float32)
    grad_vw = jnp.dot(flat_attn.T, grad_vlin, preferred_element_type=jnp.float32)
    grad_norm_attn = jnp.dot(grad_qlin, back_q.T, preferred_element_type=jnp.float32)
    grad_norm_attn = grad_norm_attn + jnp.dot(
        grad_klin, back_k.T, preferred_element_type=jnp.float32
    )
    grad_norm_attn = grad_norm_attn + jnp.dot(
        grad_vlin, back_v.T, preferred_element_type=jnp.float32
    )
    grad_from_attn, grad_gain_one = rms_back(
        inputs_f, scale_one, back_ga.astype(jnp.float32), grad_norm_attn
    )
    grad_input = (grad_hidden + grad_from_attn).reshape(shape_flat)
    totals = (
        lax.psum_scatter(grad_qw, ("dp", "seq"), scatter_dimension=0, tiled=True),
        lax.psum_scatter(grad_kw, ("dp", "seq"), scatter_dimension=0, tiled=True),
        lax.psum_scatter(grad_vw, ("dp", "seq"), scatter_dimension=0, tiled=True),
        lax.psum_scatter(grad_outw, ("dp", "seq"), scatter_dimension=0, tiled=True),
        lax.psum_scatter(grad_upw, ("dp", "seq"), scatter_dimension=0, tiled=True),
        lax.psum_scatter(grad_downw, ("dp", "seq"), scatter_dimension=0, tiled=True),
        lax.psum_scatter(grad_gain_one, ("dp", "seq"), scatter_dimension=0, tiled=True),
        lax.psum_scatter(grad_gain_two, ("dp", "seq"), scatter_dimension=0, tiled=True),
    )
    return (
        layer_out,
        grad_input,
        totals[0],
        totals[1],
        totals[2],
        totals[3],
        totals[4],
        totals[5],
        totals[6],
        totals[7],
    )


def fast_body(
    inputs,
    w_query,
    w_key,
    w_value,
    w_out,
    w_up,
    w_down,
    gain_attn,
    gain_mlp,
    pad_patches,
    cotangent,
):
    contexts, patches, model_width = inputs.shape
    head_count = HEADS
    head_size = HEAD_DIM
    seq_count = lax.axis_size("seq")
    seq_rank = lax.axis_index("seq")
    token_rows = contexts * patches
    shape_heads = (contexts, patches, head_count, head_size)
    shape_flat = (contexts, patches, model_width)
    shards = (w_query, w_key, w_value, w_out, w_up, w_down, gain_attn, gain_mlp)
    tile = jnp.pad(jnp.stack([gain_attn, gain_mlp]).astype(jnp.float32), ((0, 6), (0, 88)))
    gathered_w, tiles = gather_all(shards[:6], tile)
    gathered_w = jnp.concatenate([gathered_w[:, 0], gathered_w[:, 1]], axis=-1).reshape(6, 1280, 1280)
    gains = tiles.reshape(32, 8, 128)[:, :2, :40].swapaxes(0, 1).reshape(2, 1280)
    gathered = tuple(gathered_w[i] for i in range(6)) + (gains[0], gains[1])
    full_q, full_k, full_v, full_o, full_up, full_down, full_ga, full_gm = gathered
    positions = seq_rank * patches + jnp.arange(patches, dtype=jnp.int32)
    cosine, sine = rope_tables(positions, head_size // 2)
    inputs_f = inputs.astype(jnp.float32).reshape(token_rows, model_width)
    gain_one = full_ga.astype(jnp.float32)
    scale_one = rms_scale(inputs_f)
    flat_attn = (inputs_f * scale_one * gain_one).astype(jnp.bfloat16)
    query_lin = jnp.dot(flat_attn, full_q, preferred_element_type=jnp.float32).reshape(shape_heads)
    key_lin = jnp.dot(flat_attn, full_k, preferred_element_type=jnp.float32).reshape(shape_heads)
    value_flat = jnp.dot(flat_attn, full_v, preferred_element_type=jnp.float32).astype(jnp.bfloat16)
    queries = rotate_pairs(query_lin, cosine, sine).astype(jnp.bfloat16)
    key_flat = rotate_pairs(key_lin, cosine, sine).astype(jnp.bfloat16)
    own_blocks = (key_flat.reshape(shape_flat), value_flat.reshape(shape_flat))
    kept = []
    sources = []
    current = own_blocks
    for offset in range(seq_count):
        if offset > 0:
            current = shifted((current[0], current[1]), "seq", 1)
        kept.append(current)
        sources.append(seq_rank - offset)
    stats = []
    for block_pair, source_idx in zip(kept, sources):
        stats.append(
            block_forward(
                queries,
                block_pair[0].reshape(shape_heads),
                block_pair[1].reshape(shape_heads),
                source_idx,
                positions,
                pad_patches,
                patches,
            )
        )
    peaks = jnp.stack([entry[0] for entry in stats])
    masses = jnp.stack([entry[1] for entry in stats])
    partials = jnp.stack([entry[2] for entry in stats])
    summit = jnp.max(peaks, axis=0)
    weights_blk = jnp.exp(peaks - summit[None])
    total = jnp.sum(weights_blk * masses, axis=0)
    attended = (
        jnp.sum(jnp.swapaxes(weights_blk, 2, 3)[..., None] * partials, axis=0)
        / jnp.swapaxes(total, 1, 2)[..., None]
    )
    attn_low = attended.astype(jnp.bfloat16).reshape(token_rows, model_width)
    branch = jnp.dot(attn_low, full_o, preferred_element_type=jnp.float32)
    hidden = inputs_f + branch
    gain_two = full_gm.astype(jnp.float32)
    scale_two = rms_scale(hidden)
    norm_mlp = (hidden * scale_two * gain_two).astype(jnp.bfloat16)
    upper = jnp.dot(norm_mlp, full_up, preferred_element_type=jnp.float32)
    active = jax.nn.silu(upper).astype(jnp.bfloat16)
    mlp_out = jnp.dot(active, full_down, preferred_element_type=jnp.float32)
    layer_out = (hidden + mlp_out).astype(jnp.bfloat16).reshape(shape_flat)
    back_q, back_k, back_v, back_o, back_up, back_down, back_ga, back_gm = gathered
    cot_low = cotangent.reshape(token_rows, model_width)
    cot_full = cot_low.astype(jnp.float32)
    grad_downw = jnp.dot(active.T, cot_low, preferred_element_type=jnp.float32)
    grad_active = jnp.dot(cot_low, back_down.T, preferred_element_type=jnp.float32)
    sigmoid_up = jax.nn.sigmoid(upper)
    grad_upper = (grad_active * sigmoid_up * (1.0 + upper * (1.0 - sigmoid_up))).astype(
        jnp.bfloat16
    )
    grad_upw = jnp.dot(norm_mlp.T, grad_upper, preferred_element_type=jnp.float32)
    grad_norm_mlp = jnp.dot(grad_upper, back_up.T, preferred_element_type=jnp.float32)
    grad_from_mlp, grad_gain_two = rms_back(
        hidden, scale_two, back_gm.astype(jnp.float32), grad_norm_mlp
    )
    grad_hidden = cot_full + grad_from_mlp
    hid_low = grad_hidden.astype(jnp.bfloat16)
    grad_outw = jnp.dot(attn_low.T, hid_low, preferred_element_type=jnp.float32)
    grad_attn = jnp.dot(hid_low, back_o.T, preferred_element_type=jnp.float32).astype(jnp.bfloat16)
    grad_attn_f = grad_attn.astype(jnp.float32).reshape(shape_heads)
    delta = jnp.swapaxes(jnp.sum(grad_attn_f * attended, axis=-1), 1, 2)
    grad_queries = jnp.zeros(shape_heads, jnp.float32)
    carried = (jnp.zeros(shape_flat, jnp.float32), jnp.zeros(shape_flat, jnp.float32))
    for offset in reversed(range(seq_count)):
        block_pair = kept[offset]
        part_q, part_k, part_v = block_backward(
            queries,
            block_pair[0].reshape(shape_heads),
            block_pair[1].reshape(shape_heads),
            sources[offset],
            positions,
            pad_patches,
            patches,
            summit,
            total,
            delta,
            grad_attn_f,
        )
        grad_queries = grad_queries + part_q
        carried = (carried[0] + part_k.reshape(shape_flat), carried[1] + part_v.reshape(shape_flat))
        if offset > 0:
            carried = (
                shifted(carried[0].astype(jnp.bfloat16), "seq", -1).astype(jnp.float32),
                shifted(carried[1].astype(jnp.bfloat16), "seq", -1).astype(jnp.float32),
            )
    grad_keys, grad_values = carried
    scale_factor = head_size ** (-0.5)
    grad_qlin = (
        rotate_back(grad_queries * scale_factor, cosine, sine)
        .astype(jnp.bfloat16)
        .reshape(token_rows, model_width)
    )
    grad_klin = (
        rotate_back(grad_keys.reshape(shape_heads) * scale_factor, cosine, sine)
        .astype(jnp.bfloat16)
        .reshape(token_rows, model_width)
    )
    grad_vlin = grad_values.astype(jnp.bfloat16).reshape(token_rows, model_width)
    grad_qw = jnp.dot(flat_attn.T, grad_qlin, preferred_element_type=jnp.float32)
    grad_kw = jnp.dot(flat_attn.T, grad_klin, preferred_element_type=jnp.float32)
    grad_vw = jnp.dot(flat_attn.T, grad_vlin, preferred_element_type=jnp.float32)
    grad_norm_attn = jnp.dot(grad_qlin, back_q.T, preferred_element_type=jnp.float32)
    grad_norm_attn = grad_norm_attn + jnp.dot(
        grad_klin, back_k.T, preferred_element_type=jnp.float32
    )
    grad_norm_attn = grad_norm_attn + jnp.dot(
        grad_vlin, back_v.T, preferred_element_type=jnp.float32
    )
    grad_from_attn, grad_gain_one = rms_back(
        inputs_f, scale_one, back_ga.astype(jnp.float32), grad_norm_attn
    )
    grad_input = (grad_hidden + grad_from_attn).reshape(shape_flat)
    gain_tile = jnp.stack([grad_gain_one, grad_gain_two]).reshape(2, 16, 80).swapaxes(0, 1)
    gain_tile = jnp.pad(gain_tile, ((0, 0), (0, 6), (0, 48))).reshape(4, 2, 2, 8, 128)
    sums, tile_sum = scatter_all((grad_qw, grad_kw, grad_vw, grad_outw, grad_upw, grad_downw), gain_tile)
    own_gain = lax.dynamic_slice(tile_sum, (0, 40 * (seq_rank % 2)), (2, 40))
    totals = tuple(sums[i] for i in range(6)) + (own_gain[0], own_gain[1])
    return (
        layer_out,
        grad_input,
        totals[0],
        totals[1],
        totals[2],
        totals[3],
        totals[4],
        totals[5],
        totals[6],
        totals[7],
    )


def solution(mesh):
    placed = (
        P("dp", "seq", None),
        P(("dp", "seq"), None),
        P(("dp", "seq"), None),
        P(("dp", "seq"), None),
        P(("dp", "seq"), None),
        P(("dp", "seq"), None),
        P(("dp", "seq"), None),
        P(("dp", "seq")),
        P(("dp", "seq")),
        P("dp"),
        P("dp", "seq", None),
    )
    return jax.shard_map(
        fast_body if dict(mesh.shape) == {"dp": 8, "seq": 4} else body,
        mesh=mesh,
        in_specs=placed,
        out_specs=(
            P("dp", "seq", None),
            P("dp", "seq", None),
            P(("dp", "seq"), None),
            P(("dp", "seq"), None),
            P(("dp", "seq"), None),
            P(("dp", "seq"), None),
            P(("dp", "seq"), None),
            P(("dp", "seq"), None),
            P(("dp", "seq")),
            P(("dp", "seq")),
        ),
        check_vma=False,
    )
```

```python
import jax
import jax.numpy as jnp
import numpy as np
from jax import lax
from jax.experimental import pallas as pl
from jax.experimental.pallas import tpu as pltpu
from jax.sharding import PartitionSpec as P

HEADS = 16
HEAD_DIM = 80


def shifted(value, axis, steps):
    count = lax.axis_size(axis)
    initial, last = (max(0, -steps), min(count, count - steps))
    return lax.ppermute(value, axis, [(source, source + steps) for source in range(initial, last)])


def rms_scale(values):
    return lax.rsqrt(jnp.mean(values * values, axis=-1, keepdims=True) + 1e-06)


def rms_back(values, scale, gain, grad_norm):
    scaled_grad = grad_norm * gain
    grad_gain = jnp.sum(grad_norm * values * scale, axis=0)
    grad_values = scale * scaled_grad - values * (scale * scale * scale) * jnp.mean(
        scaled_grad * values, axis=-1, keepdims=True
    )
    return (grad_values, grad_gain)


def rope_tables(positions, half):
    freqs = 10000.0 ** (-jnp.arange(half, dtype=jnp.float32) / half)
    angles = positions[:, None].astype(jnp.float32) * freqs[None, :]
    return (jnp.cos(angles), jnp.sin(angles))


def rotate_pairs(tensor, cosine, sine):
    half = tensor.shape[-1] // 2
    first = tensor[..., :half]
    second = tensor[..., half:]
    cos_b = cosine[None, :, None, :]
    sin_b = sine[None, :, None, :]
    return jnp.concatenate(
        [first * cos_b - second * sin_b, first * sin_b + second * cos_b], axis=-1
    )


def rotate_back(tensor, cosine, sine):
    half = tensor.shape[-1] // 2
    first = tensor[..., :half]
    second = tensor[..., half:]
    cos_b = cosine[None, :, None, :]
    sin_b = sine[None, :, None, :]
    return jnp.concatenate(
        [first * cos_b + second * sin_b, second * cos_b - first * sin_b], axis=-1
    )


def block_weights(queries, key_block, source, positions, pad_patches, patches):
    scale_factor = queries.shape[-1] ** (-0.5)
    scores = scale_factor * jnp.einsum(
        "sqhd,skhd->shqk", queries, key_block, preferred_element_type=jnp.float32
    )
    key_pos = source * patches + jnp.arange(patches, dtype=jnp.int32)
    key_grid = key_pos[None, None, :]
    query_grid = positions[None, :, None]
    allowed = (
        (key_grid <= query_grid)
        & ((key_grid >= pad_patches[:, None, None]) | (key_grid == query_grid))
        & (source >= 0)
    )
    allowed = allowed[:, None]
    masked = jnp.where(allowed, scores, -1e30)
    peaks = jnp.max(masked, axis=-1)
    expo = jnp.exp(masked - peaks[..., None]) * allowed.astype(jnp.float32)
    return (expo, peaks)


def block_forward(queries, key_block, value_block, source, positions, pad_patches, patches):
    expo, peaks = block_weights(queries, key_block, source, positions, pad_patches, patches)
    masses = jnp.sum(expo, axis=-1)
    partials = jnp.einsum(
        "shqk,skhd->sqhd",
        expo.astype(jnp.bfloat16),
        value_block,
        preferred_element_type=jnp.float32,
    )
    return (peaks, masses, partials)


def block_backward(
    queries,
    key_block,
    value_block,
    source,
    positions,
    pad_patches,
    patches,
    summit,
    total,
    delta,
    grad_attn,
):
    expo, peaks = block_weights(queries, key_block, source, positions, pad_patches, patches)
    share = jnp.exp(peaks - summit) / total
    share_tok = jnp.swapaxes(share, 1, 2)[..., None]
    grad_part = (share_tok * grad_attn).astype(jnp.bfloat16)
    grad_vblock = jnp.einsum(
        "shqk,sqhd->skhd", expo.astype(jnp.bfloat16), grad_part, preferred_element_type=jnp.float32
    )
    grad_prob = jnp.einsum(
        "sqhd,skhd->shqk", grad_part, value_block, preferred_element_type=jnp.float32
    )
    grad_scores = (expo * (grad_prob - (share * delta)[..., None])).astype(jnp.bfloat16)
    grad_qblock = jnp.einsum(
        "shqk,skhd->sqhd", grad_scores, key_block, preferred_element_type=jnp.float32
    )
    grad_kblock = jnp.einsum(
        "shqk,sqhd->skhd", grad_scores, queries, preferred_element_type=jnp.float32
    )
    return (grad_qblock, grad_kblock, grad_vblock)


MESH_ID = pl.DeviceIdType.MESH
CUT = 256


def coordinates():
    dp = lax.axis_index("dp")
    seq = lax.axis_index("seq")
    return (dp // 2, lax.rem(dp, 2), seq // 2, lax.rem(seq, 2))


def device(z, y, x, c):
    return (z * 2 + y, x * 2 + c)


def peers_of(z, y, x, c):
    along = [device(lax.rem(z + k, 4), y, x, c) for k in (1, 2, 3)]
    return along + [device(z, 1 - y, x, c), device(z, y, 1 - x, c), device(z, y, x, 1 - c)]


def greet(peers):
    barrier = pltpu.get_barrier_semaphore()
    for peer in peers:
        pl.semaphore_signal(barrier, inc=1, device_id=peer, device_id_type=MESH_ID)
    pl.semaphore_wait(barrier, len(peers))


def send(src, dst, sems, peer):
    copy = pltpu.make_async_remote_copy(
        src_ref=src,
        dst_ref=dst,
        send_sem=sems[0],
        recv_sem=sems[1],
        device_id=peer,
        device_id_type=MESH_ID,
    )
    copy.start()
    return copy


class Gather:
    def __init__(self, ref, cut, sems, where):
        self.ref, self.cut, self.sems, self.where = ref, cut, sems, where
        self.copies = [[], [], []]
        self.phase = 0

    def sem(self, i):
        return (self.sems[0].at[i], self.sems[1].at[i])

    def start(self):
        z, y, x, c = self.where
        ref, low, high = self.ref, pl.ds(0, self.cut), pl.ds(self.cut, self.ref.shape[-1] - self.cut)
        phase = self.phase
        made = []
        if phase == 0:
            blocks = [ref.at[z, y, x, :, low]] * 3 + [ref.at[z, y, x, :, high]]
            for k in (1, 2, 3):
                made.append(send(blocks[0], blocks[0], self.sem(k - 1), device(lax.rem(z + k, 4), y, x, c)))
            made.append(send(blocks[3], blocks[3], self.sem(3), device(z, y, 1 - x, c)))
        elif phase == 1:
            block = ref.at[:, y, x, :, low]
            made.append(send(block, block, self.sem(4), device(z, 1 - y, x, c)))
            block = ref.at[z, y, :, :, high]
            for k in (1, 2, 3):
                made.append(send(block, block, self.sem(4 + k), device(lax.rem(z + k, 4), y, x, c)))
        else:
            block = ref.at[:, :, x, :, low]
            made.append(send(block, block, self.sem(8), device(z, y, 1 - x, c)))
            block = ref.at[:, y, :, :, high]
            made.append(send(block, block, self.sem(9), device(z, 1 - y, x, c)))
        self.copies[phase] = made
        self.phase = phase + 1

    def arrive(self, phase):
        for copy in self.copies[phase]:
            copy.wait_recv()

    def sent(self):
        for made in self.copies:
            for copy in made:
                copy.wait_send()


HEADS_HERE = 8
SPAN = 256
OFFSETS = (0, 256, 768, 1536, 2560)
NT = (((1,), (1,)), ((), ()))
TN = (((0,), (0,)), ((), ()))


def dot(a, b, dims=(((1,), (0,)), ((), ()))):
    return lax.dot_general(a, b, dims, preferred_element_type=jnp.float32)


def unpack_gains(tiles):
    rows = []
    for z in range(4):
        for y in range(2):
            for x in range(2):
                for c in range(2):
                    rows.append(tiles[z, y, x, c][:, :40])
    full = jnp.concatenate(rows, axis=1)
    return full[0:1], full[1:2]


def turn(value, cosine, sine):
    half = 40
    zeros = jnp.zeros((value.shape[0], 48), jnp.float32)
    for h in range(HEADS_HERE):
        a = value[:, 80 * h : 80 * h + half]
        b = value[:, 80 * h + half : 80 * h + 80]
        yield h, jnp.concatenate([a * cosine - b * sine, a * sine + b * cosine, zeros], axis=1)


def forward_kernel(*refs):
    (inputs, cot), weights, tile, pads, cos_ref, sin_ref = refs[:2], refs[2:8], refs[8], refs[9], refs[10], refs[11]
    (out_qkv, out_o, out_up, out_down, tiles, x_own, dy_own, norm_t, out_heads, out_p, out_oh, out_al) = refs[12:24]
    (full, own, other, held, norm, normt, heads, probs, oh, flat, masks,
     ssem, rsem, gs, gr, xs, osem, ws, wr, ns, nr, ls, ps, als, alr) = refs[24:]
    where = coordinates()
    z, y, x, c = where
    f32, low = jnp.float32, jnp.bfloat16
    across, sibling = device(z, y, 1 - x, c), device(z, y, x, 1 - c)
    keep = pltpu.make_async_copy(inputs.at[x], held.at[x], ls.at[0])
    keep.start()
    keep_dy = pltpu.make_async_copy(cot.at[x], dy_own.at[x], ls.at[1])
    keep_dy.start()
    greet(peers_of(*where))
    swap = send(inputs.at[1 - x], held.at[x * 0 + x], (ws.at[0], wr.at[0]), across)
    for w in range(6):
        for h in range(2):
            own[h, w] = weights[w][:, 640 * h : 640 * h + 640].astype(f32)
    tiles[z, y, x, c] = tile[...]
    pair = send(own.at[1 - c], other, (xs.at[0], xs.at[1]), sibling)
    pair_tile = send(tiles.at[z, y, x, c], tiles.at[z, y, x, c], (xs.at[2], xs.at[3]), sibling)
    pair.wait_recv()
    pair_tile.wait_recv()
    steps, shares, stores, sends = [], {}, [], [swap, pair, pair_tile]
    for w in range(6):
        mine, theirs = own[c, w], other[w]
        first = c == 0
        block = jnp.concatenate([jnp.where(first, mine, theirs), jnp.where(first, theirs, mine)], axis=0)
        full[w, c, z, y, x] = block.astype(low)
        steps.append(Gather(full.at[w, c], CUT, (ssem.at[w], rsem.at[w]), where))

    def tile_step(i, block, peers):
        return [send(block, block, (gs.at[i + j], gr.at[i + j]), peer) for j, peer in enumerate(peers)]

    state = {"made": tile_step(0, tiles.at[z, y, x], [device(lax.rem(z + k, 4), y, x, c) for k in (1, 2, 3)])}

    def store(src, dst, sem):
        copy = pltpu.make_async_copy(src, dst, sem)
        copy.start()
        stores.append(copy)

    full_out = {3: out_o, 4: out_up, 5: out_down}

    def settle(w):
        if w < 3:
            store(full.at[w, c], out_qkv.at[w], osem.at[w])
            return
        columns = pl.ds(pl.multiple_of(640 * c, 128), 640)
        store(full.at[w, c], full_out[w].at[:, :, :, :, columns], osem.at[w])
        shares[w] = send(full.at[w, c], full_out[w].at[:, :, :, :, columns], (gs.at[5 + w], gr.at[5 + w]), sibling)

    def advance(t):
        if t < 6:
            steps[t].start()
        if 0 <= t - 1 < 6:
            steps[t - 1].arrive(0)
            steps[t - 1].start()
        if t in (1, 2, 3):
            for m in state["made"]:
                m.wait_recv()
            sends.extend(state["made"])
            state["made"] = []
        if t == 1:
            state["made"] = tile_step(3, tiles.at[:, y, x], [device(z, 1 - y, x, c)])
        if t == 2:
            state["made"] = tile_step(4, tiles.at[:, :, x], [device(z, y, 1 - x, c)])
        if 0 <= t - 2 < 6:
            steps[t - 2].arrive(1)
            steps[t - 2].start()
        if 0 <= t - 3 < 6:
            steps[t - 3].arrive(2)
            settle(t - 3)

    advance(0)
    pad = pads[x]
    row = lax.broadcasted_iota(jnp.int32, (SPAN, SPAN), 0)
    col = lax.broadcasted_iota(jnp.int32, (SPAN, SPAN), 1)
    for i in range(4):
        good = (col <= row) & ((col + SPAN * i >= pad) | (col == row))
        masks[i] = jnp.where(good, 0.0, -1e30).astype(f32)
    before = jnp.where(lax.broadcasted_iota(jnp.int32, (1, 3 * SPAN), 1) >= pad, 0.0, -1e30).astype(f32)
    advance(1)
    advance(2)
    swap_dy = send(cot.at[1 - x], dy_own.at[x], (ws.at[1], wr.at[1]), across)
    sends.append(swap_dy)
    advance(3)
    keep.wait()
    swap.wait_recv()
    gain_attn, _ = unpack_gains(tiles)
    passed = []
    for j in range(2):
        value = held[j].astype(f32)
        scale = lax.rsqrt(jnp.mean(value * value, axis=-1, keepdims=True) + 1e-06)
        block = 2 * j + c
        norm[block] = (value * scale * gain_attn).astype(low)
        passed.append(send(norm.at[block], norm.at[block], (ns.at[j], nr.at[j]), sibling))
    store(held, x_own, ls.at[2])
    for copy in passed:
        copy.wait_recv()
    sends.extend(passed)

    def project(t):
        def step(b, _):
            rows = pl.ds(pl.multiple_of(b * SPAN, SPAN), SPAN)
            matrix = full[t, c].reshape(1280, 640)
            value = dot(norm[b], matrix)
            if t < 2:
                for h, turned in turn(value, cos_ref[rows, :40], sin_ref[rows, :40]):
                    if t == 0:
                        turned = turned * (80.0**-0.5)
                    heads[t, h, rows, :] = turned.astype(low)
            else:
                zeros = jnp.zeros((SPAN, 48), f32)
                for h in range(HEADS_HERE):
                    padded = jnp.concatenate([value[:, 80 * h : 80 * h + 80], zeros], axis=1)
                    heads[t, h, rows, :] = padded.astype(low)
            if t == 0:
                normt[:, rows] = jnp.transpose(norm[b])
            return 0

        lax.fori_loop(0, 4, step, 0)

    project(0)
    store(normt, norm_t, ls.at[3])
    advance(4)
    project(1)
    advance(5)
    project(2)
    store(heads, out_heads, ls.at[4])

    def attend(h, _):
        slot = lax.rem(h, 2)

        @pl.when(h >= 2)
        def _():
            pltpu.make_async_copy(probs.at[slot], out_p.at[h - 2], ps.at[slot]).wait()

        for i in range(4):
            n = SPAN * (i + 1)
            rows = slice(SPAN * i, SPAN * i + SPAN)
            score = dot(heads[0, h, rows, :], heads[1, h, :n, :], NT)
            last = score[:, n - SPAN :] + masks[i]
            score = last if i == 0 else jnp.concatenate([score[:, : n - SPAN] + before[:, : n - SPAN], last], axis=1)
            peak = jnp.max(score, axis=-1, keepdims=True)
            expo = jnp.exp(score - peak)
            share = (expo * (1.0 / jnp.sum(expo, axis=-1, keepdims=True))).astype(low)
            probs[slot, :, OFFSETS[i] : OFFSETS[i + 1]] = share
            oh[h, rows, :] = dot(share, heads[2, h, :n, :]).astype(low)
        pltpu.make_async_copy(probs.at[slot], out_p.at[h], ps.at[slot]).start()
        return 0

    lax.fori_loop(0, 3, attend, 0)
    advance(6)
    lax.fori_loop(3, 6, attend, 0)
    advance(7)
    lax.fori_loop(6, 8, attend, 0)
    store(oh, out_oh, ls.at[5])

    def flatten(b, _):
        rows = pl.ds(pl.multiple_of(b * SPAN, SPAN), SPAN)
        parts = [oh[h, rows, :].astype(f32)[:, :80] for h in range(HEADS_HERE)]
        flat[b] = jnp.concatenate(parts, axis=1).astype(low)
        return 0

    lax.fori_loop(0, 4, flatten, 0)
    columns = pl.ds(pl.multiple_of(640 * c, 128), 640)
    joined = []
    for j in range(2):
        store(flat.at[2 * j + c], out_al.at[j, :, columns], ls.at[6 + j])
        joined.append(send(flat.at[2 * j + 1 - c], out_al.at[j, :, columns], (als.at[j], alr.at[j]), sibling))
    advance(8)
    for h in (6, 7):
        pltpu.make_async_copy(probs.at[h % 2], out_p.at[h], ps.at[h % 2]).wait()
    for copy in joined:
        copy.wait_recv()
    swap_dy.wait_recv()
    keep_dy.wait()
    for w in (3, 4, 5):
        shares[w].wait()
    for item in steps:
        item.sent()
    for copy in sends + joined:
        copy.wait_send()
    for copy in stores:
        copy.wait()


def forward_part(inputs, cot, weights, tile, pads, cosine, sine):
    dma = pltpu.SemaphoreType.DMA
    low, f32 = jnp.bfloat16, jnp.float32
    shape = jax.ShapeDtypeStruct
    vmem, anywhere = pl.BlockSpec(memory_space=pltpu.VMEM), pl.BlockSpec(memory_space=pl.ANY)
    wide = shape((4, 2, 2, 80, 1280), low)
    return pl.pallas_call(
        forward_kernel,
        name="gather_attend",
        out_shape=(
            shape((3, 4, 2, 2, 80, 640), low),
            wide,
            wide,
            wide,
            shape((4, 2, 2, 2, 8, 128), f32),
            shape((2, 256, 1280), low),
            shape((2, 256, 1280), low),
            shape((1280, 1024), low),
            shape((3, 8, 1024, 128), low),
            shape((8, 256, 2560), low),
            shape((8, 1024, 128), low),
            shape((2, 256, 1280), low),
        ),
        in_specs=[anywhere] * 2 + [vmem] * 7 + [pl.BlockSpec(memory_space=pltpu.SMEM)] + [vmem] * 2,
        out_specs=(anywhere,) * 4 + (vmem,) + (anywhere,) * 7,
        scratch_shapes=[
            pltpu.VMEM((6, 2, 4, 2, 2, 80, 640), low),
            pltpu.VMEM((2, 6, 40, 640), f32),
            pltpu.VMEM((6, 40, 640), f32),
            pltpu.VMEM((2, 256, 1280), low),
            pltpu.VMEM((4, 256, 1280), low),
            pltpu.VMEM((1280, 1024), low),
            pltpu.VMEM((3, 8, 1024, 128), low),
            pltpu.VMEM((2, 256, 2560), low),
            pltpu.VMEM((8, 1024, 128), low),
            pltpu.VMEM((4, 256, 640), low),
            pltpu.VMEM((4, 256, 256), f32),
            dma((6, 10)), dma((6, 10)), dma((11,)), dma((11,)), dma((4,)), dma((6,)),
            dma((2,)), dma((2,)), dma((2,)), dma((2,)), dma((8,)), dma((2,)), dma((2,)), dma((2,)),
        ],
        compiler_params=pltpu.CompilerParams(
            collective_id=0, has_side_effects=True, vmem_limit_bytes=58 << 20
        ),
    )(inputs, cot, *weights, tile, pads, cosine, sine)


class Scatter:
    def __init__(self, ref, cut, bufs, sems, where):
        self.ref, self.cut, self.bufs, self.sems, self.where = ref, cut, bufs, sems, where
        self.low, self.high = pl.ds(0, cut), pl.ds(cut, ref.shape[-1] - cut)
        self.copies = []
        self.next = []

    def sem(self, i):
        return (self.sems[0].at[i], self.sems[1].at[i])

    def post(self, copies):
        self.next = copies
        self.copies += copies

    def arrive(self):
        for copy in self.next:
            copy.wait_recv()

    def start(self):
        z, y, x, c = self.where
        ref, b = self.ref, self.bufs
        self.post([
            send(ref.at[:, :, 1 - x, :, self.low], b["a1"], self.sem(0), device(z, y, 1 - x, c)),
            send(ref.at[:, 1 - y, :, :, self.high], b["b1"], self.sem(1), device(z, 1 - y, x, c)),
        ])

    def second(self):
        z, y, x, c = self.where
        ref, b, cut = self.ref, self.bufs, self.cut
        f32, low = jnp.float32, jnp.bfloat16
        self.arrive()

        def fold(i, _):
            zi, yi = i // 2, lax.rem(i, 2)
            ref[zi, yi, x, :, :cut] = (ref[zi, yi, x, :, :cut].astype(f32) + b["a1"][zi, yi].astype(f32)).astype(low)
            ref[zi, y, yi, :, cut:] = (ref[zi, y, yi, :, cut:].astype(f32) + b["b1"][zi, yi].astype(f32)).astype(low)
            return 0

        lax.fori_loop(0, 8, fold, 0)
        made = [send(ref.at[:, 1 - y, x, :, self.low], b["a2"], self.sem(2), device(z, 1 - y, x, c))]
        for k in (1, 2, 3):
            other = lax.rem(z + k, 4)
            made.append(send(ref.at[other, y, :, :, self.high], b["b2"].at[k - 1], self.sem(2 + k), device(other, y, x, c)))
        self.post(made)

    def third(self):
        z, y, x, c = self.where
        ref, b, cut = self.ref, self.bufs, self.cut
        f32, low = jnp.float32, jnp.bfloat16
        self.arrive()

        def fold(zi, _):
            ref[zi, y, x, :, :cut] = (ref[zi, y, x, :, :cut].astype(f32) + b["a2"][zi].astype(f32)).astype(low)
            return 0

        lax.fori_loop(0, 4, fold, 0)
        value = ref[z, y, 1 - x, :, cut:].astype(f32)
        for k in range(3):
            value = value + b["b2"][k, 1 - x].astype(f32)
        ref[z, y, 1 - x, :, cut:] = value.astype(low)
        made = [send(ref.at[z, y, 1 - x, :, self.high], b["b3"], self.sem(6), device(z, y, 1 - x, c))]
        for k in (1, 2, 3):
            other = lax.rem(z + k, 4)
            made.append(send(ref.at[other, y, x, :, self.low], b["a3"].at[k - 1], self.sem(6 + k), device(other, y, x, c)))
        self.post(made)

    def finish(self, out):
        z, y, x, c = self.where
        ref, b, cut = self.ref, self.bufs, self.cut
        f32 = jnp.float32
        self.arrive()
        left = ref[z, y, x, :, :cut].astype(f32)
        right = ref[z, y, x, :, cut:].astype(f32) + b["b3"][...].astype(f32)
        for k in range(3):
            left = left + b["a3"][k].astype(f32)
            right = right + b["b2"][k, x].astype(f32)
        half = left.shape[0] // 2
        for part in range(2):
            rows = slice(part * half, part * half + half)
            out[part, :, :cut] = left[rows]
            out[part, :, cut:] = right[rows]

    def sent(self):
        for copy in self.copies:
            copy.wait_send()
        self.copies = []


def scatter_buffers(rows, columns, cut, low):
    rest = columns - cut
    return {
        "a1": (4, 2, rows, cut),
        "a2": (4, rows, cut),
        "a3": (3, rows, cut),
        "b1": (4, 2, rows, rest),
        "b2": (3, 2, rows, rest),
        "b3": (rows, rest),
    }


SLOTS = 4


def backward_kernel(*refs):
    (layer, gattn, ghid, gmlp, dw_down, dw_up, dw_out, weights_in, tiles, x_own, norm_t, heads_in, p_in, oh_in,
     cos_ref, sin_ref) = refs[:16]
    (out_layer, out_input, o_q, o_k, o_v, o_o, o_up, o_down, o_ga, o_gm) = refs[16:26]
    (sums, extra, heads, probs, oh, doh, flat_in, acc, flat, normt, xs_own, hid, part_send, part_recv,
     in_send, in_recv, in_own, fins, finr, tot, trecv,
     ls, es, er, ss, sr, fs, fr, gs, gr, ps, qs, qr, ts, tr, ys, yr, os) = refs[26:64]
    names = list(scatter_buffers(8, 640, CUT, None))
    bufs = dict(zip(names, refs[64:]))
    where = coordinates()
    z, y, x, c = where
    f32, low = jnp.float32, jnp.bfloat16
    across, sibling = device(z, y, 1 - x, c), device(z, y, x, 1 - c)
    mine = pl.ds(pl.multiple_of(640 * c, 128), 640)
    yours = pl.ds(pl.multiple_of(640 * (1 - c), 128), 640)
    sends, locals_ = [], []

    def local(src, dst, sem):
        copy = pltpu.make_async_copy(src, dst, sem)
        copy.start()
        return copy

    load_sums = [local(dw.at[:, :, :, :, mine], sums.at[n], ls.at[n]) for n, dw in enumerate((dw_down, dw_up, dw_out))]
    load_flat = [local(gattn.at[j, :, mine], flat_in.at[2 * j + c], ls.at[3 + j]) for j in range(2)]
    load_heads = local(heads_in, heads, ls.at[5])
    load_oh = local(oh_in, oh, ls.at[6])
    load_normt = local(norm_t, normt, ls.at[7])
    load_x = local(x_own, xs_own, ls.at[9])
    load_hid = local(ghid, hid, ls.at[10])
    own_layer = local(layer.at[x], out_layer.at[x], ls.at[11])

    def fetch(h, slot):
        return pltpu.make_async_copy(p_in.at[h], probs.at[slot], ps.at[slot])

    fetch(0, 0).start()
    greet(peers_of(*where))
    moved = [send(gattn.at[j, :, yours], flat_in.at[2 * j + c], (es.at[j], er.at[j]), sibling) for j in range(2)]
    given = []
    for n, dw in enumerate((dw_down, dw_up, dw_out)):
        given.append(send(dw.at[:, :, :, :, yours], extra.at[n], (es.at[2 + n], er.at[2 + n]), sibling))
    sends += moved + given
    parts = []
    for n in range(6):
        held = {k: v.at[n] for k, v in bufs.items()}
        parts.append(Scatter(sums.at[n % SLOTS], CUT, held, (ss.at[n], sr.at[n]), where))
    outs = (o_down, o_up, o_o, o_v, o_k, o_q)
    crossing = []

    def advance(t):
        if t < 6:
            if t < 3:
                load_sums[t].wait()
                given[t].wait_recv()

                def fold(i, _):
                    zi, yi = i // 2, lax.rem(i, 2)
                    for xi in range(2):
                        value = sums[t, zi, yi, xi].astype(f32) + extra[t, zi, yi, xi].astype(f32)
                        sums[t, zi, yi, xi] = value.astype(low)
                    return 0

                lax.fori_loop(0, 8, fold, 0)
            parts[t].start()
        if 0 <= t - 1 < 6:
            parts[t - 1].second()
        if 0 <= t - 2 < 6:
            parts[t - 2].third()
        if 0 <= t - 3 < 6:
            n = t - 3
            parts[n].finish(fins.at[n])
            parts[n].sent()
            crossing.append(send(fins.at[n, 1 - c], finr.at[n], (fs.at[n], fr.at[n]), sibling))
        if 0 <= t - 4 < 6:
            n = t - 4
            crossing[n].wait_recv()
            own, theirs, first = fins[n, c], finr[n], c == 0
            outs[n][:, :640] = jnp.where(first, own, theirs)
            outs[n][:, 640:] = jnp.where(first, theirs, own)

    advance(0)
    for copy in load_flat:
        copy.wait()
    for copy in moved:
        copy.wait_recv()

    def spread(b, _):
        rows = pl.ds(pl.multiple_of(b * SPAN, SPAN), SPAN)
        value = flat_in[b].astype(f32)
        zeros = jnp.zeros((SPAN, 48), f32)
        for h in range(HEADS_HERE):
            doh[h, rows, :] = jnp.concatenate([value[:, 80 * h : 80 * h + 80], zeros], axis=1).astype(low)
        return 0

    lax.fori_loop(0, 4, spread, 0)
    load_heads.wait()
    load_oh.wait()

    def turn_back(value, rows):
        cosine, sine = cos_ref[rows, :40], sin_ref[rows, :40]
        a, b = value[:, :40], value[:, 40:80]
        zeros = jnp.zeros((value.shape[0], 48), f32)
        return jnp.concatenate([a * cosine + b * sine, b * cosine - a * sine, zeros], axis=1)

    def attend(h, _):
        slot = lax.rem(h, 2)

        @pl.when(h < 7)
        def _():
            fetch(h + 1, 1 - slot).start()

        fetch(h, slot).wait()
        for i in range(4):
            n = SPAN * (i + 1)
            rows = slice(SPAN * i, SPAN * i + SPAN)
            grad = doh[h, rows, :]
            delta = jnp.sum(grad.astype(f32) * oh[h, rows, :].astype(f32), axis=-1, keepdims=True)
            share = probs[slot, :, OFFSETS[i] : OFFSETS[i + 1]]
            grad_share = dot(grad, heads[2, h, :n, :], NT)
            grad_score = (share.astype(f32) * (grad_share - delta)).astype(low)
            grad_query = dot(grad_score, heads[1, h, :n, :]) * (80.0**-0.5)
            grad_key = dot(grad_score, heads[0, h, rows, :], TN)
            grad_value = dot(share, grad, TN)
            heads[0, h, rows, :] = turn_back(grad_query, rows).astype(low)
            if i > 0:
                acc[0, : n - SPAN] = acc[0, : n - SPAN] + grad_key[: n - SPAN]
                acc[1, : n - SPAN] = acc[1, : n - SPAN] + grad_value[: n - SPAN]
            acc[0, n - SPAN : n] = grad_key[n - SPAN :]
            acc[1, n - SPAN : n] = grad_value[n - SPAN :]
        for i in range(4):
            rows = slice(SPAN * i, SPAN * i + SPAN)
            heads[1, h, rows, :] = turn_back(acc[0, rows, :], rows).astype(low)
            heads[2, h, rows, :] = acc[1, rows, :].astype(low)
        return 0

    lax.fori_loop(0, 3, attend, 0)
    advance(1)
    lax.fori_loop(3, 6, attend, 0)
    advance(2)
    weights = extra
    load_weights = local(weights_in, weights, ls.at[8])
    lax.fori_loop(6, 8, attend, 0)
    load_normt.wait()

    def product(t, n):
        def join(b, _):
            rows = pl.ds(pl.multiple_of(b * SPAN, SPAN), SPAN)
            pieces = [heads[t, h, rows, :].astype(f32)[:, :80] for h in range(HEADS_HERE)]
            flat[t, rows, :] = jnp.concatenate(pieces, axis=1).astype(low)
            return 0

        lax.fori_loop(0, 4, join, 0)

        def step(zi, _):
            rows = pl.ds(pl.multiple_of(zi * 320, 320), 320)
            value = dot(normt[rows, :], flat[t]).astype(low)
            sums[n % SLOTS, zi] = value.reshape(2, 2, 80, 640)
            return 0

        lax.fori_loop(0, 4, step, 0)

    product(2, 3)
    advance(3)
    product(1, 4)
    advance(4)
    product(0, 5)
    advance(5)
    load_weights.wait()

    def norm_grad(block):
        rows = pl.ds(pl.multiple_of(block * SPAN, SPAN), SPAN)
        total = dot(flat[0, rows, :], weights[0].reshape(1280, 640), NT)
        for t in (1, 2):
            total = total + dot(flat[t, rows, :], weights[t].reshape(1280, 640), NT)
        return total

    def theirs_step(j, _):
        part_send[j] = norm_grad(2 * j + 1 - c).astype(low)
        return 0

    lax.fori_loop(0, 2, theirs_step, 0)
    swapped = [send(part_send.at[j], part_recv.at[j], (qs.at[j], qr.at[j]), sibling) for j in range(2)]
    sends += swapped
    gain_attn, _ = unpack_gains(tiles)
    load_x.wait()
    load_hid.wait()
    for copy in swapped:
        copy.wait_recv()

    def input_grad(j):
        grad_norm = norm_grad(2 * j + c) + part_recv[j].astype(f32)
        value = xs_own[j].astype(f32)
        scale = lax.rsqrt(jnp.mean(value * value, axis=-1, keepdims=True) + 1e-06)
        scaled = grad_norm * gain_attn
        mean = jnp.mean(scaled * value, axis=-1, keepdims=True)
        grad_gain = jnp.sum(grad_norm * value * scale, axis=0, keepdims=True)
        return hid[j] + scale * scaled - value * (scale * scale * scale) * mean, grad_gain

    result, gain_far = input_grad(1 - x)
    in_send[...] = result.astype(low)
    back = send(in_send, in_recv, (ys.at[0], yr.at[0]), across)
    back_layer = send(layer.at[1 - x], out_layer.at[x], (ys.at[1], yr.at[1]), across)
    sends += [back, back_layer]
    result, gain_near = input_grad(x)
    in_own[...] = result
    own_input = local(in_own, out_input.at[x], os.at[0])
    gain_sum = gain_far + gain_near
    mlp_sum = gmlp[...]
    for p in range(16):
        spot = (p // 4, (p // 2) % 2, p % 2)
        tot[spot[0], spot[1], spot[2], 0:1, 0:80] = gain_sum[:, 80 * p : 80 * p + 80]
        tot[spot[0], spot[1], spot[2], 1:2, 0:80] = mlp_sum[:, 80 * p : 80 * p + 80]
    hop = [send(tot, trecv.at[0], (gs.at[0], gr.at[0]), sibling)]
    advance(6)
    for copy in hop:
        copy.wait()
    tot[...] = tot[...] + trecv[0]
    hop = [send(tot.at[:, :, 1 - x], trecv.at[1, :, :, 0], (gs.at[1], gr.at[1]), device(z, y, 1 - x, c))]
    sends += hop
    advance(7)
    for copy in hop:
        copy.wait_recv()
    tot[:, :, x] = tot[:, :, x] + trecv[1, :, :, 0]
    hop = [send(tot.at[:, 1 - y, x], trecv.at[2, :, 0, 0], (gs.at[2], gr.at[2]), device(z, 1 - y, x, c))]
    sends += hop
    back.wait_recv()
    in_own_far = in_recv[...].astype(f32)
    own_input.wait()
    in_own[...] = in_own_far
    far_input = local(in_own, out_input.at[1 - x], os.at[1])
    advance(8)
    for copy in hop:
        copy.wait_recv()
    tot[:, y, x] = tot[:, y, x] + trecv[2, :, 0, 0]
    hop = []
    for k in (1, 2, 3):
        other = lax.rem(z + k, 4)
        hop.append(send(tot.at[other, y, x], trecv.at[3, k, 0, 0], (gs.at[2 + k], gr.at[2 + k]), device(other, y, x, c)))
    sends += hop
    advance(9)
    for copy in hop:
        copy.wait_recv()
    summed = tot[z, y, x] + trecv[3, 1, 0, 0] + trecv[3, 2, 0, 0] + trecv[3, 3, 0, 0]
    chosen = jnp.where(c == 0, summed[:, :40], summed[:, 40:80])
    o_ga[...] = chosen[0:1]
    o_gm[...] = chosen[1:2]
    far_input.wait()
    own_layer.wait()
    back_layer.wait_recv()
    for copy in sends + crossing:
        copy.wait_send()


def backward_part(layer, gattn, ghid, gmlp, dws, weights, tiles, x_own, norm_t, heads, p, oh, cosine, sine):
    dma = pltpu.SemaphoreType.DMA
    low, f32 = jnp.bfloat16, jnp.float32
    shape = jax.ShapeDtypeStruct
    vmem, anywhere = pl.BlockSpec(memory_space=pltpu.VMEM), pl.BlockSpec(memory_space=pl.ANY)
    row = shape((40, 1280), f32)
    bufs = [pltpu.VMEM((6,) + v, low) for v in scatter_buffers(80, 640, CUT, low).values()]
    return pl.pallas_call(
        backward_kernel,
        name="attend_back_scatter",
        out_shape=(shape((2, 256, 1280), low), shape((2, 256, 1280), f32)) + (row,) * 6 + (shape((1, 40), f32),) * 2,
        in_specs=[anywhere] * 3 + [vmem] + [anywhere] * 4 + [vmem] + [anywhere] * 5 + [vmem] * 2,
        out_specs=(anywhere,) * 2 + (vmem,) * 8,
        scratch_shapes=[
            pltpu.VMEM((SLOTS, 4, 2, 2, 80, 640), low),
            pltpu.VMEM((3, 4, 2, 2, 80, 640), low),
            pltpu.VMEM((3, 8, 1024, 128), low),
            pltpu.VMEM((2, 256, 2560), low),
            pltpu.VMEM((8, 1024, 128), low),
            pltpu.VMEM((8, 1024, 128), low),
            pltpu.VMEM((4, 256, 640), low),
            pltpu.VMEM((2, 1024, 128), f32),
            pltpu.VMEM((3, 1024, 640), low),
            pltpu.VMEM((1280, 1024), low),
            pltpu.VMEM((2, 256, 1280), low),
            pltpu.VMEM((2, 256, 1280), f32),
            pltpu.VMEM((2, 256, 1280), low),
            pltpu.VMEM((2, 256, 1280), low),
            pltpu.VMEM((256, 1280), low),
            pltpu.VMEM((256, 1280), low),
            pltpu.VMEM((256, 1280), f32),
            pltpu.VMEM((6, 2, 40, 640), f32),
            pltpu.VMEM((6, 40, 640), f32),
            pltpu.VMEM((4, 2, 2, 8, 128), f32),
            pltpu.VMEM((4, 4, 2, 2, 8, 128), f32),
            dma((12,)), dma((5,)), dma((5,)), dma((6, 10)), dma((6, 10)), dma((6,)), dma((6,)), dma((6,)), dma((6,)),
            dma((2,)), dma((2,)), dma((2,)), dma((2,)), dma((2,)), dma((2,)), dma((2,)), dma((2,)),
        ] + bufs,
        compiler_params=pltpu.CompilerParams(
            collective_id=1, has_side_effects=True, vmem_limit_bytes=62 << 20
        ),
    )(layer, gattn, ghid, gmlp, *dws, weights, tiles, x_own, norm_t, heads, p, oh, cosine, sine)


def body(
    inputs,
    w_query,
    w_key,
    w_value,
    w_out,
    w_up,
    w_down,
    gain_attn,
    gain_mlp,
    pad_patches,
    cotangent,
):
    contexts, patches, model_width = inputs.shape
    head_count = HEADS
    head_size = HEAD_DIM
    seq_count = lax.axis_size("seq")
    seq_rank = lax.axis_index("seq")
    token_rows = contexts * patches
    shape_heads = (contexts, patches, head_count, head_size)
    shape_flat = (contexts, patches, model_width)
    shards = (w_query, w_key, w_value, w_out, w_up, w_down, gain_attn, gain_mlp)
    gathered = (
        lax.all_gather(shards[0], ("dp", "seq"), axis=0, tiled=True),
        lax.all_gather(shards[1], ("dp", "seq"), axis=0, tiled=True),
        lax.all_gather(shards[2], ("dp", "seq"), axis=0, tiled=True),
        lax.all_gather(shards[3], ("dp", "seq"), axis=0, tiled=True),
        lax.all_gather(shards[4], ("dp", "seq"), axis=0, tiled=True),
        lax.all_gather(shards[5], ("dp", "seq"), axis=0, tiled=True),
        lax.all_gather(shards[6], ("dp", "seq"), axis=0, tiled=True),
        lax.all_gather(shards[7], ("dp", "seq"), axis=0, tiled=True),
    )
    full_q, full_k, full_v, full_o, full_up, full_down, full_ga, full_gm = gathered
    positions = seq_rank * patches + jnp.arange(patches, dtype=jnp.int32)
    cosine, sine = rope_tables(positions, head_size // 2)
    inputs_f = inputs.astype(jnp.float32).reshape(token_rows, model_width)
    gain_one = full_ga.astype(jnp.float32)
    scale_one = rms_scale(inputs_f)
    flat_attn = (inputs_f * scale_one * gain_one).astype(jnp.bfloat16)
    query_lin = jnp.dot(flat_attn, full_q, preferred_element_type=jnp.float32).reshape(shape_heads)
    key_lin = jnp.dot(flat_attn, full_k, preferred_element_type=jnp.float32).reshape(shape_heads)
    value_flat = jnp.dot(flat_attn, full_v, preferred_element_type=jnp.float32).astype(jnp.bfloat16)
    queries = rotate_pairs(query_lin, cosine, sine).astype(jnp.bfloat16)
    key_flat = rotate_pairs(key_lin, cosine, sine).astype(jnp.bfloat16)
    own_blocks = (key_flat.reshape(shape_flat), value_flat.reshape(shape_flat))
    kept = []
    sources = []
    current = own_blocks
    for offset in range(seq_count):
        if offset > 0:
            current = shifted((current[0], current[1]), "seq", 1)
        kept.append(current)
        sources.append(seq_rank - offset)
    stats = []
    for block_pair, source_idx in zip(kept, sources):
        stats.append(
            block_forward(
                queries,
                block_pair[0].reshape(shape_heads),
                block_pair[1].reshape(shape_heads),
                source_idx,
                positions,
                pad_patches,
                patches,
            )
        )
    peaks = jnp.stack([entry[0] for entry in stats])
    masses = jnp.stack([entry[1] for entry in stats])
    partials = jnp.stack([entry[2] for entry in stats])
    summit = jnp.max(peaks, axis=0)
    weights_blk = jnp.exp(peaks - summit[None])
    total = jnp.sum(weights_blk * masses, axis=0)
    attended = (
        jnp.sum(jnp.swapaxes(weights_blk, 2, 3)[..., None] * partials, axis=0)
        / jnp.swapaxes(total, 1, 2)[..., None]
    )
    attn_low = attended.astype(jnp.bfloat16).reshape(token_rows, model_width)
    branch = jnp.dot(attn_low, full_o, preferred_element_type=jnp.float32)
    hidden = inputs_f + branch
    gain_two = full_gm.astype(jnp.float32)
    scale_two = rms_scale(hidden)
    norm_mlp = (hidden * scale_two * gain_two).astype(jnp.bfloat16)
    upper = jnp.dot(norm_mlp, full_up, preferred_element_type=jnp.float32)
    active = jax.nn.silu(upper).astype(jnp.bfloat16)
    mlp_out = jnp.dot(active, full_down, preferred_element_type=jnp.float32)
    layer_out = (hidden + mlp_out).astype(jnp.bfloat16).reshape(shape_flat)
    back_q, back_k, back_v, back_o, back_up, back_down, back_ga, back_gm = gathered
    cot_low = cotangent.reshape(token_rows, model_width)
    cot_full = cot_low.astype(jnp.float32)
    grad_downw = jnp.dot(active.T, cot_low, preferred_element_type=jnp.float32)
    grad_active = jnp.dot(cot_low, back_down.T, preferred_element_type=jnp.float32)
    sigmoid_up = jax.nn.sigmoid(upper)
    grad_upper = (grad_active * sigmoid_up * (1.0 + upper * (1.0 - sigmoid_up))).astype(
        jnp.bfloat16
    )
    grad_upw = jnp.dot(norm_mlp.T, grad_upper, preferred_element_type=jnp.float32)
    grad_norm_mlp = jnp.dot(grad_upper, back_up.T, preferred_element_type=jnp.float32)
    grad_from_mlp, grad_gain_two = rms_back(
        hidden, scale_two, back_gm.astype(jnp.float32), grad_norm_mlp
    )
    grad_hidden = cot_full + grad_from_mlp
    hid_low = grad_hidden.astype(jnp.bfloat16)
    grad_outw = jnp.dot(attn_low.T, hid_low, preferred_element_type=jnp.float32)
    grad_attn = jnp.dot(hid_low, back_o.T, preferred_element_type=jnp.float32).astype(jnp.bfloat16)
    grad_attn_f = grad_attn.astype(jnp.float32).reshape(shape_heads)
    delta = jnp.swapaxes(jnp.sum(grad_attn_f * attended, axis=-1), 1, 2)
    grad_queries = jnp.zeros(shape_heads, jnp.float32)
    carried = (jnp.zeros(shape_flat, jnp.float32), jnp.zeros(shape_flat, jnp.float32))
    for offset in reversed(range(seq_count)):
        block_pair = kept[offset]
        part_q, part_k, part_v = block_backward(
            queries,
            block_pair[0].reshape(shape_heads),
            block_pair[1].reshape(shape_heads),
            sources[offset],
            positions,
            pad_patches,
            patches,
            summit,
            total,
            delta,
            grad_attn_f,
        )
        grad_queries = grad_queries + part_q
        carried = (carried[0] + part_k.reshape(shape_flat), carried[1] + part_v.reshape(shape_flat))
        if offset > 0:
            carried = (
                shifted(carried[0].astype(jnp.bfloat16), "seq", -1).astype(jnp.float32),
                shifted(carried[1].astype(jnp.bfloat16), "seq", -1).astype(jnp.float32),
            )
    grad_keys, grad_values = carried
    scale_factor = head_size ** (-0.5)
    grad_qlin = (
        rotate_back(grad_queries * scale_factor, cosine, sine)
        .astype(jnp.bfloat16)
        .reshape(token_rows, model_width)
    )
    grad_klin = (
        rotate_back(grad_keys.reshape(shape_heads) * scale_factor, cosine, sine)
        .astype(jnp.bfloat16)
        .reshape(token_rows, model_width)
    )
    grad_vlin = grad_values.astype(jnp.bfloat16).reshape(token_rows, model_width)
    grad_qw = jnp.dot(flat_attn.T, grad_qlin, preferred_element_type=jnp.float32)
    grad_kw = jnp.dot(flat_attn.T, grad_klin, preferred_element_type=jnp.float32)
    grad_vw = jnp.dot(flat_attn.T, grad_vlin, preferred_element_type=jnp.float32)
    grad_norm_attn = jnp.dot(grad_qlin, back_q.T, preferred_element_type=jnp.float32)
    grad_norm_attn = grad_norm_attn + jnp.dot(
        grad_klin, back_k.T, preferred_element_type=jnp.float32
    )
    grad_norm_attn = grad_norm_attn + jnp.dot(
        grad_vlin, back_v.T, preferred_element_type=jnp.float32
    )
    grad_from_attn, grad_gain_one = rms_back(
        inputs_f, scale_one, back_ga.astype(jnp.float32), grad_norm_attn
    )
    grad_input = (grad_hidden + grad_from_attn).reshape(shape_flat)
    totals = (
        lax.psum_scatter(grad_qw, ("dp", "seq"), scatter_dimension=0, tiled=True),
        lax.psum_scatter(grad_kw, ("dp", "seq"), scatter_dimension=0, tiled=True),
        lax.psum_scatter(grad_vw, ("dp", "seq"), scatter_dimension=0, tiled=True),
        lax.psum_scatter(grad_outw, ("dp", "seq"), scatter_dimension=0, tiled=True),
        lax.psum_scatter(grad_upw, ("dp", "seq"), scatter_dimension=0, tiled=True),
        lax.psum_scatter(grad_downw, ("dp", "seq"), scatter_dimension=0, tiled=True),
        lax.psum_scatter(grad_gain_one, ("dp", "seq"), scatter_dimension=0, tiled=True),
        lax.psum_scatter(grad_gain_two, ("dp", "seq"), scatter_dimension=0, tiled=True),
    )
    return (
        layer_out,
        grad_input,
        totals[0],
        totals[1],
        totals[2],
        totals[3],
        totals[4],
        totals[5],
        totals[6],
        totals[7],
    )


def tables(length):
    places = np.arange(length, dtype=np.float32)[:, None]
    freqs = np.float32(10000.0) ** (-np.arange(40, dtype=np.float32) / np.float32(40))
    angles = places * freqs[None]
    wide = ((0, 0), (0, 88))
    return jnp.asarray(np.pad(np.cos(angles), wide)), jnp.asarray(np.pad(np.sin(angles), wide))


def fast_body(
    inputs, w_query, w_key, w_value, w_out, w_up, w_down, gain_attn, gain_mlp, pad_patches, cotangent
):
    f32, low = jnp.float32, jnp.bfloat16
    cosine, sine = tables(1024)
    tile = jnp.pad(jnp.stack([gain_attn, gain_mlp]).astype(f32), ((0, 6), (0, 88)))
    weights, full_o, full_up, full_down, tiles, x_own, dy_own, norm_t, heads, p, oh, attn = forward_part(
        inputs, cotangent, (w_query, w_key, w_value, w_out, w_up, w_down), tile, pad_patches, cosine, sine
    )
    full_o, full_up, full_down = (w.reshape(1280, 1280) for w in (full_o, full_up, full_down))
    gain_two = tiles.reshape(32, 8, 128)[:, 1, :40].reshape(1280)
    attn_low = attn.reshape(512, 1280)
    hidden = x_own.reshape(512, 1280).astype(f32) + jnp.dot(attn_low, full_o, preferred_element_type=f32)
    scale_two = rms_scale(hidden)
    norm_mlp = (hidden * scale_two * gain_two).astype(low)
    upper = jnp.dot(norm_mlp, full_up, preferred_element_type=f32)
    active = jax.nn.silu(upper).astype(low)
    mlp_out = jnp.dot(active, full_down, preferred_element_type=f32)
    layer = (hidden + mlp_out).astype(low).reshape(2, 256, 1280)
    cot_low = dy_own.reshape(512, 1280)
    dw_down = jnp.dot(active.T, cot_low, preferred_element_type=f32).astype(low)
    grad_active = jnp.dot(cot_low, full_down.T, preferred_element_type=f32)
    sigmoid_up = jax.nn.sigmoid(upper)
    grad_upper = (grad_active * sigmoid_up * (1.0 + upper * (1.0 - sigmoid_up))).astype(low)
    dw_up = jnp.dot(norm_mlp.T, grad_upper, preferred_element_type=f32).astype(low)
    grad_norm = jnp.dot(grad_upper, full_up.T, preferred_element_type=f32)
    grad_mlp, grad_gain_two = rms_back(hidden, scale_two, gain_two, grad_norm)
    grad_hidden = cot_low.astype(f32) + grad_mlp
    hid_low = grad_hidden.astype(low)
    dw_out = jnp.dot(attn_low.T, hid_low, preferred_element_type=f32).astype(low)
    grad_attn = jnp.dot(hid_low, full_o.T, preferred_element_type=f32).astype(low)
    dws = tuple(dw.reshape(4, 2, 2, 80, 1280) for dw in (dw_down, dw_up, dw_out))
    results = backward_part(
        layer, grad_attn.reshape(2, 256, 1280), grad_hidden.reshape(2, 256, 1280), grad_gain_two[None],
        dws, weights, tiles, x_own, norm_t, heads, p, oh, cosine, sine,
    )
    return results[:8] + (results[8].reshape(40), results[9].reshape(40))


def solution(mesh):
    placed = (
        P("dp", "seq", None),
        P(("dp", "seq"), None),
        P(("dp", "seq"), None),
        P(("dp", "seq"), None),
        P(("dp", "seq"), None),
        P(("dp", "seq"), None),
        P(("dp", "seq"), None),
        P(("dp", "seq")),
        P(("dp", "seq")),
        P("dp"),
        P("dp", "seq", None),
    )
    return jax.shard_map(
        fast_body if dict(mesh.shape) == {"dp": 8, "seq": 4} else body,
        mesh=mesh,
        in_specs=placed,
        out_specs=(
            P("dp", "seq", None),
            P("dp", "seq", None),
            P(("dp", "seq"), None),
            P(("dp", "seq"), None),
            P(("dp", "seq"), None),
            P(("dp", "seq"), None),
            P(("dp", "seq"), None),
            P(("dp", "seq"), None),
            P(("dp", "seq")),
            P(("dp", "seq")),
        ),
        check_vma=False,
    )
```

```python
import functools

import jax
import jax.numpy as jnp
import numpy as np
from jax import lax
from jax.experimental import pallas as pl
from jax.experimental.pallas import tpu as pltpu
from jax.sharding import PartitionSpec as P

HEADS = 16
HEAD_DIM = 80


def shifted(value, axis, steps):
    count = lax.axis_size(axis)
    initial, last = (max(0, -steps), min(count, count - steps))
    return lax.ppermute(value, axis, [(source, source + steps) for source in range(initial, last)])


def rms_scale(values):
    return lax.rsqrt(jnp.mean(values * values, axis=-1, keepdims=True) + 1e-06)


def rms_back(values, scale, gain, grad_norm):
    scaled_grad = grad_norm * gain
    grad_gain = jnp.sum(grad_norm * values * scale, axis=0)
    grad_values = scale * scaled_grad - values * (scale * scale * scale) * jnp.mean(
        scaled_grad * values, axis=-1, keepdims=True
    )
    return (grad_values, grad_gain)


def rope_tables(positions, half):
    freqs = 10000.0 ** (-jnp.arange(half, dtype=jnp.float32) / half)
    angles = positions[:, None].astype(jnp.float32) * freqs[None, :]
    return (jnp.cos(angles), jnp.sin(angles))


def rotate_pairs(tensor, cosine, sine):
    half = tensor.shape[-1] // 2
    first = tensor[..., :half]
    second = tensor[..., half:]
    cos_b = cosine[None, :, None, :]
    sin_b = sine[None, :, None, :]
    return jnp.concatenate(
        [first * cos_b - second * sin_b, first * sin_b + second * cos_b], axis=-1
    )


def rotate_back(tensor, cosine, sine):
    half = tensor.shape[-1] // 2
    first = tensor[..., :half]
    second = tensor[..., half:]
    cos_b = cosine[None, :, None, :]
    sin_b = sine[None, :, None, :]
    return jnp.concatenate(
        [first * cos_b + second * sin_b, second * cos_b - first * sin_b], axis=-1
    )


def block_weights(queries, key_block, source, positions, pad_patches, patches):
    scale_factor = queries.shape[-1] ** (-0.5)
    scores = scale_factor * jnp.einsum(
        "sqhd,skhd->shqk", queries, key_block, preferred_element_type=jnp.float32
    )
    key_pos = source * patches + jnp.arange(patches, dtype=jnp.int32)
    key_grid = key_pos[None, None, :]
    query_grid = positions[None, :, None]
    allowed = (
        (key_grid <= query_grid)
        & ((key_grid >= pad_patches[:, None, None]) | (key_grid == query_grid))
        & (source >= 0)
    )
    allowed = allowed[:, None]
    masked = jnp.where(allowed, scores, -1e30)
    peaks = jnp.max(masked, axis=-1)
    expo = jnp.exp(masked - peaks[..., None]) * allowed.astype(jnp.float32)
    return (expo, peaks)


def block_forward(queries, key_block, value_block, source, positions, pad_patches, patches):
    expo, peaks = block_weights(queries, key_block, source, positions, pad_patches, patches)
    masses = jnp.sum(expo, axis=-1)
    partials = jnp.einsum(
        "shqk,skhd->sqhd",
        expo.astype(jnp.bfloat16),
        value_block,
        preferred_element_type=jnp.float32,
    )
    return (peaks, masses, partials)


def block_backward(
    queries,
    key_block,
    value_block,
    source,
    positions,
    pad_patches,
    patches,
    summit,
    total,
    delta,
    grad_attn,
):
    expo, peaks = block_weights(queries, key_block, source, positions, pad_patches, patches)
    share = jnp.exp(peaks - summit) / total
    share_tok = jnp.swapaxes(share, 1, 2)[..., None]
    grad_part = (share_tok * grad_attn).astype(jnp.bfloat16)
    grad_vblock = jnp.einsum(
        "shqk,sqhd->skhd", expo.astype(jnp.bfloat16), grad_part, preferred_element_type=jnp.float32
    )
    grad_prob = jnp.einsum(
        "sqhd,skhd->shqk", grad_part, value_block, preferred_element_type=jnp.float32
    )
    grad_scores = (expo * (grad_prob - (share * delta)[..., None])).astype(jnp.bfloat16)
    grad_qblock = jnp.einsum(
        "shqk,skhd->sqhd", grad_scores, key_block, preferred_element_type=jnp.float32
    )
    grad_kblock = jnp.einsum(
        "shqk,sqhd->skhd", grad_scores, queries, preferred_element_type=jnp.float32
    )
    return (grad_qblock, grad_kblock, grad_vblock)


MESH_ID = pl.DeviceIdType.MESH
PIECES = ((0, 48, 384), (48, 32, 256))


def coordinates():
    dp = lax.axis_index("dp")
    seq = lax.axis_index("seq")
    return (dp // 2, lax.rem(dp, 2), seq // 2, lax.rem(seq, 2))


def device(z, y, x, c):
    return (z * 2 + y, x * 2 + c)


def peers_of(z, y, x, c):
    along = [device(lax.rem(z + k, 4), y, x, c) for k in (1, 2, 3)]
    return along + [device(z, 1 - y, x, c), device(z, y, 1 - x, c), device(z, y, x, 1 - c)]


def greet(peers):
    barrier = pltpu.get_barrier_semaphore()
    for peer in peers:
        pl.semaphore_signal(barrier, inc=1, device_id=peer, device_id_type=MESH_ID)
    pl.semaphore_wait(barrier, len(peers))


def remote(src, dst, sems, peer):
    return pltpu.make_async_remote_copy(
        src_ref=src,
        dst_ref=dst,
        send_sem=sems[0],
        recv_sem=sems[1],
        device_id=peer,
        device_id_type=MESH_ID,
    )


def send(src, dst, sems, peer):
    copy = remote(src, dst, sems, peer)
    copy.start()
    return copy


class Gather:
    def __init__(self, ref, piece, sems, where):
        first, count, cut = piece
        self.ref, self.sems, self.where = ref, sems, where
        self.rows = pl.ds(first, count)
        self.low, self.high = pl.ds(0, cut), pl.ds(cut, ref.shape[-1] - cut)
        self.copies = [[], [], []]
        self.phase = 0

    def sem(self, i):
        return (self.sems[0].at[i], self.sems[1].at[i])

    def start(self):
        z, y, x, c = self.where
        ref, rows, low, high = self.ref, self.rows, self.low, self.high
        phase = self.phase
        made = []
        if phase == 0:
            block = ref.at[z, y, x, rows, low]
            for k in (1, 2, 3):
                made.append(send(block, block, self.sem(k - 1), device(lax.rem(z + k, 4), y, x, c)))
            block = ref.at[z, y, x, rows, high]
            made.append(send(block, block, self.sem(3), device(z, y, 1 - x, c)))
        elif phase == 1:
            block = ref.at[:, y, x, rows, low]
            made.append(send(block, block, self.sem(4), device(z, 1 - y, x, c)))
            block = ref.at[z, y, :, rows, high]
            for k in (1, 2, 3):
                made.append(send(block, block, self.sem(4 + k), device(lax.rem(z + k, 4), y, x, c)))
        else:
            block = ref.at[:, :, x, rows, low]
            made.append(send(block, block, self.sem(8), device(z, y, 1 - x, c)))
            block = ref.at[:, y, :, rows, high]
            made.append(send(block, block, self.sem(9), device(z, 1 - y, x, c)))
        self.copies[phase] = made
        self.phase = phase + 1

    def arrive(self, phase):
        for copy in self.copies[phase]:
            copy.wait_recv()

    def sent(self):
        for made in self.copies:
            for copy in made:
                copy.wait_send()


HEADS_HERE = 8
SPAN = 256
OFFSETS = (0, 256, 768, 1536, 2560)
NT = (((1,), (1,)), ((), ()))
TN = (((0,), (0,)), ((), ()))


def dot(a, b, dims=(((1,), (0,)), ((), ()))):
    return lax.dot_general(a, b, dims, preferred_element_type=jnp.float32)


def unpack_gains(tiles):
    rows = []
    for z in range(4):
        for y in range(2):
            for x in range(2):
                for c in range(2):
                    rows.append(tiles[z, y, x, c][:, :40])
    full = jnp.concatenate(rows, axis=1)
    return full[0:1], full[1:2]


def spread_heads(value, place):
    for g in range(4):
        pair = dot(value[:, 128 * g : 128 * g + 256], place[g])
        yield pair[:, :128]
        yield pair[:, 128:]


def join_heads(pairs, place):
    wide = [dot(pair, place[g], NT) for g, pair in enumerate(pairs)]
    tiles = [wide[0][:, :128]]
    for g in range(1, 4):
        tiles.append(wide[g - 1][:, 128:] + wide[g][:, :128])
    tiles.append(wide[3][:, 128:])
    return jnp.concatenate(tiles, axis=1)


def forward_kernel(*refs):
    (inputs, cot), weights, tile, pads, cos_ref, sin_ref, places = refs[:2], refs[2:8], refs[8], refs[9], refs[10], refs[11], refs[12]
    (out_qkv, out_wide, tiles, x_own, dy_own, norm_t, out_heads, out_p, out_oh, out_hidden, out_layer, out_slope,
     out_turned) = refs[13:26]
    (narrow, wide, own, other, held, held_dy, norm, normt, heads, probs, oh, flat, masks, attn, hidden, low_norm, active,
     slope, layer, turned_t,
     ssem, rsem, gs, gr, hs, hr, xs, osem, ws, wr, ns, nr, ls, ps, als, alr) = refs[26:]
    where = coordinates()
    z, y, x, c = where
    f32, low = jnp.float32, jnp.bfloat16
    across, sibling = device(z, y, 1 - x, c), device(z, y, x, 1 - c)
    keep = pltpu.make_async_copy(inputs.at[x], held.at[x], ls.at[0])
    keep.start()
    keep_dy = pltpu.make_async_copy(cot.at[x], held_dy.at[x], ls.at[1])
    keep_dy.start()
    greet(peers_of(*where))
    for w in range(6):
        for h in range(2):
            own[h, w] = weights[w][:, 640 * h : 640 * h + 640].astype(f32)
    tiles[z, y, x, c] = tile[...]
    pair = send(own.at[1 - c], other, (xs.at[0], xs.at[1]), sibling)
    pair_tile = send(tiles.at[z, y, x, c], tiles.at[z, y, x, c], (xs.at[2], xs.at[3]), sibling)
    pair.wait_recv()
    pair_tile.wait_recv()
    steps, shares, stores, sends = [], {}, [], [pair, pair_tile]

    def place(w):
        return narrow.at[w] if w < 3 else wide.at[w - 3, c]

    for w in range(6):
        mine, theirs = own[c, w], other[w]
        first = c == 0
        block = jnp.concatenate([jnp.where(first, mine, theirs), jnp.where(first, theirs, mine)], axis=0)
        place(w)[z, y, x] = block.astype(low)
        for i, piece in enumerate(PIECES):
            n = len(steps)
            steps.append(Gather(place(w), piece, (ssem.at[n], rsem.at[n]), where))

    def tile_step(i, block, peers):
        return [send(block, block, (gs.at[i + j], gr.at[i + j]), peer) for j, peer in enumerate(peers)]

    state = {"made": tile_step(0, tiles.at[z, y, x], [device(lax.rem(z + k, 4), y, x, c) for k in (1, 2, 3)])}

    def store(src, dst, sem):
        copy = pltpu.make_async_copy(src, dst, sem)
        copy.start()
        stores.append(copy)

    per = len(PIECES)
    count = 6 * per

    def settle(n):
        w, i = n // per, n % per
        if w < 3:
            if i == per - 1:
                store(narrow.at[w], out_qkv.at[w], osem.at[w])
            return
        part = wide.at[w - 3, c, :, :, :, pl.ds(PIECES[i][0], PIECES[i][1])]
        shares.setdefault(w, []).append(send(part, part, (hs.at[n], hr.at[n]), sibling))

    def whole(w):
        for copy in shares[w]:
            copy.wait_recv()
        sends.extend(shares[w])
        store(wide.at[w - 3], out_wide.at[w - 3], osem.at[w])

    swaps = []

    def swap(src, dst):
        n, i = len(swaps), len(swaps) % 4
        rows = pl.ds(64 * i, 64)
        swaps.append(send(src.at[1 - x, rows], dst.at[x, rows], (ws.at[n], wr.at[n]), across))
        sends.append(swaps[n])

    def advance(t):
        if t < count:
            steps[t].start()
        if 0 <= t - 1 < count:
            steps[t - 1].arrive(0)
            steps[t - 1].start()
        if t in (1, 2, 3):
            for m in state["made"]:
                m.wait_recv()
            sends.extend(state["made"])
            state["made"] = []
        if t == 1:
            state["made"] = tile_step(3, tiles.at[:, y, x], [device(z, 1 - y, x, c)])
        if t == 2:
            state["made"] = tile_step(4, tiles.at[:, :, x], [device(z, y, 1 - x, c)])
        if 0 <= t - 2 < count:
            steps[t - 2].arrive(1)
            steps[t - 2].start()
        if t < 3:
            swap(inputs, held)
            if t == 2:
                swap(inputs, held)
        if 5 <= t < 9:
            swap(cot, held_dy)
        if 0 <= t - 3 < count:
            steps[t - 3].arrive(2)
            settle(t - 3)

    advance(0)
    pad = pads[x]
    row = lax.broadcasted_iota(jnp.int32, (SPAN, SPAN), 0)
    col = lax.broadcasted_iota(jnp.int32, (SPAN, SPAN), 1)
    for i in range(4):
        good = (col <= row) & ((col + SPAN * i >= pad) | (col == row))
        masks[i] = jnp.where(good, 0.0, -1e30).astype(f32)
    before = jnp.where(lax.broadcasted_iota(jnp.int32, (1, 3 * SPAN), 1) >= pad, 0.0, -1e30).astype(f32)
    advance(1)
    advance(2)
    advance(3)
    keep.wait()
    for copy in swaps:
        copy.wait_recv()
    gain_attn, gain_mlp = unpack_gains(tiles)
    passed = []
    for j in range(2):
        value = held[j].astype(f32)
        scale = lax.rsqrt(jnp.mean(value * value, axis=-1, keepdims=True) + 1e-06)
        block = 2 * j + c
        norm[block] = (value * scale * gain_attn).astype(low)
        passed.append(send(norm.at[block], norm.at[block], (ns.at[j], nr.at[j]), sibling))
    store(held, x_own, ls.at[2])
    sends.extend(passed)
    advance(4)
    for copy in passed:
        copy.wait_recv()

    def project(t):
        def step(b, _):
            rows = pl.ds(pl.multiple_of(b * SPAN, SPAN), SPAN)
            value = dot(norm[b], narrow[t].reshape(1280, 640)).astype(low)
            plain = spread_heads(value, places.at[0])
            if t < 2:
                cosine, sine = cos_ref[rows, :], sin_ref[rows, :]
                if t == 0:
                    cosine, sine = cosine * (80.0**-0.5), sine * (80.0**-0.5)
                for h, (one, two) in enumerate(zip(plain, spread_heads(value, places.at[1]))):
                    heads[t, h, rows, :] = (one * cosine + two * sine).astype(low)
            else:
                for h, one in enumerate(plain):
                    heads[t, h, rows, :] = one.astype(low)
            if t == 0:
                normt[:, rows] = jnp.transpose(norm[b])
            return 0

        lax.fori_loop(0, 4, step, 0)

    project(0)
    store(normt, norm_t, ls.at[3])
    advance(5)
    advance(6)
    project(1)
    advance(7)
    advance(8)
    project(2)
    store(heads, out_heads, ls.at[4])

    def attend(h, _):
        slot = lax.rem(h, 2)

        @pl.when(h >= 2)
        def _():
            pltpu.make_async_copy(probs.at[slot], out_p.at[h - 2], ps.at[slot]).wait()

        for i in range(4):
            n = SPAN * (i + 1)
            rows = slice(SPAN * i, SPAN * i + SPAN)
            score = dot(heads[0, h, rows, :], heads[1, h, :n, :], NT)
            last = score[:, n - SPAN :] + masks[i]
            score = last if i == 0 else jnp.concatenate([score[:, : n - SPAN] + before[:, : n - SPAN], last], axis=1)
            peak = jnp.max(score, axis=-1, keepdims=True)
            expo = jnp.exp(score - peak)
            share = (expo * (1.0 / jnp.sum(expo, axis=-1, keepdims=True))).astype(low)
            probs[slot, :, OFFSETS[i] : OFFSETS[i + 1]] = share
            oh[h, rows, :] = dot(share, heads[2, h, :n, :]).astype(low)
        pltpu.make_async_copy(probs.at[slot], out_p.at[h], ps.at[slot]).start()
        return 0

    lax.fori_loop(0, 2, attend, 0)
    advance(9)
    lax.fori_loop(2, 4, attend, 0)
    advance(10)
    lax.fori_loop(4, 6, attend, 0)
    advance(11)
    lax.fori_loop(6, 8, attend, 0)
    store(oh, out_oh, ls.at[5])

    def flatten(b, _):
        rows = pl.ds(pl.multiple_of(b * SPAN, SPAN), SPAN)
        pairs = [jnp.concatenate([oh[2 * g, rows, :], oh[2 * g + 1, rows, :]], axis=1) for g in range(4)]
        flat[b] = join_heads(pairs, places.at[0]).astype(low)
        return 0

    lax.fori_loop(0, 4, flatten, 0)
    columns = pl.ds(pl.multiple_of(640 * c, 128), 640)
    joined = []
    for j in range(2):
        attn[j, :, columns] = flat[2 * j + c]
        joined.append(send(flat.at[2 * j + 1 - c], attn.at[j, :, columns], (als.at[j], alr.at[j]), sibling))
    sends.extend(joined)
    advance(12)
    for copy in joined:
        copy.wait_recv()
    whole(3)

    def out_step(j, _):
        rows = pl.ds(pl.multiple_of(j * SPAN, SPAN), SPAN)
        for h in range(2):
            lanes = slice(640 * h, 640 * h + 640)
            branch = dot(attn[j], wide[0, h].reshape(1280, 640))
            hidden[j, :, lanes] = held[j, :, lanes].astype(f32) + branch
        value = hidden[j]
        scale = lax.rsqrt(jnp.mean(value * value, axis=-1, keepdims=True) + 1e-06)
        low_norm[j] = (value * scale * gain_mlp).astype(low)
        turned_t[0, :, rows] = jnp.transpose(attn[j])
        turned_t[1, :, rows] = jnp.transpose(low_norm[j])
        return 0

    lax.fori_loop(0, 2, out_step, 0)
    store(hidden, out_hidden, ls.at[6])
    advance(13)
    whole(4)

    def up_step(j, _):
        rows = pl.ds(pl.multiple_of(j * SPAN, SPAN), SPAN)
        for h in range(2):
            lanes = slice(640 * h, 640 * h + 640)
            upper = dot(low_norm[j], wide[1, h].reshape(1280, 640))
            gate = 1.0 / (1.0 + jnp.exp(-upper))
            active[j, :, lanes] = (upper * gate).astype(low)
            slope[j, :, lanes] = (gate * (1.0 + upper * (1.0 - gate))).astype(low)
        turned_t[2, :, rows] = jnp.transpose(active[j])
        return 0

    lax.fori_loop(0, 2, up_step, 0)
    store(slope, out_slope, ls.at[7])
    store(turned_t, out_turned, ls.at[8])
    advance(14)
    for copy in swaps[4:]:
        copy.wait_recv()
    keep_dy.wait()
    store(held_dy, dy_own, ls.at[9])
    whole(5)

    def down_step(j, _):
        for h in range(2):
            lanes = slice(640 * h, 640 * h + 640)
            value = hidden[j, :, lanes] + dot(active[j], wide[2, h].reshape(1280, 640))
            layer[j, :, lanes] = value.astype(low)
        return 0

    lax.fori_loop(0, 2, down_step, 0)
    store(layer, out_layer, ls.at[10])
    for h in (6, 7):
        pltpu.make_async_copy(probs.at[h % 2], out_p.at[h], ps.at[h % 2]).wait()
    for item in steps:
        item.sent()
    for copy in sends:
        copy.wait_send()
    for copy in stores:
        copy.wait()


def forward_part(inputs, cot, weights, tile, pads, cosine, sine, places):
    dma = pltpu.SemaphoreType.DMA
    low, f32 = jnp.bfloat16, jnp.float32
    shape = jax.ShapeDtypeStruct
    vmem, anywhere = pl.BlockSpec(memory_space=pltpu.VMEM), pl.BlockSpec(memory_space=pl.ANY)
    tokens = (2, 256, 1280)
    n = 6 * len(PIECES)
    return pl.pallas_call(
        forward_kernel,
        name="gather_forward",
        out_shape=(
            shape((3, 4, 2, 2, 80, 640), low),
            shape((3, 2, 4, 2, 2, 80, 640), low),
            shape((4, 2, 2, 2, 8, 128), f32),
            shape(tokens, low),
            shape(tokens, low),
            shape((1280, 1024), low),
            shape((3, 8, 1024, 128), low),
            shape((8, 256, 2560), low),
            shape((8, 1024, 128), low),
            shape(tokens, f32),
            shape(tokens, low),
            shape(tokens, low),
            shape((3, 1280, 512), low),
        ),
        in_specs=[anywhere] * 2 + [vmem] * 7 + [pl.BlockSpec(memory_space=pltpu.SMEM)] + [vmem] * 3,
        out_specs=(anywhere,) * 2 + (vmem,) + (anywhere,) * 10,
        scratch_shapes=[
            pltpu.VMEM((3, 4, 2, 2, 80, 640), low),
            pltpu.VMEM((3, 2, 4, 2, 2, 80, 640), low),
            pltpu.VMEM((2, 6, 40, 640), f32),
            pltpu.VMEM((6, 40, 640), f32),
            pltpu.VMEM(tokens, low),
            pltpu.VMEM(tokens, low),
            pltpu.VMEM((4, 256, 1280), low),
            pltpu.VMEM((1280, 1024), low),
            pltpu.VMEM((3, 8, 1024, 128), low),
            pltpu.VMEM((2, 256, 2560), low),
            pltpu.VMEM((8, 1024, 128), low),
            pltpu.VMEM((4, 256, 640), low),
            pltpu.VMEM((4, 256, 256), f32),
            pltpu.VMEM(tokens, low),
            pltpu.VMEM(tokens, f32),
            pltpu.VMEM(tokens, low),
            pltpu.VMEM(tokens, low),
            pltpu.VMEM(tokens, low),
            pltpu.VMEM(tokens, low),
            pltpu.VMEM((3, 1280, 512), low),
            dma((n, 10)), dma((n, 10)), dma((5,)), dma((5,)), dma((n,)), dma((n,)), dma((4,)), dma((6,)),
            dma((8,)), dma((8,)), dma((2,)), dma((2,)), dma((11,)), dma((2,)), dma((2,)), dma((2,)),
        ],
        compiler_params=pltpu.CompilerParams(
            collective_id=0, has_side_effects=True, vmem_limit_bytes=60 << 20
        ),
    )(inputs, cot, *weights, tile, pads, cosine, sine, places)


class Scatter:
    def __init__(self, ref, piece, bufs, sems, where):
        first, count, cut = piece
        self.ref, self.cut, self.bufs, self.sems, self.where = ref, cut, bufs, sems, where
        self.rows = pl.ds(first, count)
        self.low, self.high = pl.ds(0, cut), pl.ds(cut, ref.shape[-1] - cut)
        self.copies = []
        self.next = []
        self.stage = 0

    def sem(self, i):
        return (self.sems[0].at[i], self.sems[1].at[i])

    def post(self, makers):
        self.next = makers
        self.copies += makers
        for maker in makers:
            maker().start()

    def arrive(self):
        for maker in self.next:
            maker().wait_recv()

    def start(self):
        z, y, x, c = self.where
        ref, b, rows = self.ref, self.bufs, self.rows
        self.post([
            lambda: remote(ref.at[:, :, 1 - x, rows, self.low], b["a1"], self.sem(0), device(z, y, 1 - x, c)),
            lambda: remote(ref.at[:, 1 - y, :, rows, self.high], b["b1"], self.sem(1), device(z, 1 - y, x, c)),
        ])

    def second(self):
        z, y, x, c = self.where
        ref, b, rows, wide, thin = self.ref, self.bufs, self.rows, self.low, self.high
        f32, low = jnp.float32, jnp.bfloat16
        self.arrive()

        def fold(i, _):
            zi, yi = i // 2, lax.rem(i, 2)
            ref[zi, yi, x, rows, wide] = (ref[zi, yi, x, rows, wide].astype(f32) + b["a1"][zi, yi].astype(f32)).astype(low)
            ref[zi, y, yi, rows, thin] = (ref[zi, y, yi, rows, thin].astype(f32) + b["b1"][zi, yi].astype(f32)).astype(low)
            return 0

        lax.fori_loop(0, 8, fold, 0)
        def along(k):
            other = lax.rem(z + k, 4)
            return remote(ref.at[other, y, :, rows, thin], b["b2"].at[k - 1], self.sem(2 + k), device(other, y, x, c))

        made = [lambda: remote(ref.at[:, 1 - y, x, rows, wide], b["a2"], self.sem(2), device(z, 1 - y, x, c))]
        self.post(made + [functools.partial(along, k) for k in (1, 2, 3)])

    def third(self):
        z, y, x, c = self.where
        ref, b, rows, wide, thin = self.ref, self.bufs, self.rows, self.low, self.high
        f32, low = jnp.float32, jnp.bfloat16
        self.arrive()

        def fold(zi, _):
            ref[zi, y, x, rows, wide] = (ref[zi, y, x, rows, wide].astype(f32) + b["a2"][zi].astype(f32)).astype(low)
            return 0

        lax.fori_loop(0, 4, fold, 0)
        value = ref[z, y, 1 - x, rows, thin].astype(f32)
        for k in range(3):
            value = value + b["b2"][k, 1 - x].astype(f32)
        ref[z, y, 1 - x, rows, thin] = value.astype(low)
        def along(k):
            other = lax.rem(z + k, 4)
            return remote(ref.at[other, y, x, rows, wide], b["a3"].at[k - 1], self.sem(6 + k), device(other, y, x, c))

        made = [lambda: remote(ref.at[z, y, 1 - x, rows, thin], b["b3"], self.sem(6), device(z, y, 1 - x, c))]
        self.post(made + [functools.partial(along, k) for k in (1, 2, 3)])

    def finish(self, out):
        z, y, x, c = self.where
        ref, b, rows = self.ref, self.bufs, self.rows
        f32 = jnp.float32
        self.arrive()
        left = ref[z, y, x, rows, self.low].astype(f32)
        right = ref[z, y, x, rows, self.high].astype(f32) + b["b3"][...].astype(f32)
        for k in range(3):
            left = left + b["a3"][k].astype(f32)
            right = right + b["b2"][k, x].astype(f32)
        out[rows, self.low] = left
        out[rows, self.high] = right
        for maker in self.copies:
            maker().wait_send()


def scatter_buffers(piece, columns):
    first, rows, cut = piece
    rest = columns - cut
    return {
        "a1": (4, 2, rows, cut),
        "a2": (4, rows, cut),
        "a3": (3, rows, cut),
        "b1": (4, 2, rows, rest),
        "b2": (3, 2, rows, rest),
        "b3": (rows, rest),
    }


SLOTS = 4
BACK_PIECES = PIECES


def backward_kernel(*refs):
    (layer, hidden, slope_in, turned_in, dy_in, wide_in, weights_in, tiles, x_own, norm_t, heads_in, p_in, oh_in,
     cos_ref, sin_ref, places) = refs[:16]
    (out_layer, out_input, o_q, o_k, o_v, o_o, o_up, o_down, o_ga, o_gm) = refs[16:26]
    (sums, extra, flat_in, xs_own, hid, shown, part_recv, in_recv, fins, finr, tot, trecv, gain_rows,
     ls, es, er, ss, sr, fs, fr, gs, gr, ps, qs, qr, ys, yr, os) = refs[26:54]
    per = len(BACK_PIECES)
    bufs = []
    rest = refs[54:]
    for i in range(per):
        bufs.append(dict(zip(scatter_buffers(BACK_PIECES[i], 640), rest[6 * i : 6 * i + 6])))
    where = coordinates()
    z, y, x, c = where
    f32, low = jnp.float32, jnp.bfloat16
    dma = pltpu.SemaphoreType.DMA
    across, sibling = device(z, y, 1 - x, c), device(z, y, x, 1 - c)
    mine = pl.ds(pl.multiple_of(640 * c, 128), 640)
    yours = pl.ds(pl.multiple_of(640 * (1 - c), 128), 640)
    sends = []

    def local(src, dst, sem):
        copy = pltpu.make_async_copy(src, dst, sem)
        copy.start()
        return copy

    parts = []
    for n in range(6):
        for i, piece in enumerate(BACK_PIECES):
            held = {k: v.at[n] for k, v in bufs[i].items()}
            m = per * n + i
            parts.append(Scatter(sums.at[n % SLOTS], piece, held, (ss.at[m], sr.at[m]), where))
    outs = (o_down, o_up, o_o, o_v, o_k, o_q)
    active, crossing, done = [], [], []

    def pump(*fresh):
        older = list(active)
        for m in fresh:
            parts[m].start()
        active[:0] = fresh
        for m in older:
            part = parts[m]
            part.stage += 1
            if part.stage == 1:
                part.second()
            elif part.stage == 2:
                part.third()
            elif part.stage == 3:
                n = m // per
                part.finish(fins.at[n])
                if m % per == per - 1:
                    theirs = pl.ds(pl.multiple_of(40 * (1 - c), 8), 40)
                    crossing.append((n, send(fins.at[n, theirs], finr.at[n], (fs.at[n], fr.at[n]), sibling)))
            else:
                active.remove(m)
                done.append(m)
                if m % per == per - 1:
                    n = m // per
                    dict(crossing)[n].wait_recv()
                    own = fins[n, pl.ds(pl.multiple_of(40 * c, 8), 40), :]
                    theirs, first = finr[n], c == 0
                    outs[n][:, :640] = jnp.where(first, own, theirs)
                    outs[n][:, 640:] = jnp.where(first, theirs, own)

    def fold(n):
        def step(i, _):
            zi, yi = i // 2, lax.rem(i, 2)
            for xi in range(2):
                value = sums[n, zi, yi, xi].astype(f32) + extra[n, zi, yi, xi].astype(f32)
                sums[n, zi, yi, xi] = value.astype(low)
            return 0

        lax.fori_loop(0, 8, step, 0)

    load_x = local(x_own, xs_own, ls.at[0])
    load_hid = local(hidden, hid, ls.at[1])
    load_shown = local(layer, shown, ls.at[2])

    def feed_forward(turned, dy, slope, wide, grad_upper, hid_low, give, stage):
        load_turned = [local(turned_in.at[k], turned.at[k], ls.at[3 + k]) for k in (2, 1, 0)]
        load_dy = local(dy_in, dy, ls.at[6])
        load_wide = [local(wide_in.at[k], wide.at[k], ls.at[7 + k]) for k in (2, 1, 0)]
        load_slope = local(slope_in, slope, ls.at[10])
        greet(peers_of(*where))
        _, gain_mlp = unpack_gains(tiles)
        given = []

        def product(n, k, right):
            def theirs_step(zi, _):
                rows = pl.ds(pl.multiple_of(zi * 320, 320), 320)
                give[n, zi] = dot(turned[k, rows, :], right[:, yours]).astype(low).reshape(2, 2, 80, 640)
                return 0

            lax.fori_loop(0, 4, theirs_step, 0)
            given.append(send(give.at[n], extra.at[n], (es.at[2 + n], er.at[2 + n]), sibling))

            def own_step(zi, _):
                rows = pl.ds(pl.multiple_of(zi * 320, 320), 320)
                sums[n, zi] = dot(turned[k, rows, :], right[:, mine]).astype(low).reshape(2, 2, 80, 640)
                return 0

            lax.fori_loop(0, 4, own_step, 0)

        load_turned[0].wait()
        load_dy.wait()
        product(0, 2, dy)
        load_wide[0].wait()
        load_slope.wait()

        def active_step(j, _):
            rows = pl.ds(pl.multiple_of(j * SPAN, SPAN), SPAN)
            total = dot(dy[rows, :640], wide[2, 0].reshape(1280, 640), NT)
            total = total + dot(dy[rows, 640:], wide[2, 1].reshape(1280, 640), NT)
            grad_upper[rows, :] = (total * slope[rows, :].astype(f32)).astype(low)
            return 0

        lax.fori_loop(0, 2, active_step, 0)
        given[0].wait_recv()
        fold(0)
        pump(*range(per))
        load_turned[1].wait()
        product(1, 1, grad_upper)
        load_wide[1].wait()
        load_hid.wait()
        gain_rows[...] = jnp.zeros_like(gain_rows)

        def hidden_step(j, _):
            rows = pl.ds(pl.multiple_of(j * SPAN, SPAN), SPAN)
            grad_norm = dot(grad_upper[rows, :640], wide[1, 0].reshape(1280, 640), NT)
            grad_norm = grad_norm + dot(grad_upper[rows, 640:], wide[1, 1].reshape(1280, 640), NT)
            value = hid[rows, :]
            scale = lax.rsqrt(jnp.mean(value * value, axis=-1, keepdims=True) + 1e-06)
            scaled = grad_norm * gain_mlp
            mean = jnp.mean(scaled * value, axis=-1, keepdims=True)
            gain_rows[0:1] = gain_rows[0:1] + jnp.sum(grad_norm * value * scale, axis=0, keepdims=True)
            result = dy[rows, :].astype(f32) + scale * scaled - value * (scale * scale * scale) * mean
            hid[rows, :] = result
            hid_low[rows, :] = result.astype(low)
            return 0

        lax.fori_loop(0, 2, hidden_step, 0)
        given[1].wait_recv()
        fold(1)
        pump(*range(per, 2 * per))
        load_wide[2].wait()
        moved = []

        def heads_grad(j, half):
            rows = pl.ds(SPAN * j, SPAN)
            total = dot(hid_low[rows, :640], wide[0, 0, pl.ds(2 * half, 2)].reshape(640, 640), NT)
            return total + dot(hid_low[rows, 640:], wide[0, 1, pl.ds(2 * half, 2)].reshape(640, 640), NT)

        for j in range(2):
            stage[j] = heads_grad(j, 1 - c).astype(low)
            moved.append(send(stage.at[j], flat_in.at[2 * j + c], (es.at[j], er.at[j]), sibling))
        for j in range(2):
            flat_in[2 * j + c] = heads_grad(j, c).astype(low)
        load_turned[2].wait()
        product(2, 0, hid_low)
        for copy in moved:
            copy.wait()
        given[2].wait_recv()
        fold(2)
        for copy in given:
            copy.wait_send()

    tokens = (512, 1280)
    pl.run_scoped(
        feed_forward,
        pltpu.VMEM((3, 1280, 512), low),
        pltpu.VMEM(tokens, low),
        pltpu.VMEM(tokens, low),
        pltpu.VMEM((3, 2, 4, 2, 2, 80, 640), low),
        pltpu.VMEM(tokens, low),
        pltpu.VMEM(tokens, low),
        pltpu.VMEM((3, 4, 2, 2, 80, 640), low),
        pltpu.VMEM((2, 256, 640), low),
    )

    def attention(heads, probs, oh, doh, acc, flat, normt, part_send, in_send, in_own):
        def fetch(h, slot):
            return pltpu.make_async_copy(p_in.at[h], probs.at[slot], ps.at[slot])

        load_heads = local(heads_in, heads, ls.at[3])
        fetch(0, 0).start()
        load_oh = local(oh_in, oh, ls.at[4])
        load_normt = local(norm_t, normt, ls.at[5])
        weights = extra
        load_weights = local(weights_in, weights, ls.at[6])
        pump(*range(2 * per, 3 * per))
        load_shown.wait()
        own_layer = local(shown.at[x], out_layer.at[x], ls.at[7])
        back_layer = send(shown.at[1 - x], out_layer.at[x], (ys.at[1], yr.at[1]), across)
        sends.append(back_layer)

        def spread(b, _):
            rows = pl.ds(pl.multiple_of(b * SPAN, SPAN), SPAN)
            for h, one in enumerate(spread_heads(flat_in[b], places.at[0])):
                doh[h, rows, :] = one.astype(low)
            return 0

        lax.fori_loop(0, 4, spread, 0)
        load_heads.wait()
        load_oh.wait()

        def attend(h, _):
            slot = lax.rem(h, 2)

            @pl.when(h < 7)
            def _():
                fetch(h + 1, 1 - slot).start()

            fetch(h, slot).wait()
            for i in range(4):
                n = SPAN * (i + 1)
                rows = slice(SPAN * i, SPAN * i + SPAN)
                grad = doh[h, rows, :]
                delta = jnp.sum(grad.astype(f32) * oh[h, rows, :].astype(f32), axis=-1, keepdims=True)
                share = probs[slot, :, OFFSETS[i] : OFFSETS[i + 1]]
                grad_share = dot(grad, heads[2, h, :n, :], NT)
                grad_score = (share.astype(f32) * (grad_share - delta)).astype(low)
                grad_query = dot(grad_score, heads[1, h, :n, :]) * (80.0**-0.5)
                grad_key = dot(grad_score, heads[0, h, rows, :], TN)
                grad_value = dot(share, grad, TN)
                heads[0, h, rows, :] = grad_query.astype(low)
                if i > 0:
                    acc[0, : n - SPAN] = acc[0, : n - SPAN] + grad_key[: n - SPAN]
                    acc[1, : n - SPAN] = acc[1, : n - SPAN] + grad_value[: n - SPAN]
                acc[0, n - SPAN : n] = grad_key[n - SPAN :]
                acc[1, n - SPAN : n] = grad_value[n - SPAN :]
            heads[1, h] = acc[0].astype(low)
            heads[2, h] = acc[1].astype(low)
            return 0

        lax.fori_loop(0, 3, attend, 0)
        pump()
        lax.fori_loop(3, 6, attend, 0)
        pump()
        lax.fori_loop(6, 8, attend, 0)
        load_normt.wait()

        def product(t, n):
            def join(b, _):
                rows = pl.ds(pl.multiple_of(b * SPAN, SPAN), SPAN)
                pairs = [jnp.concatenate([heads[t, 2 * g, rows, :], heads[t, 2 * g + 1, rows, :]], axis=1) for g in range(4)]
                if t == 2:
                    flat[t, rows, :] = join_heads(pairs, places.at[0]).astype(low)
                    return 0
                total = 0.0
                for move, table in ((0, cos_ref), (1, sin_ref)):
                    twice = jnp.concatenate([table[rows, :], table[rows, :]], axis=1)
                    turned = [(pair.astype(f32) * twice).astype(low) for pair in pairs]
                    total = total + join_heads(turned, places.at[move])
                flat[t, rows, :] = total.astype(low)
                return 0

            lax.fori_loop(0, 4, join, 0)

            def step(zi, _):
                rows = pl.ds(pl.multiple_of(zi * 320, 320), 320)
                sums[n % SLOTS, zi] = dot(normt[rows, :], flat[t]).astype(low).reshape(2, 2, 80, 640)
                return 0

            lax.fori_loop(0, 4, step, 0)

        product(2, 3)
        pump(*range(3 * per, 4 * per))
        product(1, 4)
        pump(*range(4 * per, 5 * per))
        product(0, 5)
        pump(*range(5 * per, 6 * per))
        load_weights.wait()

        def norm_grad(block):
            rows = pl.ds(pl.multiple_of(block * SPAN, SPAN), SPAN)
            total = dot(flat[0, rows, :], weights[0].reshape(1280, 640), NT)
            for t in (1, 2):
                total = total + dot(flat[t, rows, :], weights[t].reshape(1280, 640), NT)
            return total

        def theirs_step(j, _):
            part_send[j] = norm_grad(2 * j + 1 - c).astype(low)
            return 0

        lax.fori_loop(0, 2, theirs_step, 0)
        swapped = [send(part_send.at[j], part_recv.at[j], (qs.at[j], qr.at[j]), sibling) for j in range(2)]
        gain_attn, _ = unpack_gains(tiles)
        load_x.wait()
        for copy in swapped:
            copy.wait_recv()

        def input_grad(j):
            grad_norm = norm_grad(2 * j + c) + part_recv[j].astype(f32)
            value = xs_own[j].astype(f32)
            scale = lax.rsqrt(jnp.mean(value * value, axis=-1, keepdims=True) + 1e-06)
            scaled = grad_norm * gain_attn
            mean = jnp.mean(scaled * value, axis=-1, keepdims=True)
            gain_rows[1:2] = gain_rows[1:2] + jnp.sum(grad_norm * value * scale, axis=0, keepdims=True)
            rows = pl.ds(pl.multiple_of(j * SPAN, SPAN), SPAN)
            return hid[rows, :] + scale * scaled - value * (scale * scale * scale) * mean

        in_send[...] = input_grad(1 - x).astype(low)
        back = send(in_send, in_recv, (ys.at[0], yr.at[0]), across)
        in_own[...] = input_grad(x)
        own_input = local(in_own, out_input.at[x], os.at[0])
        both = gain_rows[0:2]
        for p in range(16):
            tot[p // 4, (p // 2) % 2, p % 2, 0:2, 0:80] = both[:, 80 * p : 80 * p + 80]
        hop = [send(tot, trecv.at[0], (gs.at[0], gr.at[0]), sibling)]
        pump()
        for copy in hop:
            copy.wait()
        tot[...] = tot[...] + trecv[0]
        hop = [send(tot.at[:, :, 1 - x], trecv.at[1, :, :, 0], (gs.at[1], gr.at[1]), device(z, y, 1 - x, c))]
        sends.extend(hop)
        pump()
        for copy in hop:
            copy.wait_recv()
        tot[:, :, x] = tot[:, :, x] + trecv[1, :, :, 0]
        hop = [send(tot.at[:, 1 - y, x], trecv.at[2, :, 0, 0], (gs.at[2], gr.at[2]), device(z, 1 - y, x, c))]
        sends.extend(hop)
        back.wait_recv()
        far = in_recv[...].astype(f32)
        own_input.wait()
        in_own[...] = far
        far_input = local(in_own, out_input.at[1 - x], os.at[1])
        pump()
        for copy in hop:
            copy.wait_recv()
        tot[:, y, x] = tot[:, y, x] + trecv[2, :, 0, 0]
        hop = []
        for k in (1, 2, 3):
            other = lax.rem(z + k, 4)
            hop.append(send(tot.at[other, y, x], trecv.at[3, k, 0, 0], (gs.at[2 + k], gr.at[2 + k]), device(other, y, x, c)))
        sends.extend(hop)
        while active:
            pump()
        for copy in hop:
            copy.wait_recv()
        summed = tot[z, y, x] + trecv[3, 1, 0, 0] + trecv[3, 2, 0, 0] + trecv[3, 3, 0, 0]
        chosen = jnp.where(c == 0, summed[:, :40], summed[:, 40:80])
        o_gm[...] = chosen[0:1]
        o_ga[...] = chosen[1:2]
        far_input.wait()
        own_layer.wait()
        back_layer.wait_recv()
        back.wait_send()
        for copy in swapped + sends + [copy for _, copy in crossing]:
            copy.wait_send()

    pl.run_scoped(
        attention,
        pltpu.VMEM((3, 8, 1024, 128), low),
        pltpu.VMEM((2, 256, 2560), low),
        pltpu.VMEM((8, 1024, 128), low),
        pltpu.VMEM((8, 1024, 128), low),
        pltpu.VMEM((2, 1024, 128), f32),
        pltpu.VMEM((3, 1024, 640), low),
        pltpu.VMEM((1280, 1024), low),
        pltpu.VMEM((2, 256, 1280), low),
        pltpu.VMEM((256, 1280), low),
        pltpu.VMEM((256, 1280), f32),
    )


def backward_part(layer, hidden, slope, turned, dy, wide, weights, tiles, x_own, norm_t, heads, p, oh, cosine, sine, places):
    dma = pltpu.SemaphoreType.DMA
    low, f32 = jnp.bfloat16, jnp.float32
    shape = jax.ShapeDtypeStruct
    vmem, anywhere = pl.BlockSpec(memory_space=pltpu.VMEM), pl.BlockSpec(memory_space=pl.ANY)
    row = shape((40, 1280), f32)
    bufs = [pltpu.VMEM((6,) + v, low) for piece in BACK_PIECES for v in scatter_buffers(piece, 640).values()]
    n = 6 * len(BACK_PIECES)
    return pl.pallas_call(
        backward_kernel,
        name="backward_scatter",
        out_shape=(shape((2, 256, 1280), low), shape((2, 256, 1280), f32)) + (row,) * 6 + (shape((1, 40), f32),) * 2,
        in_specs=[anywhere] * 7 + [vmem] + [anywhere] * 5 + [vmem] * 3,
        out_specs=(anywhere,) * 2 + (vmem,) * 8,
        scratch_shapes=[
            pltpu.VMEM((SLOTS, 4, 2, 2, 80, 640), low),
            pltpu.VMEM((3, 4, 2, 2, 80, 640), low),
            pltpu.VMEM((4, 256, 640), low),
            pltpu.VMEM((2, 256, 1280), low),
            pltpu.VMEM((512, 1280), f32),
            pltpu.VMEM((2, 256, 1280), low),
            pltpu.VMEM((2, 256, 1280), low),
            pltpu.VMEM((256, 1280), low),
            pltpu.VMEM((6, 80, 640), f32),
            pltpu.VMEM((6, 40, 640), f32),
            pltpu.VMEM((4, 2, 2, 8, 128), f32),
            pltpu.VMEM((4, 4, 2, 2, 8, 128), f32),
            pltpu.VMEM((8, 1280), f32),
            dma((11,)), dma((5,)), dma((5,)), dma((n, 10)), dma((n, 10)), dma((6,)), dma((6,)), dma((6,)), dma((6,)),
            dma((2,)), dma((2,)), dma((2,)), dma((2,)), dma((2,)), dma((2,)),
        ] + bufs,
        compiler_params=pltpu.CompilerParams(
            collective_id=1, has_side_effects=True, vmem_limit_bytes=62 << 20
        ),
    )(layer, hidden.reshape(512, 1280), slope.reshape(512, 1280), turned, dy.reshape(512, 1280), wide, weights, tiles,
      x_own, norm_t, heads, p, oh, cosine, sine, places)


def body(
    inputs,
    w_query,
    w_key,
    w_value,
    w_out,
    w_up,
    w_down,
    gain_attn,
    gain_mlp,
    pad_patches,
    cotangent,
):
    contexts, patches, model_width = inputs.shape
    head_count = HEADS
    head_size = HEAD_DIM
    seq_count = lax.axis_size("seq")
    seq_rank = lax.axis_index("seq")
    token_rows = contexts * patches
    shape_heads = (contexts, patches, head_count, head_size)
    shape_flat = (contexts, patches, model_width)
    shards = (w_query, w_key, w_value, w_out, w_up, w_down, gain_attn, gain_mlp)
    gathered = (
        lax.all_gather(shards[0], ("dp", "seq"), axis=0, tiled=True),
        lax.all_gather(shards[1], ("dp", "seq"), axis=0, tiled=True),
        lax.all_gather(shards[2], ("dp", "seq"), axis=0, tiled=True),
        lax.all_gather(shards[3], ("dp", "seq"), axis=0, tiled=True),
        lax.all_gather(shards[4], ("dp", "seq"), axis=0, tiled=True),
        lax.all_gather(shards[5], ("dp", "seq"), axis=0, tiled=True),
        lax.all_gather(shards[6], ("dp", "seq"), axis=0, tiled=True),
        lax.all_gather(shards[7], ("dp", "seq"), axis=0, tiled=True),
    )
    full_q, full_k, full_v, full_o, full_up, full_down, full_ga, full_gm = gathered
    positions = seq_rank * patches + jnp.arange(patches, dtype=jnp.int32)
    cosine, sine = rope_tables(positions, head_size // 2)
    inputs_f = inputs.astype(jnp.float32).reshape(token_rows, model_width)
    gain_one = full_ga.astype(jnp.float32)
    scale_one = rms_scale(inputs_f)
    flat_attn = (inputs_f * scale_one * gain_one).astype(jnp.bfloat16)
    query_lin = jnp.dot(flat_attn, full_q, preferred_element_type=jnp.float32).reshape(shape_heads)
    key_lin = jnp.dot(flat_attn, full_k, preferred_element_type=jnp.float32).reshape(shape_heads)
    value_flat = jnp.dot(flat_attn, full_v, preferred_element_type=jnp.float32).astype(jnp.bfloat16)
    queries = rotate_pairs(query_lin, cosine, sine).astype(jnp.bfloat16)
    key_flat = rotate_pairs(key_lin, cosine, sine).astype(jnp.bfloat16)
    own_blocks = (key_flat.reshape(shape_flat), value_flat.reshape(shape_flat))
    kept = []
    sources = []
    current = own_blocks
    for offset in range(seq_count):
        if offset > 0:
            current = shifted((current[0], current[1]), "seq", 1)
        kept.append(current)
        sources.append(seq_rank - offset)
    stats = []
    for block_pair, source_idx in zip(kept, sources):
        stats.append(
            block_forward(
                queries,
                block_pair[0].reshape(shape_heads),
                block_pair[1].reshape(shape_heads),
                source_idx,
                positions,
                pad_patches,
                patches,
            )
        )
    peaks = jnp.stack([entry[0] for entry in stats])
    masses = jnp.stack([entry[1] for entry in stats])
    partials = jnp.stack([entry[2] for entry in stats])
    summit = jnp.max(peaks, axis=0)
    weights_blk = jnp.exp(peaks - summit[None])
    total = jnp.sum(weights_blk * masses, axis=0)
    attended = (
        jnp.sum(jnp.swapaxes(weights_blk, 2, 3)[..., None] * partials, axis=0)
        / jnp.swapaxes(total, 1, 2)[..., None]
    )
    attn_low = attended.astype(jnp.bfloat16).reshape(token_rows, model_width)
    branch = jnp.dot(attn_low, full_o, preferred_element_type=jnp.float32)
    hidden = inputs_f + branch
    gain_two = full_gm.astype(jnp.float32)
    scale_two = rms_scale(hidden)
    norm_mlp = (hidden * scale_two * gain_two).astype(jnp.bfloat16)
    upper = jnp.dot(norm_mlp, full_up, preferred_element_type=jnp.float32)
    active = jax.nn.silu(upper).astype(jnp.bfloat16)
    mlp_out = jnp.dot(active, full_down, preferred_element_type=jnp.float32)
    layer_out = (hidden + mlp_out).astype(jnp.bfloat16).reshape(shape_flat)
    back_q, back_k, back_v, back_o, back_up, back_down, back_ga, back_gm = gathered
    cot_low = cotangent.reshape(token_rows, model_width)
    cot_full = cot_low.astype(jnp.float32)
    grad_downw = jnp.dot(active.T, cot_low, preferred_element_type=jnp.float32)
    grad_active = jnp.dot(cot_low, back_down.T, preferred_element_type=jnp.float32)
    sigmoid_up = jax.nn.sigmoid(upper)
    grad_upper = (grad_active * sigmoid_up * (1.0 + upper * (1.0 - sigmoid_up))).astype(
        jnp.bfloat16
    )
    grad_upw = jnp.dot(norm_mlp.T, grad_upper, preferred_element_type=jnp.float32)
    grad_norm_mlp = jnp.dot(grad_upper, back_up.T, preferred_element_type=jnp.float32)
    grad_from_mlp, grad_gain_two = rms_back(
        hidden, scale_two, back_gm.astype(jnp.float32), grad_norm_mlp
    )
    grad_hidden = cot_full + grad_from_mlp
    hid_low = grad_hidden.astype(jnp.bfloat16)
    grad_outw = jnp.dot(attn_low.T, hid_low, preferred_element_type=jnp.float32)
    grad_attn = jnp.dot(hid_low, back_o.T, preferred_element_type=jnp.float32).astype(jnp.bfloat16)
    grad_attn_f = grad_attn.astype(jnp.float32).reshape(shape_heads)
    delta = jnp.swapaxes(jnp.sum(grad_attn_f * attended, axis=-1), 1, 2)
    grad_queries = jnp.zeros(shape_heads, jnp.float32)
    carried = (jnp.zeros(shape_flat, jnp.float32), jnp.zeros(shape_flat, jnp.float32))
    for offset in reversed(range(seq_count)):
        block_pair = kept[offset]
        part_q, part_k, part_v = block_backward(
            queries,
            block_pair[0].reshape(shape_heads),
            block_pair[1].reshape(shape_heads),
            sources[offset],
            positions,
            pad_patches,
            patches,
            summit,
            total,
            delta,
            grad_attn_f,
        )
        grad_queries = grad_queries + part_q
        carried = (carried[0] + part_k.reshape(shape_flat), carried[1] + part_v.reshape(shape_flat))
        if offset > 0:
            carried = (
                shifted(carried[0].astype(jnp.bfloat16), "seq", -1).astype(jnp.float32),
                shifted(carried[1].astype(jnp.bfloat16), "seq", -1).astype(jnp.float32),
            )
    grad_keys, grad_values = carried
    scale_factor = head_size ** (-0.5)
    grad_qlin = (
        rotate_back(grad_queries * scale_factor, cosine, sine)
        .astype(jnp.bfloat16)
        .reshape(token_rows, model_width)
    )
    grad_klin = (
        rotate_back(grad_keys.reshape(shape_heads) * scale_factor, cosine, sine)
        .astype(jnp.bfloat16)
        .reshape(token_rows, model_width)
    )
    grad_vlin = grad_values.astype(jnp.bfloat16).reshape(token_rows, model_width)
    grad_qw = jnp.dot(flat_attn.T, grad_qlin, preferred_element_type=jnp.float32)
    grad_kw = jnp.dot(flat_attn.T, grad_klin, preferred_element_type=jnp.float32)
    grad_vw = jnp.dot(flat_attn.T, grad_vlin, preferred_element_type=jnp.float32)
    grad_norm_attn = jnp.dot(grad_qlin, back_q.T, preferred_element_type=jnp.float32)
    grad_norm_attn = grad_norm_attn + jnp.dot(
        grad_klin, back_k.T, preferred_element_type=jnp.float32
    )
    grad_norm_attn = grad_norm_attn + jnp.dot(
        grad_vlin, back_v.T, preferred_element_type=jnp.float32
    )
    grad_from_attn, grad_gain_one = rms_back(
        inputs_f, scale_one, back_ga.astype(jnp.float32), grad_norm_attn
    )
    grad_input = (grad_hidden + grad_from_attn).reshape(shape_flat)
    totals = (
        lax.psum_scatter(grad_qw, ("dp", "seq"), scatter_dimension=0, tiled=True),
        lax.psum_scatter(grad_kw, ("dp", "seq"), scatter_dimension=0, tiled=True),
        lax.psum_scatter(grad_vw, ("dp", "seq"), scatter_dimension=0, tiled=True),
        lax.psum_scatter(grad_outw, ("dp", "seq"), scatter_dimension=0, tiled=True),
        lax.psum_scatter(grad_upw, ("dp", "seq"), scatter_dimension=0, tiled=True),
        lax.psum_scatter(grad_downw, ("dp", "seq"), scatter_dimension=0, tiled=True),
        lax.psum_scatter(grad_gain_one, ("dp", "seq"), scatter_dimension=0, tiled=True),
        lax.psum_scatter(grad_gain_two, ("dp", "seq"), scatter_dimension=0, tiled=True),
    )
    return (
        layer_out,
        grad_input,
        totals[0],
        totals[1],
        totals[2],
        totals[3],
        totals[4],
        totals[5],
        totals[6],
        totals[7],
    )


def tables(length):
    places = np.arange(length, dtype=np.float32)[:, None]
    freqs = np.float32(10000.0) ** (-np.arange(40, dtype=np.float32) / np.float32(40))
    angles = places * freqs[None]
    wide = ((0, 0), (0, 48))
    moves = np.zeros((2, 4, 256, 256), np.float32)
    for g in range(4):
        for head in range(2):
            for entry in range(80):
                base = 80 * (2 * g + head) - 128 * g
                other = entry + 40 if entry < 40 else entry - 40
                moves[0, g, base + entry, 128 * head + entry] = 1.0
                moves[1, g, base + other, 128 * head + entry] = -1.0 if entry < 40 else 1.0
    cosine, sine = (np.pad(np.tile(f(angles), (1, 2)), wide) for f in (np.cos, np.sin))
    return jnp.asarray(cosine), jnp.asarray(sine), jnp.asarray(moves, jnp.bfloat16)


def fast_body(
    inputs, w_query, w_key, w_value, w_out, w_up, w_down, gain_attn, gain_mlp, pad_patches, cotangent
):
    moves = tables(1024)
    tile = jnp.pad(jnp.stack([gain_attn, gain_mlp]).astype(jnp.float32), ((0, 6), (0, 88)))
    weights, wide, tiles, x_own, dy_own, norm_t, heads, p, oh, hidden, layer, slope, turned = forward_part(
        inputs, cotangent, (w_query, w_key, w_value, w_out, w_up, w_down), tile, pad_patches, *moves
    )
    results = backward_part(
        layer, hidden, slope, turned, dy_own, wide, weights, tiles, x_own, norm_t, heads, p, oh, *moves
    )
    return results[:8] + (results[8].reshape(40), results[9].reshape(40))


def solution(mesh):
    placed = (
        P("dp", "seq", None),
        P(("dp", "seq"), None),
        P(("dp", "seq"), None),
        P(("dp", "seq"), None),
        P(("dp", "seq"), None),
        P(("dp", "seq"), None),
        P(("dp", "seq"), None),
        P(("dp", "seq")),
        P(("dp", "seq")),
        P("dp"),
        P("dp", "seq", None),
    )
    return jax.shard_map(
        fast_body if dict(mesh.shape) == {"dp": 8, "seq": 4} else body,
        mesh=mesh,
        in_specs=placed,
        out_specs=(
            P("dp", "seq", None),
            P("dp", "seq", None),
            P(("dp", "seq"), None),
            P(("dp", "seq"), None),
            P(("dp", "seq"), None),
            P(("dp", "seq"), None),
            P(("dp", "seq"), None),
            P(("dp", "seq"), None),
            P(("dp", "seq")),
            P(("dp", "seq")),
        ),
        check_vma=False,
    )
```

```python
import functools

import jax
import jax.numpy as jnp
import numpy as np
from jax import lax
from jax.experimental import pallas as pl
from jax.experimental.pallas import tpu as pltpu
from jax.sharding import PartitionSpec as P

HEADS = 16
HEAD_DIM = 80


def shifted(value, axis, steps):
    count = lax.axis_size(axis)
    initial, last = (max(0, -steps), min(count, count - steps))
    return lax.ppermute(value, axis, [(source, source + steps) for source in range(initial, last)])


def rms_scale(values):
    return lax.rsqrt(jnp.mean(values * values, axis=-1, keepdims=True) + 1e-06)


def rms_back(values, scale, gain, grad_norm):
    scaled_grad = grad_norm * gain
    grad_gain = jnp.sum(grad_norm * values * scale, axis=0)
    grad_values = scale * scaled_grad - values * (scale * scale * scale) * jnp.mean(
        scaled_grad * values, axis=-1, keepdims=True
    )
    return (grad_values, grad_gain)


def rope_tables(positions, half):
    freqs = 10000.0 ** (-jnp.arange(half, dtype=jnp.float32) / half)
    angles = positions[:, None].astype(jnp.float32) * freqs[None, :]
    return (jnp.cos(angles), jnp.sin(angles))


def rotate_pairs(tensor, cosine, sine):
    half = tensor.shape[-1] // 2
    first = tensor[..., :half]
    second = tensor[..., half:]
    cos_b = cosine[None, :, None, :]
    sin_b = sine[None, :, None, :]
    return jnp.concatenate(
        [first * cos_b - second * sin_b, first * sin_b + second * cos_b], axis=-1
    )


def rotate_back(tensor, cosine, sine):
    half = tensor.shape[-1] // 2
    first = tensor[..., :half]
    second = tensor[..., half:]
    cos_b = cosine[None, :, None, :]
    sin_b = sine[None, :, None, :]
    return jnp.concatenate(
        [first * cos_b + second * sin_b, second * cos_b - first * sin_b], axis=-1
    )


def block_weights(queries, key_block, source, positions, pad_patches, patches):
    scale_factor = queries.shape[-1] ** (-0.5)
    scores = scale_factor * jnp.einsum(
        "sqhd,skhd->shqk", queries, key_block, preferred_element_type=jnp.float32
    )
    key_pos = source * patches + jnp.arange(patches, dtype=jnp.int32)
    key_grid = key_pos[None, None, :]
    query_grid = positions[None, :, None]
    allowed = (
        (key_grid <= query_grid)
        & ((key_grid >= pad_patches[:, None, None]) | (key_grid == query_grid))
        & (source >= 0)
    )
    allowed = allowed[:, None]
    masked = jnp.where(allowed, scores, -1e30)
    peaks = jnp.max(masked, axis=-1)
    expo = jnp.exp(masked - peaks[..., None]) * allowed.astype(jnp.float32)
    return (expo, peaks)


def block_forward(queries, key_block, value_block, source, positions, pad_patches, patches):
    expo, peaks = block_weights(queries, key_block, source, positions, pad_patches, patches)
    masses = jnp.sum(expo, axis=-1)
    partials = jnp.einsum(
        "shqk,skhd->sqhd",
        expo.astype(jnp.bfloat16),
        value_block,
        preferred_element_type=jnp.float32,
    )
    return (peaks, masses, partials)


def block_backward(
    queries,
    key_block,
    value_block,
    source,
    positions,
    pad_patches,
    patches,
    summit,
    total,
    delta,
    grad_attn,
):
    expo, peaks = block_weights(queries, key_block, source, positions, pad_patches, patches)
    share = jnp.exp(peaks - summit) / total
    share_tok = jnp.swapaxes(share, 1, 2)[..., None]
    grad_part = (share_tok * grad_attn).astype(jnp.bfloat16)
    grad_vblock = jnp.einsum(
        "shqk,sqhd->skhd", expo.astype(jnp.bfloat16), grad_part, preferred_element_type=jnp.float32
    )
    grad_prob = jnp.einsum(
        "sqhd,skhd->shqk", grad_part, value_block, preferred_element_type=jnp.float32
    )
    grad_scores = (expo * (grad_prob - (share * delta)[..., None])).astype(jnp.bfloat16)
    grad_qblock = jnp.einsum(
        "shqk,skhd->sqhd", grad_scores, key_block, preferred_element_type=jnp.float32
    )
    grad_kblock = jnp.einsum(
        "shqk,sqhd->skhd", grad_scores, queries, preferred_element_type=jnp.float32
    )
    return (grad_qblock, grad_kblock, grad_vblock)


MESH_ID = pl.DeviceIdType.MESH
PIECES = ((0, 48, 384), (48, 32, 256))


def coordinates():
    dp = lax.axis_index("dp")
    seq = lax.axis_index("seq")
    return (dp // 2, lax.rem(dp, 2), seq // 2, lax.rem(seq, 2))


def device(z, y, x, c):
    return (z * 2 + y, x * 2 + c)


def peers_of(z, y, x, c):
    along = [device(lax.rem(z + k, 4), y, x, c) for k in (1, 2, 3)]
    return along + [device(z, 1 - y, x, c), device(z, y, 1 - x, c), device(z, y, x, 1 - c)]


def greet(peers):
    barrier = pltpu.get_barrier_semaphore()
    for peer in peers:
        pl.semaphore_signal(barrier, inc=1, device_id=peer, device_id_type=MESH_ID)
    pl.semaphore_wait(barrier, len(peers))


def remote(src, dst, sems, peer):
    return pltpu.make_async_remote_copy(
        src_ref=src,
        dst_ref=dst,
        send_sem=sems[0],
        recv_sem=sems[1],
        device_id=peer,
        device_id_type=MESH_ID,
    )


def send(src, dst, sems, peer):
    copy = remote(src, dst, sems, peer)
    copy.start()
    return copy


class Gather:
    def __init__(self, ref, piece, sems, where):
        first, count, cut = piece
        self.ref, self.sems, self.where = ref, sems, where
        self.rows = pl.ds(first, count)
        self.low, self.high = pl.ds(0, cut), pl.ds(cut, ref.shape[-1] - cut)
        self.copies = [[], [], []]
        self.phase = 0

    def sem(self, i):
        return (self.sems[0].at[i], self.sems[1].at[i])

    def start(self):
        z, y, x, c = self.where
        ref, rows, low, high = self.ref, self.rows, self.low, self.high
        phase = self.phase
        made = []
        if phase == 0:
            block = ref.at[z, y, x, rows, low]
            for k in (1, 2, 3):
                made.append(send(block, block, self.sem(k - 1), device(lax.rem(z + k, 4), y, x, c)))
            block = ref.at[z, y, x, rows, high]
            made.append(send(block, block, self.sem(3), device(z, y, 1 - x, c)))
        elif phase == 1:
            block = ref.at[:, y, x, rows, low]
            made.append(send(block, block, self.sem(4), device(z, 1 - y, x, c)))
            block = ref.at[z, y, :, rows, high]
            for k in (1, 2, 3):
                made.append(send(block, block, self.sem(4 + k), device(lax.rem(z + k, 4), y, x, c)))
        else:
            block = ref.at[:, :, x, rows, low]
            made.append(send(block, block, self.sem(8), device(z, y, 1 - x, c)))
            block = ref.at[:, y, :, rows, high]
            made.append(send(block, block, self.sem(9), device(z, 1 - y, x, c)))
        self.copies[phase] = made
        self.phase = phase + 1

    def arrive(self, phase):
        for copy in self.copies[phase]:
            copy.wait_recv()

    def sent(self):
        for made in self.copies:
            for copy in made:
                copy.wait_send()


HEADS_HERE = 8
SPAN = 256
OFFSETS = (0, 256, 768, 1536, 2560)
NT = (((1,), (1,)), ((), ()))
TN = (((0,), (0,)), ((), ()))


def dot(a, b, dims=(((1,), (0,)), ((), ()))):
    return lax.dot_general(a, b, dims, preferred_element_type=jnp.float32)


def unpack_gains(tiles):
    rows = []
    for z in range(4):
        for y in range(2):
            for x in range(2):
                for c in range(2):
                    rows.append(tiles[z, y, x, c][:, :40])
    full = jnp.concatenate(rows, axis=1)
    return full[0:1], full[1:2]


def spread_heads(value, place):
    for g in range(4):
        pair = dot(value[:, 128 * g : 128 * g + 256], place[g])
        yield pair[:, :128]
        yield pair[:, 128:]


def join_heads(pairs, place):
    wide = [dot(pair, place[g], NT) for g, pair in enumerate(pairs)]
    tiles = [wide[0][:, :128]]
    for g in range(1, 4):
        tiles.append(wide[g - 1][:, 128:] + wide[g][:, :128])
    tiles.append(wide[3][:, 128:])
    return jnp.concatenate(tiles, axis=1)


def join_some(pairs, place, part):
    wide = {g: dot(pair, place[g], NT) for g, pair in pairs.items()}
    if part == 0:
        return jnp.concatenate([wide[0][:, :128], wide[0][:, 128:] + wide[1][:, :128]], axis=1)
    middle = [wide[g - 1][:, 128:] + wide[g][:, :128] for g in (2, 3)]
    return jnp.concatenate(middle + [wide[3][:, 128:]], axis=1)


def forward_kernel(*refs):
    (inputs, cot), weights, tile, pads, cos_ref, sin_ref, places = refs[:2], refs[2:8], refs[8], refs[9], refs[10], refs[11], refs[12]
    (out_qkv, out_wide, tiles, x_own, dy_own, norm_t, out_heads, out_p, out_oh, out_hidden, out_layer, out_slope,
     out_turned, out_down) = refs[13:27]
    (narrow, wide, own, other, held, held_dy, norm, normt, heads, probs, oh, flat, masks, attn, hidden, low_norm, active,
     slope, layer, turned_t,
     ssem, rsem, gs, gr, hs, hr, xs, osem, ws, wr, ns, nr, ls, ps, als, alr, gives, giver, give, extra, total) = refs[27:]
    where = coordinates()
    z, y, x, c = where
    f32, low = jnp.float32, jnp.bfloat16
    across, sibling = device(z, y, 1 - x, c), device(z, y, x, 1 - c)
    keep = pltpu.make_async_copy(inputs.at[x], held.at[x], ls.at[0])
    keep.start()
    keep_dy = pltpu.make_async_copy(cot.at[x], held_dy.at[x], ls.at[1])
    keep_dy.start()
    greet(peers_of(*where))
    for w in range(6):
        for h in range(2):
            own[h, w] = weights[w][:, 640 * h : 640 * h + 640].astype(f32)
    tiles[z, y, x, c] = tile[...]
    pair = send(own.at[1 - c], other, (xs.at[0], xs.at[1]), sibling)
    pair_tile = send(tiles.at[z, y, x, c], tiles.at[z, y, x, c], (xs.at[2], xs.at[3]), sibling)
    pair.wait_recv()
    pair_tile.wait_recv()
    steps, shares, stores, sends = [], {}, [], [pair, pair_tile]

    def place(w):
        return narrow.at[w] if w < 3 else wide.at[w - 3, c]

    for w in range(6):
        mine, theirs = own[c, w], other[w]
        first = c == 0
        block = jnp.concatenate([jnp.where(first, mine, theirs), jnp.where(first, theirs, mine)], axis=0)
        place(w)[z, y, x] = block.astype(low)
        for i, piece in enumerate(PIECES):
            n = len(steps)
            steps.append(Gather(place(w), piece, (ssem.at[n], rsem.at[n]), where))

    def tile_step(i, block, peers):
        return [send(block, block, (gs.at[i + j], gr.at[i + j]), peer) for j, peer in enumerate(peers)]

    state = {"made": tile_step(0, tiles.at[z, y, x], [device(lax.rem(z + k, 4), y, x, c) for k in (1, 2, 3)])}

    def store(src, dst, sem):
        copy = pltpu.make_async_copy(src, dst, sem)
        copy.start()
        stores.append(copy)

    per = len(PIECES)
    count = 6 * per

    def settle(n):
        w, i = n // per, n % per
        if w < 3:
            if i == per - 1:
                store(narrow.at[w], out_qkv.at[w], osem.at[w])
            return
        part = wide.at[w - 3, c, :, :, :, pl.ds(PIECES[i][0], PIECES[i][1])]
        shares.setdefault(w, []).append(send(part, part, (hs.at[n], hr.at[n]), sibling))

    def whole(w):
        for copy in shares[w]:
            copy.wait_recv()
        sends.extend(shares[w])
        store(wide.at[w - 3], out_wide.at[w - 3], osem.at[w])

    swaps = []

    def swap(src, dst):
        n, i = len(swaps), len(swaps) % 4
        rows = pl.ds(64 * i, 64)
        swaps.append(send(src.at[1 - x, rows], dst.at[x, rows], (ws.at[n], wr.at[n]), across))
        sends.append(swaps[n])

    def advance(t):
        if t < count:
            steps[t].start()
        if 0 <= t - 1 < count:
            steps[t - 1].arrive(0)
            steps[t - 1].start()
        if t in (1, 2, 3):
            for m in state["made"]:
                m.wait_recv()
            sends.extend(state["made"])
            state["made"] = []
        if t == 1:
            state["made"] = tile_step(3, tiles.at[:, y, x], [device(z, 1 - y, x, c)])
        if t == 2:
            state["made"] = tile_step(4, tiles.at[:, :, x], [device(z, y, 1 - x, c)])
        if 0 <= t - 2 < count:
            steps[t - 2].arrive(1)
            steps[t - 2].start()
        if t < 3:
            swap(inputs, held)
            if t == 2:
                swap(inputs, held)
        if 5 <= t < 9:
            swap(cot, held_dy)
        if 0 <= t - 3 < count:
            steps[t - 3].arrive(2)
            settle(t - 3)

    advance(0)
    pad = pads[x]
    row = lax.broadcasted_iota(jnp.int32, (SPAN, SPAN), 0)
    col = lax.broadcasted_iota(jnp.int32, (SPAN, SPAN), 1)
    for i in range(4):
        good = (col <= row) & ((col + SPAN * i >= pad) | (col == row))
        masks[i] = jnp.where(good, 0.0, -1e30).astype(f32)
    before = jnp.where(lax.broadcasted_iota(jnp.int32, (1, 3 * SPAN), 1) >= pad, 0.0, -1e30).astype(f32)
    advance(1)
    advance(2)
    advance(3)
    keep.wait()
    for copy in swaps:
        copy.wait_recv()
    gain_attn, gain_mlp = unpack_gains(tiles)
    passed = []
    for j in range(2):
        value = held[j].astype(f32)
        scale = lax.rsqrt(jnp.mean(value * value, axis=-1, keepdims=True) + 1e-06)
        block = 2 * j + c
        norm[block] = (value * scale * gain_attn).astype(low)
        passed.append(send(norm.at[block], norm.at[block], (ns.at[j], nr.at[j]), sibling))
    store(held, x_own, ls.at[2])
    sends.extend(passed)
    advance(4)
    for copy in passed:
        copy.wait_recv()

    def project(t):
        def step(b, _):
            rows = pl.ds(pl.multiple_of(b * SPAN, SPAN), SPAN)
            value = dot(norm[b], narrow[t].reshape(1280, 640)).astype(low)
            plain = spread_heads(value, places.at[0])
            if t < 2:
                cosine, sine = cos_ref[rows, :], sin_ref[rows, :]
                if t == 0:
                    cosine, sine = cosine * (80.0**-0.5), sine * (80.0**-0.5)
                for h, (one, two) in enumerate(zip(plain, spread_heads(value, places.at[1]))):
                    heads[t, h, rows, :] = (one * cosine + two * sine).astype(low)
            else:
                for h, one in enumerate(plain):
                    heads[t, h, rows, :] = one.astype(low)
            if t == 0:
                normt[:, rows] = jnp.transpose(norm[b])
            return 0

        lax.fori_loop(0, 4, step, 0)

    project(0)
    store(normt, norm_t, ls.at[3])
    advance(5)
    advance(6)
    project(1)
    advance(7)
    advance(8)
    project(2)
    store(heads, out_heads, ls.at[4])

    def attend(h, _):
        slot = lax.rem(h, 2)

        @pl.when(h >= 2)
        def _():
            pltpu.make_async_copy(probs.at[slot], out_p.at[h - 2], ps.at[slot]).wait()

        for i in range(4):
            n = SPAN * (i + 1)
            rows = slice(SPAN * i, SPAN * i + SPAN)
            score = dot(heads[0, h, rows, :], heads[1, h, :n, :], NT)
            last = score[:, n - SPAN :] + masks[i]
            score = last if i == 0 else jnp.concatenate([score[:, : n - SPAN] + before[:, : n - SPAN], last], axis=1)
            peak = jnp.max(score, axis=-1, keepdims=True)
            expo = jnp.exp(score - peak)
            share = (expo * (1.0 / jnp.sum(expo, axis=-1, keepdims=True))).astype(low)
            probs[slot, :, OFFSETS[i] : OFFSETS[i + 1]] = share
            oh[h, rows, :] = dot(share, heads[2, h, :n, :]).astype(low)
        pltpu.make_async_copy(probs.at[slot], out_p.at[h], ps.at[slot]).start()
        return 0

    lax.fori_loop(0, 2, attend, 0)
    advance(9)
    lax.fori_loop(2, 4, attend, 0)
    advance(10)
    lax.fori_loop(4, 6, attend, 0)
    advance(11)
    lax.fori_loop(6, 8, attend, 0)
    store(oh, out_oh, ls.at[5])

    def flatten(b, _):
        rows = pl.ds(pl.multiple_of(b * SPAN, SPAN), SPAN)
        pairs = [jnp.concatenate([oh[2 * g, rows, :], oh[2 * g + 1, rows, :]], axis=1) for g in range(4)]
        flat[b] = join_heads(pairs, places.at[0]).astype(low)
        return 0

    lax.fori_loop(0, 4, flatten, 0)
    columns = pl.ds(pl.multiple_of(640 * c, 128), 640)
    joined = []
    for j in range(2):
        attn[j, :, columns] = flat[2 * j + c]
        joined.append(send(flat.at[2 * j + 1 - c], attn.at[j, :, columns], (als.at[j], alr.at[j]), sibling))
    sends.extend(joined)
    advance(12)
    for copy in joined:
        copy.wait_recv()
    whole(3)

    def out_step(j, _):
        rows = pl.ds(pl.multiple_of(j * SPAN, SPAN), SPAN)
        for h in range(2):
            lanes = slice(640 * h, 640 * h + 640)
            branch = dot(attn[j], wide[0, h].reshape(1280, 640))
            hidden[j, :, lanes] = held[j, :, lanes].astype(f32) + branch
        value = hidden[j]
        scale = lax.rsqrt(jnp.mean(value * value, axis=-1, keepdims=True) + 1e-06)
        low_norm[j] = (value * scale * gain_mlp).astype(low)
        turned_t[0, :, rows] = jnp.transpose(attn[j])
        turned_t[1, :, rows] = jnp.transpose(low_norm[j])
        return 0

    lax.fori_loop(0, 2, out_step, 0)
    store(hidden, out_hidden, ls.at[6])
    advance(13)
    whole(4)

    def up_step(j, _):
        rows = pl.ds(pl.multiple_of(j * SPAN, SPAN), SPAN)
        for h in range(2):
            lanes = slice(640 * h, 640 * h + 640)
            upper = dot(low_norm[j], wide[1, h].reshape(1280, 640))
            gate = 1.0 / (1.0 + jnp.exp(-upper))
            active[j, :, lanes] = (upper * gate).astype(low)
            slope[j, :, lanes] = (gate * (1.0 + upper * (1.0 - gate))).astype(low)
        turned_t[2, :, rows] = jnp.transpose(active[j])
        return 0

    lax.fori_loop(0, 2, up_step, 0)
    store(slope, out_slope, ls.at[7])
    store(turned_t, out_turned, ls.at[8])
    for copy in swaps[4:]:
        copy.wait_recv()
    keep_dy.wait()
    store(held_dy, dy_own, ls.at[9])
    yours = pl.ds(pl.multiple_of(640 * (1 - c), 128), 640)

    def grad_step(zi, half, ref):
        rows = pl.ds(pl.multiple_of(zi * 320, 320), 320)
        value = dot(turned_t[2, rows, :256], held_dy[0, :, half]) + dot(turned_t[2, rows, 256:], held_dy[1, :, half])
        ref[zi] = value.astype(low).reshape(2, 2, 80, 640)
        return 0

    lax.fori_loop(0, 4, lambda zi, _: grad_step(zi, yours, give), 0)
    given = send(give, extra, (gives.at[0], giver.at[0]), sibling)
    sends.append(given)
    advance(14)
    lax.fori_loop(0, 4, lambda zi, _: grad_step(zi, columns, total), 0)
    given.wait_recv()

    def fold(i, _):
        zi, yi = i // 2, lax.rem(i, 2)
        for xi in range(2):
            total[zi, yi, xi] = (total[zi, yi, xi].astype(f32) + extra[zi, yi, xi].astype(f32)).astype(low)
        return 0

    lax.fori_loop(0, 8, fold, 0)
    store(total, out_down, ls.at[11])
    whole(5)

    def down_step(j, _):
        for h in range(2):
            lanes = slice(640 * h, 640 * h + 640)
            value = hidden[j, :, lanes] + dot(active[j], wide[2, h].reshape(1280, 640))
            layer[j, :, lanes] = value.astype(low)
        return 0

    lax.fori_loop(0, 2, down_step, 0)
    store(layer, out_layer, ls.at[10])
    for h in (6, 7):
        pltpu.make_async_copy(probs.at[h % 2], out_p.at[h], ps.at[h % 2]).wait()
    for item in steps:
        item.sent()
    for copy in sends:
        copy.wait_send()
    for copy in stores:
        copy.wait()


def forward_part(inputs, cot, weights, tile, pads, cosine, sine, places):
    dma = pltpu.SemaphoreType.DMA
    low, f32 = jnp.bfloat16, jnp.float32
    shape = jax.ShapeDtypeStruct
    vmem, anywhere = pl.BlockSpec(memory_space=pltpu.VMEM), pl.BlockSpec(memory_space=pl.ANY)
    tokens = (2, 256, 1280)
    n = 6 * len(PIECES)
    return pl.pallas_call(
        forward_kernel,
        name="gather_forward",
        out_shape=(
            shape((3, 4, 2, 2, 80, 640), low),
            shape((3, 2, 4, 2, 2, 80, 640), low),
            shape((4, 2, 2, 2, 8, 128), f32),
            shape(tokens, low),
            shape(tokens, low),
            shape((1280, 1024), low),
            shape((3, 8, 1024, 128), low),
            shape((8, 256, 2560), low),
            shape((8, 1024, 128), low),
            shape(tokens, f32),
            shape(tokens, low),
            shape(tokens, low),
            shape((3, 1280, 512), low),
            shape((4, 2, 2, 80, 640), low),
        ),
        in_specs=[anywhere] * 2 + [vmem] * 7 + [pl.BlockSpec(memory_space=pltpu.SMEM)] + [vmem] * 3,
        out_specs=(anywhere,) * 2 + (vmem,) + (anywhere,) * 11,
        scratch_shapes=[
            pltpu.VMEM((3, 4, 2, 2, 80, 640), low),
            pltpu.VMEM((3, 2, 4, 2, 2, 80, 640), low),
            pltpu.VMEM((2, 6, 40, 640), f32),
            pltpu.VMEM((6, 40, 640), f32),
            pltpu.VMEM(tokens, low),
            pltpu.VMEM(tokens, low),
            pltpu.VMEM((4, 256, 1280), low),
            pltpu.VMEM((1280, 1024), low),
            pltpu.VMEM((3, 8, 1024, 128), low),
            pltpu.VMEM((2, 256, 2560), low),
            pltpu.VMEM((8, 1024, 128), low),
            pltpu.VMEM((4, 256, 640), low),
            pltpu.VMEM((4, 256, 256), f32),
            pltpu.VMEM(tokens, low),
            pltpu.VMEM(tokens, f32),
            pltpu.VMEM(tokens, low),
            pltpu.VMEM(tokens, low),
            pltpu.VMEM(tokens, low),
            pltpu.VMEM(tokens, low),
            pltpu.VMEM((3, 1280, 512), low),
            dma((n, 10)), dma((n, 10)), dma((5,)), dma((5,)), dma((n,)), dma((n,)), dma((4,)), dma((6,)),
            dma((8,)), dma((8,)), dma((2,)), dma((2,)), dma((12,)), dma((2,)), dma((2,)), dma((2,)),
            dma((1,)), dma((1,)),
        ] + [pltpu.VMEM((4, 2, 2, 80, 640), low)] * 3 + [
        ],
        compiler_params=pltpu.CompilerParams(
            collective_id=0, has_side_effects=True, vmem_limit_bytes=60 << 20
        ),
    )(inputs, cot, *weights, tile, pads, cosine, sine, places)


class Scatter:
    def __init__(self, ref, piece, bufs, sems, where):
        first, count, cut = piece
        self.ref, self.cut, self.bufs, self.sems, self.where = ref, cut, bufs, sems, where
        self.rows = pl.ds(first, count)
        self.low, self.high = pl.ds(0, cut), pl.ds(cut, ref.shape[-1] - cut)
        self.copies = []
        self.next = []
        self.stage = 0

    def sem(self, i):
        return (self.sems[0].at[i], self.sems[1].at[i])

    def post(self, makers):
        self.next = makers
        self.copies += makers
        for maker in makers:
            maker().start()

    def arrive(self):
        for maker in self.next:
            maker().wait_recv()

    def start(self):
        z, y, x, c = self.where
        ref, b, rows = self.ref, self.bufs, self.rows
        self.post([
            lambda: remote(ref.at[:, :, 1 - x, rows, self.low], b["a1"], self.sem(0), device(z, y, 1 - x, c)),
            lambda: remote(ref.at[:, 1 - y, :, rows, self.high], b["b1"], self.sem(1), device(z, 1 - y, x, c)),
        ])

    def second(self):
        z, y, x, c = self.where
        ref, b, rows, wide, thin = self.ref, self.bufs, self.rows, self.low, self.high
        f32, low = jnp.float32, jnp.bfloat16
        self.arrive()

        def fold(i, _):
            zi, yi = i // 2, lax.rem(i, 2)
            ref[zi, yi, x, rows, wide] = (ref[zi, yi, x, rows, wide].astype(f32) + b["a1"][zi, yi].astype(f32)).astype(low)
            ref[zi, y, yi, rows, thin] = (ref[zi, y, yi, rows, thin].astype(f32) + b["b1"][zi, yi].astype(f32)).astype(low)
            return 0

        lax.fori_loop(0, 8, fold, 0)
        def along(k):
            other = lax.rem(z + k, 4)
            return remote(ref.at[other, y, :, rows, thin], b["b2"].at[k - 1], self.sem(2 + k), device(other, y, x, c))

        made = [lambda: remote(ref.at[:, 1 - y, x, rows, wide], b["a2"], self.sem(2), device(z, 1 - y, x, c))]
        self.post(made + [functools.partial(along, k) for k in (1, 2, 3)])

    def third(self):
        z, y, x, c = self.where
        ref, b, rows, wide, thin = self.ref, self.bufs, self.rows, self.low, self.high
        f32, low = jnp.float32, jnp.bfloat16
        self.arrive()

        def fold(zi, _):
            ref[zi, y, x, rows, wide] = (ref[zi, y, x, rows, wide].astype(f32) + b["a2"][zi].astype(f32)).astype(low)
            return 0

        lax.fori_loop(0, 4, fold, 0)
        value = ref[z, y, 1 - x, rows, thin].astype(f32)
        for k in range(3):
            value = value + b["b2"][k, 1 - x].astype(f32)
        ref[z, y, 1 - x, rows, thin] = value.astype(low)
        def along(k):
            other = lax.rem(z + k, 4)
            return remote(ref.at[other, y, x, rows, wide], b["a3"].at[k - 1], self.sem(6 + k), device(other, y, x, c))

        made = [lambda: remote(ref.at[z, y, 1 - x, rows, thin], b["b3"], self.sem(6), device(z, y, 1 - x, c))]
        self.post(made + [functools.partial(along, k) for k in (1, 2, 3)])

    def finish(self, out):
        z, y, x, c = self.where
        ref, b, rows = self.ref, self.bufs, self.rows
        f32 = jnp.float32
        self.arrive()
        left = ref[z, y, x, rows, self.low].astype(f32)
        right = ref[z, y, x, rows, self.high].astype(f32) + b["b3"][...].astype(f32)
        for k in range(3):
            left = left + b["a3"][k].astype(f32)
            right = right + b["b2"][k, x].astype(f32)
        out[rows, self.low] = left
        out[rows, self.high] = right
        for maker in self.copies:
            maker().wait_send()


def scatter_buffers(piece, columns):
    first, rows, cut = piece
    rest = columns - cut
    return {
        "a1": (4, 2, rows, cut),
        "a2": (4, rows, cut),
        "a3": (3, rows, cut),
        "b1": (4, 2, rows, rest),
        "b2": (3, 2, rows, rest),
        "b3": (rows, rest),
    }


SLOTS = 4
BACK_PIECES = ((0, 80, 384),)


def backward_kernel(*refs):
    (layer, hidden, slope_in, turned_in, down_in, dy_in, wide_in, weights_in, tiles, x_own, norm_t, heads_in, p_in, oh_in,
     cos_ref, sin_ref, places) = refs[:17]
    (out_layer, out_near, out_far, o_q, o_k, o_v, o_o, o_up, o_down, o_ga, o_gm) = refs[17:28]
    (sums, extra, flat_in, xs_own, hid, shown, part_recv, in_recv, fins, finr, tot, trecv, gain_rows,
     ls, es, er, ss, sr, fs, fr, gs, gr, ps, qs, qr, ys, yr, os) = refs[28:56]
    per = len(BACK_PIECES)
    bufs = []
    rest = refs[56:]
    for i in range(per):
        bufs.append(dict(zip(scatter_buffers(BACK_PIECES[i], 640), rest[6 * i : 6 * i + 6])))
    where = coordinates()
    z, y, x, c = where
    f32, low = jnp.float32, jnp.bfloat16
    dma = pltpu.SemaphoreType.DMA
    across, sibling = device(z, y, 1 - x, c), device(z, y, x, 1 - c)
    mine = pl.ds(pl.multiple_of(640 * c, 128), 640)
    yours = pl.ds(pl.multiple_of(640 * (1 - c), 128), 640)
    sends = []

    def local(src, dst, sem):
        copy = pltpu.make_async_copy(src, dst, sem)
        copy.start()
        return copy

    parts = []
    for n in range(6):
        for i, piece in enumerate(BACK_PIECES):
            held = {k: v.at[n] for k, v in bufs[i].items()}
            m = per * n + i
            parts.append(Scatter(sums.at[n % SLOTS], piece, held, (ss.at[m], sr.at[m]), where))
    outs = (o_down, o_up, o_o, o_v, o_k, o_q)
    active, crossing, done = [], [], []

    def pump(*fresh):
        older = list(active)
        for m in fresh:
            parts[m].start()
        active[:0] = fresh
        for m in older:
            part = parts[m]
            part.stage += 1
            if part.stage == 1:
                part.second()
            elif part.stage == 2:
                part.third()
            elif part.stage == 3:
                n = m // per
                part.finish(fins.at[n])
                if m % per == per - 1:
                    theirs = pl.ds(pl.multiple_of(40 * (1 - c), 8), 40)
                    crossing.append((n, send(fins.at[n, theirs], finr.at[n], (fs.at[n], fr.at[n]), sibling)))
            else:
                active.remove(m)
                done.append(m)
                if m % per == per - 1:
                    n = m // per
                    dict(crossing)[n].wait_recv()
                    own = fins[n, pl.ds(pl.multiple_of(40 * c, 8), 40), :]
                    theirs, first = finr[n], c == 0
                    outs[n][:, :640] = jnp.where(first, own, theirs)
                    outs[n][:, 640:] = jnp.where(first, theirs, own)

    def fold(n):
        def step(i, _):
            zi, yi = i // 2, lax.rem(i, 2)
            for xi in range(2):
                value = sums[n, zi, yi, xi].astype(f32) + extra[n, zi, yi, xi].astype(f32)
                sums[n, zi, yi, xi] = value.astype(low)
            return 0

        lax.fori_loop(0, 8, step, 0)

    load_x = local(x_own, xs_own, ls.at[0])
    load_hid = local(hidden, hid, ls.at[1])
    load_shown = local(layer, shown, ls.at[2])

    def feed_forward(turned, dy, slope, wide, grad_upper, hid_low, give, stage):
        load_down = local(down_in, sums.at[0], ls.at[5])
        load_turned = [local(turned_in.at[k], turned.at[k], ls.at[3 + k]) for k in (1, 0)]
        load_dy = local(dy_in, dy, ls.at[6])
        load_wide = [local(wide_in.at[k], wide.at[k], ls.at[7 + k]) for k in (2, 1, 0)]
        load_slope = local(slope_in, slope, ls.at[10])
        greet(peers_of(*where))
        _, gain_mlp = unpack_gains(tiles)
        given = []

        def product(n, k, right):
            def theirs_step(zi, _):
                rows = pl.ds(pl.multiple_of(zi * 320, 320), 320)
                give[n - 1, zi] = dot(turned[k, rows, :], right[:, yours]).astype(low).reshape(2, 2, 80, 640)
                return 0

            lax.fori_loop(0, 4, theirs_step, 0)
            given.append(send(give.at[n - 1], extra.at[n], (es.at[2 + n], er.at[2 + n]), sibling))

            def own_step(zi, _):
                rows = pl.ds(pl.multiple_of(zi * 320, 320), 320)
                sums[n, zi] = dot(turned[k, rows, :], right[:, mine]).astype(low).reshape(2, 2, 80, 640)
                return 0

            lax.fori_loop(0, 4, own_step, 0)

        load_down.wait()
        pump(*range(per))
        load_dy.wait()
        load_wide[0].wait()
        load_slope.wait()

        def active_step(j, _):
            rows = pl.ds(pl.multiple_of(j * SPAN, SPAN), SPAN)
            total = dot(dy[rows, :640], wide[2, 0].reshape(1280, 640), NT)
            total = total + dot(dy[rows, 640:], wide[2, 1].reshape(1280, 640), NT)
            grad_upper[rows, :] = (total * slope[rows, :].astype(f32)).astype(low)
            return 0

        lax.fori_loop(0, 2, active_step, 0)
        load_turned[0].wait()
        product(1, 1, grad_upper)
        load_wide[1].wait()
        load_hid.wait()
        gain_rows[...] = jnp.zeros_like(gain_rows)

        def hidden_step(j, _):
            rows = pl.ds(pl.multiple_of(j * SPAN, SPAN), SPAN)
            grad_norm = dot(grad_upper[rows, :640], wide[1, 0].reshape(1280, 640), NT)
            grad_norm = grad_norm + dot(grad_upper[rows, 640:], wide[1, 1].reshape(1280, 640), NT)
            value = hid[rows, :]
            scale = lax.rsqrt(jnp.mean(value * value, axis=-1, keepdims=True) + 1e-06)
            scaled = grad_norm * gain_mlp
            mean = jnp.mean(scaled * value, axis=-1, keepdims=True)
            gain_rows[0:1] = gain_rows[0:1] + jnp.sum(grad_norm * value * scale, axis=0, keepdims=True)
            result = dy[rows, :].astype(f32) + scale * scaled - value * (scale * scale * scale) * mean
            hid[rows, :] = result
            hid_low[rows, :] = result.astype(low)
            return 0

        lax.fori_loop(0, 2, hidden_step, 0)
        given[0].wait_recv()
        fold(1)
        pump(*range(per, 2 * per))
        load_wide[2].wait()
        moved = []

        def heads_grad(j, half):
            rows = pl.ds(SPAN * j, SPAN)
            total = dot(hid_low[rows, :640], wide[0, 0, pl.ds(2 * half, 2)].reshape(640, 640), NT)
            return total + dot(hid_low[rows, 640:], wide[0, 1, pl.ds(2 * half, 2)].reshape(640, 640), NT)

        for j in range(2):
            stage[j] = heads_grad(j, 1 - c).astype(low)
            moved.append(send(stage.at[j], flat_in.at[2 * j + c], (es.at[j], er.at[j]), sibling))
        for j in range(2):
            flat_in[2 * j + c] = heads_grad(j, c).astype(low)
        load_turned[1].wait()
        product(2, 0, hid_low)
        for copy in moved:
            copy.wait()
        given[1].wait_recv()
        fold(2)
        for copy in given:
            copy.wait_send()

    tokens = (512, 1280)
    pl.run_scoped(
        feed_forward,
        pltpu.VMEM((2, 1280, 512), low),
        pltpu.VMEM(tokens, low),
        pltpu.VMEM(tokens, low),
        pltpu.VMEM((3, 2, 4, 2, 2, 80, 640), low),
        pltpu.VMEM(tokens, low),
        pltpu.VMEM(tokens, low),
        pltpu.VMEM((2, 4, 2, 2, 80, 640), low),
        pltpu.VMEM((2, 256, 640), low),
    )

    def attention(heads, probs, oh, doh, acc, flat, normt, part_send, in_send, in_own):
        def fetch(h, slot):
            return pltpu.make_async_copy(p_in.at[h], probs.at[slot], ps.at[slot])

        load_heads = local(heads_in, heads, ls.at[3])
        fetch(0, 0).start()
        load_oh = local(oh_in, oh, ls.at[4])
        load_normt = local(norm_t, normt, ls.at[5])
        weights = extra
        load_weights = local(weights_in, weights, ls.at[6])
        pump(*range(2 * per, 3 * per))
        load_shown.wait()
        own_layer = local(shown.at[x], out_layer.at[x], ls.at[7])
        back_layer = send(shown.at[1 - x], out_layer.at[x], (ys.at[1], yr.at[1]), across)
        sends.append(back_layer)

        def spread(b, _):
            rows = pl.ds(pl.multiple_of(b * SPAN, SPAN), SPAN)
            for h, one in enumerate(spread_heads(flat_in[b], places.at[0])):
                doh[h, rows, :] = one.astype(low)
            return 0

        lax.fori_loop(0, 4, spread, 0)
        load_heads.wait()
        load_oh.wait()

        def attend(h, _):
            slot = lax.rem(h, 2)

            @pl.when(h < 7)
            def _():
                fetch(h + 1, 1 - slot).start()

            fetch(h, slot).wait()
            for i in range(4):
                n = SPAN * (i + 1)
                rows = slice(SPAN * i, SPAN * i + SPAN)
                grad = doh[h, rows, :]
                delta = jnp.sum(grad.astype(f32) * oh[h, rows, :].astype(f32), axis=-1, keepdims=True)
                share = probs[slot, :, OFFSETS[i] : OFFSETS[i + 1]]
                grad_share = dot(grad, heads[2, h, :n, :], NT)
                grad_score = (share.astype(f32) * (grad_share - delta)).astype(low)
                grad_query = dot(grad_score, heads[1, h, :n, :]) * (80.0**-0.5)
                grad_key = dot(grad_score, heads[0, h, rows, :], TN)
                grad_value = dot(share, grad, TN)
                heads[0, h, rows, :] = grad_query.astype(low)
                if i > 0:
                    acc[0, : n - SPAN] = acc[0, : n - SPAN] + grad_key[: n - SPAN]
                    acc[1, : n - SPAN] = acc[1, : n - SPAN] + grad_value[: n - SPAN]
                acc[0, n - SPAN : n] = grad_key[n - SPAN :]
                acc[1, n - SPAN : n] = grad_value[n - SPAN :]
            heads[1, h] = acc[0].astype(low)
            heads[2, h] = acc[1].astype(low)
            return 0

        lax.fori_loop(0, 5, attend, 0)
        pump()
        lax.fori_loop(5, 8, attend, 0)
        load_normt.wait()

        def product(t, n):
            def join(b, _):
                rows = pl.ds(pl.multiple_of(b * SPAN, SPAN), SPAN)
                pairs = [jnp.concatenate([heads[t, 2 * g, rows, :], heads[t, 2 * g + 1, rows, :]], axis=1) for g in range(4)]
                if t == 2:
                    flat[t, rows, :] = join_heads(pairs, places.at[0]).astype(low)
                    return 0
                total = 0.0
                for move, table in ((0, cos_ref), (1, sin_ref)):
                    twice = jnp.concatenate([table[rows, :], table[rows, :]], axis=1)
                    turned = [(pair.astype(f32) * twice).astype(low) for pair in pairs]
                    total = total + join_heads(turned, places.at[move])
                flat[t, rows, :] = total.astype(low)
                return 0

            lax.fori_loop(0, 4, join, 0)

            def step(zi, _):
                rows = pl.ds(pl.multiple_of(zi * 320, 320), 320)
                sums[n % SLOTS, zi] = dot(normt[rows, :], flat[t]).astype(low).reshape(2, 2, 80, 640)
                return 0

            lax.fori_loop(0, 4, step, 0)

        product(2, 3)
        pump(*range(3 * per, 4 * per))
        product(1, 4)
        pump(*range(4 * per, 5 * per))
        product(0, 5)
        pump(*range(5 * per, 6 * per))
        load_weights.wait()

        def norm_grad(block):
            rows = pl.ds(pl.multiple_of(block * SPAN, SPAN), SPAN)
            total = dot(flat[0, rows, :], weights[0].reshape(1280, 640), NT)
            for t in (1, 2):
                total = total + dot(flat[t, rows, :], weights[t].reshape(1280, 640), NT)
            return total

        def theirs_step(j, _):
            part_send[j] = norm_grad(2 * j + 1 - c).astype(low)
            return 0

        lax.fori_loop(0, 2, theirs_step, 0)
        swapped = [send(part_send.at[j], part_recv.at[j], (qs.at[j], qr.at[j]), sibling) for j in range(2)]
        gain_attn, _ = unpack_gains(tiles)
        load_x.wait()
        for copy in swapped:
            copy.wait_recv()

        def input_grad(j):
            grad_norm = norm_grad(2 * j + c) + part_recv[j].astype(f32)
            value = xs_own[j].astype(f32)
            scale = lax.rsqrt(jnp.mean(value * value, axis=-1, keepdims=True) + 1e-06)
            scaled = grad_norm * gain_attn
            mean = jnp.mean(scaled * value, axis=-1, keepdims=True)
            gain_rows[1:2] = gain_rows[1:2] + jnp.sum(grad_norm * value * scale, axis=0, keepdims=True)
            rows = pl.ds(pl.multiple_of(j * SPAN, SPAN), SPAN)
            return hid[rows, :] + scale * scaled - value * (scale * scale * scale) * mean

        in_send[...] = input_grad(1 - x).astype(low)
        back = send(in_send, in_recv, (ys.at[0], yr.at[0]), across)
        in_own[...] = input_grad(x)
        own_input = local(in_own, out_near, os.at[0])
        both = gain_rows[0:2]
        for p in range(16):
            tot[p // 4, (p // 2) % 2, p % 2, 0:2, 0:80] = both[:, 80 * p : 80 * p + 80]
        hop = [send(tot, trecv.at[0], (gs.at[0], gr.at[0]), sibling)]
        pump()
        for copy in hop:
            copy.wait()
        tot[...] = tot[...] + trecv[0]
        hop = [send(tot.at[:, :, 1 - x], trecv.at[1, :, :, 0], (gs.at[1], gr.at[1]), device(z, y, 1 - x, c))]
        sends.extend(hop)
        pump()
        for copy in hop:
            copy.wait_recv()
        tot[:, :, x] = tot[:, :, x] + trecv[1, :, :, 0]
        hop = [send(tot.at[:, 1 - y, x], trecv.at[2, :, 0, 0], (gs.at[2], gr.at[2]), device(z, 1 - y, x, c))]
        sends.extend(hop)
        back.wait_recv()
        far_input = local(in_recv, out_far, os.at[1])
        pump()
        for copy in hop:
            copy.wait_recv()
        tot[:, y, x] = tot[:, y, x] + trecv[2, :, 0, 0]
        hop = []
        for k in (1, 2, 3):
            other = lax.rem(z + k, 4)
            hop.append(send(tot.at[other, y, x], trecv.at[3, k, 0, 0], (gs.at[2 + k], gr.at[2 + k]), device(other, y, x, c)))
        sends.extend(hop)
        while active:
            pump()
        for copy in hop:
            copy.wait_recv()
        summed = tot[z, y, x] + trecv[3, 1, 0, 0] + trecv[3, 2, 0, 0] + trecv[3, 3, 0, 0]
        chosen = jnp.where(c == 0, summed[:, :40], summed[:, 40:80])
        o_gm[...] = chosen[0:1]
        o_ga[...] = chosen[1:2]
        own_input.wait()
        far_input.wait()
        own_layer.wait()
        back_layer.wait_recv()
        back.wait_send()
        for copy in swapped + sends + [copy for _, copy in crossing]:
            copy.wait_send()

    pl.run_scoped(
        attention,
        pltpu.VMEM((3, 8, 1024, 128), low),
        pltpu.VMEM((2, 256, 2560), low),
        pltpu.VMEM((8, 1024, 128), low),
        pltpu.VMEM((8, 1024, 128), low),
        pltpu.VMEM((2, 1024, 128), f32),
        pltpu.VMEM((3, 1024, 640), low),
        pltpu.VMEM((1280, 1024), low),
        pltpu.VMEM((2, 256, 1280), low),
        pltpu.VMEM((256, 1280), low),
        pltpu.VMEM((256, 1280), f32),
    )


def backward_part(layer, hidden, slope, turned, down, dy, wide, weights, tiles, x_own, norm_t, heads, p, oh, cosine, sine, places):
    dma = pltpu.SemaphoreType.DMA
    low, f32 = jnp.bfloat16, jnp.float32
    shape = jax.ShapeDtypeStruct
    vmem, anywhere = pl.BlockSpec(memory_space=pltpu.VMEM), pl.BlockSpec(memory_space=pl.ANY)
    row = shape((40, 1280), f32)
    bufs = [pltpu.VMEM((6,) + v, low) for piece in BACK_PIECES for v in scatter_buffers(piece, 640).values()]
    n = 6 * len(BACK_PIECES)
    return pl.pallas_call(
        backward_kernel,
        name="backward_scatter",
        out_shape=(shape((2, 256, 1280), low), shape((256, 1280), f32), shape((256, 1280), low)) + (row,) * 6 + (shape((1, 40), f32),) * 2,
        in_specs=[anywhere] * 8 + [vmem] + [anywhere] * 5 + [vmem] * 3,
        out_specs=(anywhere,) * 3 + (vmem,) * 8,
        scratch_shapes=[
            pltpu.VMEM((SLOTS, 4, 2, 2, 80, 640), low),
            pltpu.VMEM((3, 4, 2, 2, 80, 640), low),
            pltpu.VMEM((4, 256, 640), low),
            pltpu.VMEM((2, 256, 1280), low),
            pltpu.VMEM((512, 1280), f32),
            pltpu.VMEM((2, 256, 1280), low),
            pltpu.VMEM((2, 256, 1280), low),
            pltpu.VMEM((256, 1280), low),
            pltpu.VMEM((6, 80, 640), f32),
            pltpu.VMEM((6, 40, 640), f32),
            pltpu.VMEM((4, 2, 2, 8, 128), f32),
            pltpu.VMEM((4, 4, 2, 2, 8, 128), f32),
            pltpu.VMEM((8, 1280), f32),
            dma((11,)), dma((5,)), dma((5,)), dma((n, 10)), dma((n, 10)), dma((6,)), dma((6,)), dma((6,)), dma((6,)),
            dma((2,)), dma((2,)), dma((2,)), dma((2,)), dma((2,)), dma((2,)),
        ] + bufs,
        compiler_params=pltpu.CompilerParams(
            collective_id=1, has_side_effects=True, vmem_limit_bytes=62 << 20
        ),
    )(layer, hidden.reshape(512, 1280), slope.reshape(512, 1280), turned, down, dy.reshape(512, 1280), wide, weights, tiles,
      x_own, norm_t, heads, p, oh, cosine, sine, places)


def last_kernel(*refs):
    given, made, held = refs[:11], refs[11:21], refs[21:32]
    wide, ins, outs = refs[32:]
    x = lax.axis_index("seq") // 2
    arrivals = [pltpu.make_async_copy(given[i], held[i], ins.at[i]) for i in range(11)]
    for copy in arrivals:
        copy.start()
    leaving = [pltpu.make_async_copy(held[0], made[0], outs.at[0]), pltpu.make_async_copy(held[1], made[1].at[x], outs.at[1])]
    leaving += [pltpu.make_async_copy(held[i], made[i - 1], outs.at[i]) for i in range(3, 11)]
    arrivals[2].wait()
    wide[...] = held[2][...].astype(jnp.float32)
    far = pltpu.make_async_copy(wide, made[1].at[1 - x], outs.at[2])
    far.start()
    for copy, after in zip(arrivals[:2] + arrivals[3:], leaving):
        copy.wait()
        after.start()
    for copy in leaving + [far]:
        copy.wait()


def last_part(layer, near, far, *others):
    shape = jax.ShapeDtypeStruct
    anywhere = pl.BlockSpec(memory_space=pl.ANY)
    given = (layer, near, far) + others
    made = (shape(layer.shape, layer.dtype), shape(layer.shape, near.dtype)) + tuple(shape(o.shape, o.dtype) for o in others)
    return pl.pallas_call(
        last_kernel,
        name="lay_out",
        out_shape=made,
        in_specs=[anywhere] * len(given),
        out_specs=(anywhere,) * len(made),
        scratch_shapes=[pltpu.VMEM(g.shape, g.dtype) for g in given]
        + [pltpu.VMEM(near.shape, near.dtype), pltpu.SemaphoreType.DMA((11,)), pltpu.SemaphoreType.DMA((11,))],
        compiler_params=pltpu.CompilerParams(vmem_limit_bytes=60 << 20),
    )(*given)


def body(
    inputs,
    w_query,
    w_key,
    w_value,
    w_out,
    w_up,
    w_down,
    gain_attn,
    gain_mlp,
    pad_patches,
    cotangent,
):
    contexts, patches, model_width = inputs.shape
    head_count = HEADS
    head_size = HEAD_DIM
    seq_count = lax.axis_size("seq")
    seq_rank = lax.axis_index("seq")
    token_rows = contexts * patches
    shape_heads = (contexts, patches, head_count, head_size)
    shape_flat = (contexts, patches, model_width)
    shards = (w_query, w_key, w_value, w_out, w_up, w_down, gain_attn, gain_mlp)
    gathered = (
        lax.all_gather(shards[0], ("dp", "seq"), axis=0, tiled=True),
        lax.all_gather(shards[1], ("dp", "seq"), axis=0, tiled=True),
        lax.all_gather(shards[2], ("dp", "seq"), axis=0, tiled=True),
        lax.all_gather(shards[3], ("dp", "seq"), axis=0, tiled=True),
        lax.all_gather(shards[4], ("dp", "seq"), axis=0, tiled=True),
        lax.all_gather(shards[5], ("dp", "seq"), axis=0, tiled=True),
        lax.all_gather(shards[6], ("dp", "seq"), axis=0, tiled=True),
        lax.all_gather(shards[7], ("dp", "seq"), axis=0, tiled=True),
    )
    full_q, full_k, full_v, full_o, full_up, full_down, full_ga, full_gm = gathered
    positions = seq_rank * patches + jnp.arange(patches, dtype=jnp.int32)
    cosine, sine = rope_tables(positions, head_size // 2)
    inputs_f = inputs.astype(jnp.float32).reshape(token_rows, model_width)
    gain_one = full_ga.astype(jnp.float32)
    scale_one = rms_scale(inputs_f)
    flat_attn = (inputs_f * scale_one * gain_one).astype(jnp.bfloat16)
    query_lin = jnp.dot(flat_attn, full_q, preferred_element_type=jnp.float32).reshape(shape_heads)
    key_lin = jnp.dot(flat_attn, full_k, preferred_element_type=jnp.float32).reshape(shape_heads)
    value_flat = jnp.dot(flat_attn, full_v, preferred_element_type=jnp.float32).astype(jnp.bfloat16)
    queries = rotate_pairs(query_lin, cosine, sine).astype(jnp.bfloat16)
    key_flat = rotate_pairs(key_lin, cosine, sine).astype(jnp.bfloat16)
    own_blocks = (key_flat.reshape(shape_flat), value_flat.reshape(shape_flat))
    kept = []
    sources = []
    current = own_blocks
    for offset in range(seq_count):
        if offset > 0:
            current = shifted((current[0], current[1]), "seq", 1)
        kept.append(current)
        sources.append(seq_rank - offset)
    stats = []
    for block_pair, source_idx in zip(kept, sources):
        stats.append(
            block_forward(
                queries,
                block_pair[0].reshape(shape_heads),
                block_pair[1].reshape(shape_heads),
                source_idx,
                positions,
                pad_patches,
                patches,
            )
        )
    peaks = jnp.stack([entry[0] for entry in stats])
    masses = jnp.stack([entry[1] for entry in stats])
    partials = jnp.stack([entry[2] for entry in stats])
    summit = jnp.max(peaks, axis=0)
    weights_blk = jnp.exp(peaks - summit[None])
    total = jnp.sum(weights_blk * masses, axis=0)
    attended = (
        jnp.sum(jnp.swapaxes(weights_blk, 2, 3)[..., None] * partials, axis=0)
        / jnp.swapaxes(total, 1, 2)[..., None]
    )
    attn_low = attended.astype(jnp.bfloat16).reshape(token_rows, model_width)
    branch = jnp.dot(attn_low, full_o, preferred_element_type=jnp.float32)
    hidden = inputs_f + branch
    gain_two = full_gm.astype(jnp.float32)
    scale_two = rms_scale(hidden)
    norm_mlp = (hidden * scale_two * gain_two).astype(jnp.bfloat16)
    upper = jnp.dot(norm_mlp, full_up, preferred_element_type=jnp.float32)
    active = jax.nn.silu(upper).astype(jnp.bfloat16)
    mlp_out = jnp.dot(active, full_down, preferred_element_type=jnp.float32)
    layer_out = (hidden + mlp_out).astype(jnp.bfloat16).reshape(shape_flat)
    back_q, back_k, back_v, back_o, back_up, back_down, back_ga, back_gm = gathered
    cot_low = cotangent.reshape(token_rows, model_width)
    cot_full = cot_low.astype(jnp.float32)
    grad_downw = jnp.dot(active.T, cot_low, preferred_element_type=jnp.float32)
    grad_active = jnp.dot(cot_low, back_down.T, preferred_element_type=jnp.float32)
    sigmoid_up = jax.nn.sigmoid(upper)
    grad_upper = (grad_active * sigmoid_up * (1.0 + upper * (1.0 - sigmoid_up))).astype(
        jnp.bfloat16
    )
    grad_upw = jnp.dot(norm_mlp.T, grad_upper, preferred_element_type=jnp.float32)
    grad_norm_mlp = jnp.dot(grad_upper, back_up.T, preferred_element_type=jnp.float32)
    grad_from_mlp, grad_gain_two = rms_back(
        hidden, scale_two, back_gm.astype(jnp.float32), grad_norm_mlp
    )
    grad_hidden = cot_full + grad_from_mlp
    hid_low = grad_hidden.astype(jnp.bfloat16)
    grad_outw = jnp.dot(attn_low.T, hid_low, preferred_element_type=jnp.float32)
    grad_attn = jnp.dot(hid_low, back_o.T, preferred_element_type=jnp.float32).astype(jnp.bfloat16)
    grad_attn_f = grad_attn.astype(jnp.float32).reshape(shape_heads)
    delta = jnp.swapaxes(jnp.sum(grad_attn_f * attended, axis=-1), 1, 2)
    grad_queries = jnp.zeros(shape_heads, jnp.float32)
    carried = (jnp.zeros(shape_flat, jnp.float32), jnp.zeros(shape_flat, jnp.float32))
    for offset in reversed(range(seq_count)):
        block_pair = kept[offset]
        part_q, part_k, part_v = block_backward(
            queries,
            block_pair[0].reshape(shape_heads),
            block_pair[1].reshape(shape_heads),
            sources[offset],
            positions,
            pad_patches,
            patches,
            summit,
            total,
            delta,
            grad_attn_f,
        )
        grad_queries = grad_queries + part_q
        carried = (carried[0] + part_k.reshape(shape_flat), carried[1] + part_v.reshape(shape_flat))
        if offset > 0:
            carried = (
                shifted(carried[0].astype(jnp.bfloat16), "seq", -1).astype(jnp.float32),
                shifted(carried[1].astype(jnp.bfloat16), "seq", -1).astype(jnp.float32),
            )
    grad_keys, grad_values = carried
    scale_factor = head_size ** (-0.5)
    grad_qlin = (
        rotate_back(grad_queries * scale_factor, cosine, sine)
        .astype(jnp.bfloat16)
        .reshape(token_rows, model_width)
    )
    grad_klin = (
        rotate_back(grad_keys.reshape(shape_heads) * scale_factor, cosine, sine)
        .astype(jnp.bfloat16)
        .reshape(token_rows, model_width)
    )
    grad_vlin = grad_values.astype(jnp.bfloat16).reshape(token_rows, model_width)
    grad_qw = jnp.dot(flat_attn.T, grad_qlin, preferred_element_type=jnp.float32)
    grad_kw = jnp.dot(flat_attn.T, grad_klin, preferred_element_type=jnp.float32)
    grad_vw = jnp.dot(flat_attn.T, grad_vlin, preferred_element_type=jnp.float32)
    grad_norm_attn = jnp.dot(grad_qlin, back_q.T, preferred_element_type=jnp.float32)
    grad_norm_attn = grad_norm_attn + jnp.dot(
        grad_klin, back_k.T, preferred_element_type=jnp.float32
    )
    grad_norm_attn = grad_norm_attn + jnp.dot(
        grad_vlin, back_v.T, preferred_element_type=jnp.float32
    )
    grad_from_attn, grad_gain_one = rms_back(
        inputs_f, scale_one, back_ga.astype(jnp.float32), grad_norm_attn
    )
    grad_input = (grad_hidden + grad_from_attn).reshape(shape_flat)
    totals = (
        lax.psum_scatter(grad_qw, ("dp", "seq"), scatter_dimension=0, tiled=True),
        lax.psum_scatter(grad_kw, ("dp", "seq"), scatter_dimension=0, tiled=True),
        lax.psum_scatter(grad_vw, ("dp", "seq"), scatter_dimension=0, tiled=True),
        lax.psum_scatter(grad_outw, ("dp", "seq"), scatter_dimension=0, tiled=True),
        lax.psum_scatter(grad_upw, ("dp", "seq"), scatter_dimension=0, tiled=True),
        lax.psum_scatter(grad_downw, ("dp", "seq"), scatter_dimension=0, tiled=True),
        lax.psum_scatter(grad_gain_one, ("dp", "seq"), scatter_dimension=0, tiled=True),
        lax.psum_scatter(grad_gain_two, ("dp", "seq"), scatter_dimension=0, tiled=True),
    )
    return (
        layer_out,
        grad_input,
        totals[0],
        totals[1],
        totals[2],
        totals[3],
        totals[4],
        totals[5],
        totals[6],
        totals[7],
    )


def tables(length):
    places = np.arange(length, dtype=np.float32)[:, None]
    freqs = np.float32(10000.0) ** (-np.arange(40, dtype=np.float32) / np.float32(40))
    angles = places * freqs[None]
    wide = ((0, 0), (0, 48))
    moves = np.zeros((2, 4, 256, 256), np.float32)
    for g in range(4):
        for head in range(2):
            for entry in range(80):
                base = 80 * (2 * g + head) - 128 * g
                other = entry + 40 if entry < 40 else entry - 40
                moves[0, g, base + entry, 128 * head + entry] = 1.0
                moves[1, g, base + other, 128 * head + entry] = -1.0 if entry < 40 else 1.0
    cosine, sine = (np.pad(np.tile(f(angles), (1, 2)), wide) for f in (np.cos, np.sin))
    return jnp.asarray(cosine), jnp.asarray(sine), jnp.asarray(moves, jnp.bfloat16)


def fast_body(
    inputs, w_query, w_key, w_value, w_out, w_up, w_down, gain_attn, gain_mlp, pad_patches, cotangent
):
    moves = tables(1024)
    tile = jnp.pad(jnp.stack([gain_attn, gain_mlp]).astype(jnp.float32), ((0, 6), (0, 88)))
    weights, wide, tiles, x_own, dy_own, norm_t, heads, p, oh, hidden, layer, slope, turned, down = forward_part(
        inputs, cotangent, (w_query, w_key, w_value, w_out, w_up, w_down), tile, pad_patches, *moves
    )
    results = last_part(*backward_part(
        layer, hidden, slope, turned, down, dy_own, wide, weights, tiles, x_own, norm_t, heads, p, oh, *moves
    ))
    return results[:8] + (results[8].reshape(40), results[9].reshape(40))


def solution(mesh):
    placed = (
        P("dp", "seq", None),
        P(("dp", "seq"), None),
        P(("dp", "seq"), None),
        P(("dp", "seq"), None),
        P(("dp", "seq"), None),
        P(("dp", "seq"), None),
        P(("dp", "seq"), None),
        P(("dp", "seq")),
        P(("dp", "seq")),
        P("dp"),
        P("dp", "seq", None),
    )
    return jax.shard_map(
        fast_body if dict(mesh.shape) == {"dp": 8, "seq": 4} else body,
        mesh=mesh,
        in_specs=placed,
        out_specs=(
            P("dp", "seq", None),
            P("dp", "seq", None),
            P(("dp", "seq"), None),
            P(("dp", "seq"), None),
            P(("dp", "seq"), None),
            P(("dp", "seq"), None),
            P(("dp", "seq"), None),
            P(("dp", "seq"), None),
            P(("dp", "seq")),
            P(("dp", "seq")),
        ),
        check_vma=False,
    )
```

```python
import functools

import jax
import jax.numpy as jnp
import numpy as np
from jax import lax
from jax.experimental import pallas as pl
from jax.experimental.pallas import tpu as pltpu
from jax.sharding import PartitionSpec as P

HEADS = 16
HEAD_DIM = 80


def shifted(value, axis, steps):
    count = lax.axis_size(axis)
    initial, last = (max(0, -steps), min(count, count - steps))
    return lax.ppermute(value, axis, [(source, source + steps) for source in range(initial, last)])


def rms_scale(values):
    return lax.rsqrt(jnp.mean(values * values, axis=-1, keepdims=True) + 1e-06)


def rms_back(values, scale, gain, grad_norm):
    scaled_grad = grad_norm * gain
    grad_gain = jnp.sum(grad_norm * values * scale, axis=0)
    grad_values = scale * scaled_grad - values * (scale * scale * scale) * jnp.mean(
        scaled_grad * values, axis=-1, keepdims=True
    )
    return (grad_values, grad_gain)


def rope_tables(positions, half):
    freqs = 10000.0 ** (-jnp.arange(half, dtype=jnp.float32) / half)
    angles = positions[:, None].astype(jnp.float32) * freqs[None, :]
    return (jnp.cos(angles), jnp.sin(angles))


def rotate_pairs(tensor, cosine, sine):
    half = tensor.shape[-1] // 2
    first = tensor[..., :half]
    second = tensor[..., half:]
    cos_b = cosine[None, :, None, :]
    sin_b = sine[None, :, None, :]
    return jnp.concatenate(
        [first * cos_b - second * sin_b, first * sin_b + second * cos_b], axis=-1
    )


def rotate_back(tensor, cosine, sine):
    half = tensor.shape[-1] // 2
    first = tensor[..., :half]
    second = tensor[..., half:]
    cos_b = cosine[None, :, None, :]
    sin_b = sine[None, :, None, :]
    return jnp.concatenate(
        [first * cos_b + second * sin_b, second * cos_b - first * sin_b], axis=-1
    )


def block_weights(queries, key_block, source, positions, pad_patches, patches):
    scale_factor = queries.shape[-1] ** (-0.5)
    scores = scale_factor * jnp.einsum(
        "sqhd,skhd->shqk", queries, key_block, preferred_element_type=jnp.float32
    )
    key_pos = source * patches + jnp.arange(patches, dtype=jnp.int32)
    key_grid = key_pos[None, None, :]
    query_grid = positions[None, :, None]
    allowed = (
        (key_grid <= query_grid)
        & ((key_grid >= pad_patches[:, None, None]) | (key_grid == query_grid))
        & (source >= 0)
    )
    allowed = allowed[:, None]
    masked = jnp.where(allowed, scores, -1e30)
    peaks = jnp.max(masked, axis=-1)
    expo = jnp.exp(masked - peaks[..., None]) * allowed.astype(jnp.float32)
    return (expo, peaks)


def block_forward(queries, key_block, value_block, source, positions, pad_patches, patches):
    expo, peaks = block_weights(queries, key_block, source, positions, pad_patches, patches)
    masses = jnp.sum(expo, axis=-1)
    partials = jnp.einsum(
        "shqk,skhd->sqhd",
        expo.astype(jnp.bfloat16),
        value_block,
        preferred_element_type=jnp.float32,
    )
    return (peaks, masses, partials)


def block_backward(
    queries,
    key_block,
    value_block,
    source,
    positions,
    pad_patches,
    patches,
    summit,
    total,
    delta,
    grad_attn,
):
    expo, peaks = block_weights(queries, key_block, source, positions, pad_patches, patches)
    share = jnp.exp(peaks - summit) / total
    share_tok = jnp.swapaxes(share, 1, 2)[..., None]
    grad_part = (share_tok * grad_attn).astype(jnp.bfloat16)
    grad_vblock = jnp.einsum(
        "shqk,sqhd->skhd", expo.astype(jnp.bfloat16), grad_part, preferred_element_type=jnp.float32
    )
    grad_prob = jnp.einsum(
        "sqhd,skhd->shqk", grad_part, value_block, preferred_element_type=jnp.float32
    )
    grad_scores = (expo * (grad_prob - (share * delta)[..., None])).astype(jnp.bfloat16)
    grad_qblock = jnp.einsum(
        "shqk,skhd->sqhd", grad_scores, key_block, preferred_element_type=jnp.float32
    )
    grad_kblock = jnp.einsum(
        "shqk,sqhd->skhd", grad_scores, queries, preferred_element_type=jnp.float32
    )
    return (grad_qblock, grad_kblock, grad_vblock)


MESH_ID = pl.DeviceIdType.MESH
PIECES = ((0, 48, 384), (48, 32, 256))


def coordinates():
    dp = lax.axis_index("dp")
    seq = lax.axis_index("seq")
    return (dp // 2, lax.rem(dp, 2), seq // 2, lax.rem(seq, 2))


def device(z, y, x, c):
    return (z * 2 + y, x * 2 + c)


def peers_of(z, y, x, c):
    along = [device(lax.rem(z + k, 4), y, x, c) for k in (1, 2, 3)]
    return along + [device(z, 1 - y, x, c), device(z, y, 1 - x, c), device(z, y, x, 1 - c)]


def greet(peers):
    barrier = pltpu.get_barrier_semaphore()
    for peer in peers:
        pl.semaphore_signal(barrier, inc=1, device_id=peer, device_id_type=MESH_ID)
    pl.semaphore_wait(barrier, len(peers))


def remote(src, dst, sems, peer):
    return pltpu.make_async_remote_copy(
        src_ref=src,
        dst_ref=dst,
        send_sem=sems[0],
        recv_sem=sems[1],
        device_id=peer,
        device_id_type=MESH_ID,
    )


def send(src, dst, sems, peer):
    copy = remote(src, dst, sems, peer)
    copy.start()
    return copy


class Gather:
    def __init__(self, ref, piece, sems, where):
        first, count, cut = piece
        self.ref, self.sems, self.where = ref, sems, where
        self.rows = pl.ds(first, count)
        self.low, self.high = pl.ds(0, cut), pl.ds(cut, ref.shape[-1] - cut)
        self.copies = [[], [], []]
        self.phase = 0

    def sem(self, i):
        return (self.sems[0].at[i], self.sems[1].at[i])

    def start(self):
        z, y, x, c = self.where
        ref, rows, low, high = self.ref, self.rows, self.low, self.high
        phase = self.phase
        made = []
        if phase == 0:
            block = ref.at[z, y, x, rows, low]
            for k in (1, 2, 3):
                made.append(send(block, block, self.sem(k - 1), device(lax.rem(z + k, 4), y, x, c)))
            block = ref.at[z, y, x, rows, high]
            made.append(send(block, block, self.sem(3), device(z, y, 1 - x, c)))
        elif phase == 1:
            block = ref.at[:, y, x, rows, low]
            made.append(send(block, block, self.sem(4), device(z, 1 - y, x, c)))
            block = ref.at[z, y, :, rows, high]
            for k in (1, 2, 3):
                made.append(send(block, block, self.sem(4 + k), device(lax.rem(z + k, 4), y, x, c)))
        else:
            block = ref.at[:, :, x, rows, low]
            made.append(send(block, block, self.sem(8), device(z, y, 1 - x, c)))
            block = ref.at[:, y, :, rows, high]
            made.append(send(block, block, self.sem(9), device(z, 1 - y, x, c)))
        self.copies[phase] = made
        self.phase = phase + 1

    def arrive(self, phase):
        for copy in self.copies[phase]:
            copy.wait_recv()

    def sent(self):
        for made in self.copies:
            for copy in made:
                copy.wait_send()


HEADS_HERE = 8
SPAN = 256
OFFSETS = (0, 256, 768, 1536, 2560)
NT = (((1,), (1,)), ((), ()))
TN = (((0,), (0,)), ((), ()))


def dot(a, b, dims=(((1,), (0,)), ((), ()))):
    return lax.dot_general(a, b, dims, preferred_element_type=jnp.float32)


def unpack_gains(tiles):
    rows = []
    for z in range(4):
        for y in range(2):
            for x in range(2):
                for c in range(2):
                    rows.append(tiles[z, y, x, c][:, :40])
    full = jnp.concatenate(rows, axis=1)
    return full[0:1], full[1:2]


def spread_heads(value, place):
    for g in range(4):
        pair = dot(value[:, 128 * g : 128 * g + 256], place[g])
        yield pair[:, :128]
        yield pair[:, 128:]


def join_heads(pairs, place):
    wide = [dot(pair, place[g], NT) for g, pair in enumerate(pairs)]
    tiles = [wide[0][:, :128]]
    for g in range(1, 4):
        tiles.append(wide[g - 1][:, 128:] + wide[g][:, :128])
    tiles.append(wide[3][:, 128:])
    return jnp.concatenate(tiles, axis=1)


def join_some(pairs, place, part):
    wide = {g: dot(pair, place[g], NT) for g, pair in pairs.items()}
    if part == 0:
        return jnp.concatenate([wide[0][:, :128], wide[0][:, 128:] + wide[1][:, :128]], axis=1)
    middle = [wide[g - 1][:, 128:] + wide[g][:, :128] for g in (2, 3)]
    return jnp.concatenate(middle + [wide[3][:, 128:]], axis=1)


def forward_kernel(*refs):
    (inputs, cot), weights, tile, pads, cos_ref, sin_ref, places = refs[:2], refs[2:8], refs[8], refs[9], refs[10], refs[11], refs[12]
    (out_qkv, out_wide, tiles, x_own, dy_own, norm_t, out_heads, out_p, out_oh, out_hidden, out_layer, out_slope,
     out_turned, out_down) = refs[13:27]
    (narrow, wide, own, other, held, held_dy, norm, normt, heads, probs, oh, flat, masks, attn, hidden, low_norm, active,
     slope, layer, turned_t,
     ssem, rsem, gs, gr, hs, hr, xs, osem, ws, wr, ns, nr, ls, ps, als, alr, gives, giver, give, extra, total) = refs[27:]
    where = coordinates()
    z, y, x, c = where
    f32, low = jnp.float32, jnp.bfloat16
    across, sibling = device(z, y, 1 - x, c), device(z, y, x, 1 - c)
    keep = pltpu.make_async_copy(inputs.at[x], held.at[x], ls.at[0])
    keep.start()
    keep_dy = pltpu.make_async_copy(cot.at[x], held_dy.at[x], ls.at[1])
    keep_dy.start()
    greet(peers_of(*where))
    for w in range(6):
        for h in range(2):
            own[h, w] = weights[w][:, 640 * h : 640 * h + 640].astype(f32)
    tiles[z, y, x, c] = tile[...]
    pair = send(own.at[1 - c], other, (xs.at[0], xs.at[1]), sibling)
    pair_tile = send(tiles.at[z, y, x, c], tiles.at[z, y, x, c], (xs.at[2], xs.at[3]), sibling)
    pair.wait_recv()
    pair_tile.wait_recv()
    steps, shares, stores, sends = [], {}, [], [pair, pair_tile]

    def place(w):
        return narrow.at[w] if w < 3 else wide.at[w - 3, c]

    for w in range(6):
        mine, theirs = own[c, w], other[w]
        first = c == 0
        block = jnp.concatenate([jnp.where(first, mine, theirs), jnp.where(first, theirs, mine)], axis=0)
        place(w)[z, y, x] = block.astype(low)
        for i, piece in enumerate(PIECES):
            n = len(steps)
            steps.append(Gather(place(w), piece, (ssem.at[n], rsem.at[n]), where))

    def tile_step(i, block, peers):
        return [send(block, block, (gs.at[i + j], gr.at[i + j]), peer) for j, peer in enumerate(peers)]

    state = {"made": tile_step(0, tiles.at[z, y, x], [device(lax.rem(z + k, 4), y, x, c) for k in (1, 2, 3)])}

    def store(src, dst, sem):
        copy = pltpu.make_async_copy(src, dst, sem)
        copy.start()
        stores.append(copy)

    per = len(PIECES)
    count = 6 * per

    def settle(n):
        w, i = n // per, n % per
        if w < 3:
            if i == per - 1:
                store(narrow.at[w], out_qkv.at[w], osem.at[w])
            return
        part = wide.at[w - 3, c, :, :, :, pl.ds(PIECES[i][0], PIECES[i][1])]
        shares.setdefault(w, []).append(send(part, part, (hs.at[n], hr.at[n]), sibling))

    def whole(w):
        for copy in shares[w]:
            copy.wait_recv()
        sends.extend(shares[w])
        store(wide.at[w - 3], out_wide.at[w - 3], osem.at[w])

    swaps = []

    def swap(src, dst):
        n, i = len(swaps), len(swaps) % 4
        rows = pl.ds(64 * i, 64)
        swaps.append(send(src.at[1 - x, rows], dst.at[x, rows], (ws.at[n], wr.at[n]), across))
        sends.append(swaps[n])

    def advance(t):
        if t < count:
            steps[t].start()
        if 0 <= t - 1 < count:
            steps[t - 1].arrive(0)
            steps[t - 1].start()
        if t in (1, 2, 3):
            for m in state["made"]:
                m.wait_recv()
            sends.extend(state["made"])
            state["made"] = []
        if t == 1:
            state["made"] = tile_step(3, tiles.at[:, y, x], [device(z, 1 - y, x, c)])
        if t == 2:
            state["made"] = tile_step(4, tiles.at[:, :, x], [device(z, y, 1 - x, c)])
        if 0 <= t - 2 < count:
            steps[t - 2].arrive(1)
            steps[t - 2].start()
        if t < 3:
            swap(inputs, held)
            if t == 2:
                swap(inputs, held)
        if 7 <= t < 11:
            swap(cot, held_dy)
        if 0 <= t - 3 < count:
            steps[t - 3].arrive(2)
            settle(t - 3)

    advance(0)
    pad = pads[x]
    row = lax.broadcasted_iota(jnp.int32, (SPAN, SPAN), 0)
    col = lax.broadcasted_iota(jnp.int32, (SPAN, SPAN), 1)
    for i in range(4):
        good = (col <= row) & ((col + SPAN * i >= pad) | (col == row))
        masks[i] = jnp.where(good, 0.0, -1e30).astype(f32)
    before = jnp.where(lax.broadcasted_iota(jnp.int32, (1, 3 * SPAN), 1) >= pad, 0.0, -1e30).astype(f32)
    advance(1)
    advance(2)
    advance(3)
    keep.wait()
    for copy in swaps:
        copy.wait_recv()
    gain_attn, gain_mlp = unpack_gains(tiles)
    passed = []
    for j in range(2):
        value = held[j].astype(f32)
        scale = lax.rsqrt(jnp.mean(value * value, axis=-1, keepdims=True) + 1e-06)
        block = 2 * j + c
        norm[block] = (value * scale * gain_attn).astype(low)
        passed.append(send(norm.at[block], norm.at[block], (ns.at[j], nr.at[j]), sibling))
    store(held, x_own, ls.at[2])
    sends.extend(passed)
    advance(4)
    for copy in passed:
        copy.wait_recv()

    def project(t):
        def step(b, _):
            rows = pl.ds(pl.multiple_of(b * SPAN, SPAN), SPAN)
            value = dot(norm[b], narrow[t].reshape(1280, 640)).astype(low)
            plain = spread_heads(value, places.at[0])
            if t < 2:
                cosine, sine = cos_ref[rows, :], sin_ref[rows, :]
                if t == 0:
                    cosine, sine = cosine * (80.0**-0.5), sine * (80.0**-0.5)
                for h, (one, two) in enumerate(zip(plain, spread_heads(value, places.at[1]))):
                    heads[t, h, rows, :] = (one * cosine + two * sine).astype(low)
            else:
                for h, one in enumerate(plain):
                    heads[t, h, rows, :] = one.astype(low)
            if t == 0:
                normt[:, rows] = jnp.transpose(norm[b])
            return 0

        lax.fori_loop(0, 4, step, 0)

    project(0)
    store(normt, norm_t, ls.at[3])
    advance(5)
    advance(6)
    project(1)
    advance(7)
    advance(8)
    project(2)
    store(heads, out_heads, ls.at[4])

    def attend(h, _):
        slot = lax.rem(h, 2)

        @pl.when(h >= 2)
        def _():
            pltpu.make_async_copy(probs.at[slot], out_p.at[h - 2], ps.at[slot]).wait()

        for i in range(4):
            n = SPAN * (i + 1)
            rows = slice(SPAN * i, SPAN * i + SPAN)
            score = dot(heads[0, h, rows, :], heads[1, h, :n, :], NT)
            last = score[:, n - SPAN :] + masks[i]
            score = last if i == 0 else jnp.concatenate([score[:, : n - SPAN] + before[:, : n - SPAN], last], axis=1)
            peak = jnp.max(score, axis=-1, keepdims=True)
            expo = jnp.exp(score - peak)
            share = (expo * (1.0 / jnp.sum(expo, axis=-1, keepdims=True))).astype(low)
            probs[slot, :, OFFSETS[i] : OFFSETS[i + 1]] = share
            oh[h, rows, :] = dot(share, heads[2, h, :n, :]).astype(low)
        pltpu.make_async_copy(probs.at[slot], out_p.at[h], ps.at[slot]).start()
        return 0

    lax.fori_loop(0, 2, attend, 0)
    advance(9)
    lax.fori_loop(2, 4, attend, 0)
    advance(10)
    lax.fori_loop(4, 6, attend, 0)
    advance(11)
    lax.fori_loop(6, 8, attend, 0)
    store(oh, out_oh, ls.at[5])

    def flatten(b, _):
        rows = pl.ds(pl.multiple_of(b * SPAN, SPAN), SPAN)
        pairs = [jnp.concatenate([oh[2 * g, rows, :], oh[2 * g + 1, rows, :]], axis=1) for g in range(4)]
        flat[b] = join_heads(pairs, places.at[0]).astype(low)
        return 0

    lax.fori_loop(0, 4, flatten, 0)
    columns = pl.ds(pl.multiple_of(640 * c, 128), 640)
    joined = []
    for j in range(2):
        attn[j, :, columns] = flat[2 * j + c]
        joined.append(send(flat.at[2 * j + 1 - c], attn.at[j, :, columns], (als.at[j], alr.at[j]), sibling))
    sends.extend(joined)
    advance(12)
    for copy in joined:
        copy.wait_recv()
    whole(3)

    def out_step(j, _):
        rows = pl.ds(pl.multiple_of(j * SPAN, SPAN), SPAN)
        for h in range(2):
            lanes = slice(640 * h, 640 * h + 640)
            branch = dot(attn[j], wide[0, h].reshape(1280, 640))
            hidden[j, :, lanes] = held[j, :, lanes].astype(f32) + branch
        value = hidden[j]
        scale = lax.rsqrt(jnp.mean(value * value, axis=-1, keepdims=True) + 1e-06)
        low_norm[j] = (value * scale * gain_mlp).astype(low)
        turned_t[0, :, rows] = jnp.transpose(attn[j])
        turned_t[1, :, rows] = jnp.transpose(low_norm[j])
        return 0

    lax.fori_loop(0, 2, out_step, 0)
    store(hidden, out_hidden, ls.at[6])
    advance(13)
    whole(4)

    def up_step(j, _):
        rows = pl.ds(pl.multiple_of(j * SPAN, SPAN), SPAN)
        for h in range(2):
            lanes = slice(640 * h, 640 * h + 640)
            upper = dot(low_norm[j], wide[1, h].reshape(1280, 640))
            gate = 1.0 / (1.0 + jnp.exp(-upper))
            active[j, :, lanes] = (upper * gate).astype(low)
            slope[j, :, lanes] = (gate * (1.0 + upper * (1.0 - gate))).astype(low)
        turned_t[2, :, rows] = jnp.transpose(active[j])
        return 0

    lax.fori_loop(0, 2, up_step, 0)
    store(slope, out_slope, ls.at[7])
    store(turned_t, out_turned, ls.at[8])
    for copy in swaps[4:]:
        copy.wait_recv()
    keep_dy.wait()
    store(held_dy, dy_own, ls.at[9])
    yours = pl.ds(pl.multiple_of(640 * (1 - c), 128), 640)

    def grad_step(zi, half, ref):
        rows = pl.ds(pl.multiple_of(zi * 320, 320), 320)
        value = dot(turned_t[2, rows, :256], held_dy[0, :, half]) + dot(turned_t[2, rows, 256:], held_dy[1, :, half])
        ref[zi] = value.astype(low).reshape(2, 2, 80, 640)
        return 0

    lax.fori_loop(0, 4, lambda zi, _: grad_step(zi, yours, give), 0)
    given = send(give, extra, (gives.at[0], giver.at[0]), sibling)
    sends.append(given)
    advance(14)
    lax.fori_loop(0, 4, lambda zi, _: grad_step(zi, columns, total), 0)
    given.wait_recv()

    def fold(i, _):
        zi, yi = i // 2, lax.rem(i, 2)
        for xi in range(2):
            total[zi, yi, xi] = (total[zi, yi, xi].astype(f32) + extra[zi, yi, xi].astype(f32)).astype(low)
        return 0

    lax.fori_loop(0, 8, fold, 0)
    store(total, out_down, ls.at[11])
    whole(5)

    def down_step(j, _):
        for h in range(2):
            lanes = slice(640 * h, 640 * h + 640)
            value = hidden[j, :, lanes] + dot(active[j], wide[2, h].reshape(1280, 640))
            layer[j, :, lanes] = value.astype(low)
        return 0

    lax.fori_loop(0, 2, down_step, 0)
    store(layer, out_layer, ls.at[10])
    for h in (6, 7):
        pltpu.make_async_copy(probs.at[h % 2], out_p.at[h], ps.at[h % 2]).wait()
    for item in steps:
        item.sent()
    for copy in sends:
        copy.wait_send()
    for copy in stores:
        copy.wait()


def forward_part(inputs, cot, weights, tile, pads, cosine, sine, places):
    dma = pltpu.SemaphoreType.DMA
    low, f32 = jnp.bfloat16, jnp.float32
    shape = jax.ShapeDtypeStruct
    vmem, anywhere = pl.BlockSpec(memory_space=pltpu.VMEM), pl.BlockSpec(memory_space=pl.ANY)
    tokens = (2, 256, 1280)
    n = 6 * len(PIECES)
    return pl.pallas_call(
        forward_kernel,
        name="gather_forward",
        out_shape=(
            shape((3, 4, 2, 2, 80, 640), low),
            shape((3, 2, 4, 2, 2, 80, 640), low),
            shape((4, 2, 2, 2, 8, 128), f32),
            shape(tokens, low),
            shape(tokens, low),
            shape((1280, 1024), low),
            shape((3, 8, 1024, 128), low),
            shape((8, 256, 2560), low),
            shape((8, 1024, 128), low),
            shape(tokens, f32),
            shape(tokens, low),
            shape(tokens, low),
            shape((3, 1280, 512), low),
            shape((4, 2, 2, 80, 640), low),
        ),
        in_specs=[anywhere] * 2 + [vmem] * 7 + [pl.BlockSpec(memory_space=pltpu.SMEM)] + [vmem] * 3,
        out_specs=(anywhere,) * 2 + (vmem,) + (anywhere,) * 11,
        scratch_shapes=[
            pltpu.VMEM((3, 4, 2, 2, 80, 640), low),
            pltpu.VMEM((3, 2, 4, 2, 2, 80, 640), low),
            pltpu.VMEM((2, 6, 40, 640), f32),
            pltpu.VMEM((6, 40, 640), f32),
            pltpu.VMEM(tokens, low),
            pltpu.VMEM(tokens, low),
            pltpu.VMEM((4, 256, 1280), low),
            pltpu.VMEM((1280, 1024), low),
            pltpu.VMEM((3, 8, 1024, 128), low),
            pltpu.VMEM((2, 256, 2560), low),
            pltpu.VMEM((8, 1024, 128), low),
            pltpu.VMEM((4, 256, 640), low),
            pltpu.VMEM((4, 256, 256), f32),
            pltpu.VMEM(tokens, low),
            pltpu.VMEM(tokens, f32),
            pltpu.VMEM(tokens, low),
            pltpu.VMEM(tokens, low),
            pltpu.VMEM(tokens, low),
            pltpu.VMEM(tokens, low),
            pltpu.VMEM((3, 1280, 512), low),
            dma((n, 10)), dma((n, 10)), dma((5,)), dma((5,)), dma((n,)), dma((n,)), dma((4,)), dma((6,)),
            dma((8,)), dma((8,)), dma((2,)), dma((2,)), dma((12,)), dma((2,)), dma((2,)), dma((2,)),
            dma((1,)), dma((1,)),
        ] + [pltpu.VMEM((4, 2, 2, 80, 640), low)] * 3 + [
        ],
        compiler_params=pltpu.CompilerParams(
            collective_id=0, has_side_effects=True, vmem_limit_bytes=60 << 20
        ),
    )(inputs, cot, *weights, tile, pads, cosine, sine, places)


class Scatter:
    def __init__(self, ref, piece, bufs, sems, where):
        first, count, cut = piece
        self.ref, self.cut, self.bufs, self.sems, self.where = ref, cut, bufs, sems, where
        self.rows = pl.ds(first, count)
        self.low, self.high = pl.ds(0, cut), pl.ds(cut, ref.shape[-1] - cut)
        self.copies = []
        self.next = []
        self.stage = 0

    def sem(self, i):
        return (self.sems[0].at[i], self.sems[1].at[i])

    def post(self, makers):
        self.next = makers
        self.copies += makers
        for maker in makers:
            maker().start()

    def arrive(self):
        for maker in self.next:
            maker().wait_recv()

    def start(self):
        z, y, x, c = self.where
        ref, b, rows = self.ref, self.bufs, self.rows
        self.post([
            lambda: remote(ref.at[:, :, 1 - x, rows, self.low], b["a1"], self.sem(0), device(z, y, 1 - x, c)),
            lambda: remote(ref.at[:, 1 - y, :, rows, self.high], b["b1"], self.sem(1), device(z, 1 - y, x, c)),
        ])

    def second(self):
        z, y, x, c = self.where
        ref, b, rows, wide, thin = self.ref, self.bufs, self.rows, self.low, self.high
        f32, low = jnp.float32, jnp.bfloat16
        self.arrive()

        def fold(i, _):
            zi, yi = i // 2, lax.rem(i, 2)
            ref[zi, yi, x, rows, wide] = (ref[zi, yi, x, rows, wide].astype(f32) + b["a1"][zi, yi].astype(f32)).astype(low)
            ref[zi, y, yi, rows, thin] = (ref[zi, y, yi, rows, thin].astype(f32) + b["b1"][zi, yi].astype(f32)).astype(low)
            return 0

        lax.fori_loop(0, 8, fold, 0)
        def along(k):
            other = lax.rem(z + k, 4)
            return remote(ref.at[other, y, :, rows, thin], b["b2"].at[k - 1], self.sem(2 + k), device(other, y, x, c))

        made = [lambda: remote(ref.at[:, 1 - y, x, rows, wide], b["a2"], self.sem(2), device(z, 1 - y, x, c))]
        self.post(made + [functools.partial(along, k) for k in (1, 2, 3)])

    def third(self):
        z, y, x, c = self.where
        ref, b, rows, wide, thin = self.ref, self.bufs, self.rows, self.low, self.high
        f32, low = jnp.float32, jnp.bfloat16
        self.arrive()

        def fold(zi, _):
            ref[zi, y, x, rows, wide] = (ref[zi, y, x, rows, wide].astype(f32) + b["a2"][zi].astype(f32)).astype(low)
            return 0

        lax.fori_loop(0, 4, fold, 0)
        value = ref[z, y, 1 - x, rows, thin].astype(f32)
        for k in range(3):
            value = value + b["b2"][k, 1 - x].astype(f32)
        ref[z, y, 1 - x, rows, thin] = value.astype(low)
        def along(k):
            other = lax.rem(z + k, 4)
            return remote(ref.at[other, y, x, rows, wide], b["a3"].at[k - 1], self.sem(6 + k), device(other, y, x, c))

        made = [lambda: remote(ref.at[z, y, 1 - x, rows, thin], b["b3"], self.sem(6), device(z, y, 1 - x, c))]
        self.post(made + [functools.partial(along, k) for k in (1, 2, 3)])

    def finish(self, out):
        z, y, x, c = self.where
        ref, b, rows = self.ref, self.bufs, self.rows
        f32 = jnp.float32
        self.arrive()
        left = ref[z, y, x, rows, self.low].astype(f32)
        right = ref[z, y, x, rows, self.high].astype(f32) + b["b3"][...].astype(f32)
        for k in range(3):
            left = left + b["a3"][k].astype(f32)
            right = right + b["b2"][k, x].astype(f32)
        out[rows, self.low] = left
        out[rows, self.high] = right
        for maker in self.copies:
            maker().wait_send()


def scatter_buffers(piece, columns):
    first, rows, cut = piece
    rest = columns - cut
    return {
        "a1": (4, 2, rows, cut),
        "a2": (4, rows, cut),
        "a3": (3, rows, cut),
        "b1": (4, 2, rows, rest),
        "b2": (3, 2, rows, rest),
        "b3": (rows, rest),
    }


SLOTS = 4
BACK_PIECES = ((0, 80, 384),)


def backward_kernel(*refs):
    (layer, hidden, slope_in, turned_in, down_in, dy_in, wide_in, weights_in, tiles, x_own, norm_t, heads_in, p_in, oh_in,
     cos_ref, sin_ref, places) = refs[:17]
    (out_layer, out_near, out_far, o_q, o_k, o_v, o_o, o_up, o_down, o_ga, o_gm) = refs[17:28]
    (sums, extra, flat_in, xs_own, hid, shown, part_recv, in_recv, fins, finr, tot, trecv, gain_rows,
     ls, es, er, ss, sr, fs, fr, gs, gr, ps, qs, qr, ys, yr, os) = refs[28:56]
    per = len(BACK_PIECES)
    bufs = []
    rest = refs[56:]
    for i in range(per):
        bufs.append(dict(zip(scatter_buffers(BACK_PIECES[i], 640), rest[6 * i : 6 * i + 6])))
    where = coordinates()
    z, y, x, c = where
    f32, low = jnp.float32, jnp.bfloat16
    dma = pltpu.SemaphoreType.DMA
    across, sibling = device(z, y, 1 - x, c), device(z, y, x, 1 - c)
    mine = pl.ds(pl.multiple_of(640 * c, 128), 640)
    yours = pl.ds(pl.multiple_of(640 * (1 - c), 128), 640)
    sends = []

    def local(src, dst, sem):
        copy = pltpu.make_async_copy(src, dst, sem)
        copy.start()
        return copy

    parts = []
    for n in range(6):
        for i, piece in enumerate(BACK_PIECES):
            held = {k: v.at[n] for k, v in bufs[i].items()}
            m = per * n + i
            parts.append(Scatter(sums.at[n % SLOTS], piece, held, (ss.at[m], sr.at[m]), where))
    outs = (o_down, o_up, o_o, o_v, o_k, o_q)
    active, crossing, done = [], [], []

    def pump(*fresh):
        older = list(active)
        for m in fresh:
            parts[m].start()
        active[:0] = fresh
        for m in older:
            part = parts[m]
            part.stage += 1
            if part.stage == 1:
                part.second()
            elif part.stage == 2:
                part.third()
            elif part.stage == 3:
                n = m // per
                part.finish(fins.at[n])
                if m % per == per - 1:
                    theirs = pl.ds(pl.multiple_of(40 * (1 - c), 8), 40)
                    crossing.append((n, send(fins.at[n, theirs], finr.at[n], (fs.at[n], fr.at[n]), sibling)))
            else:
                active.remove(m)
                done.append(m)
                if m % per == per - 1:
                    n = m // per
                    dict(crossing)[n].wait_recv()
                    own = fins[n, pl.ds(pl.multiple_of(40 * c, 8), 40), :]
                    theirs, first = finr[n], c == 0
                    outs[n][:, :640] = jnp.where(first, own, theirs)
                    outs[n][:, 640:] = jnp.where(first, theirs, own)

    def fold(n):
        def step(i, _):
            zi, yi = i // 2, lax.rem(i, 2)
            for xi in range(2):
                value = sums[n, zi, yi, xi].astype(f32) + extra[n, zi, yi, xi].astype(f32)
                sums[n, zi, yi, xi] = value.astype(low)
            return 0

        lax.fori_loop(0, 8, step, 0)

    load_x = local(x_own, xs_own, ls.at[0])
    load_hid = local(hidden, hid, ls.at[1])
    load_shown = local(layer, shown, ls.at[2])

    def feed_forward(turned, dy, slope, wide, grad_upper, hid_low, give, stage):
        load_down = local(down_in, sums.at[0], ls.at[5])
        load_turned = [local(turned_in.at[k], turned.at[k], ls.at[3 + k]) for k in (1, 0)]
        load_dy = local(dy_in, dy, ls.at[6])
        load_wide = [local(wide_in.at[k], wide.at[k], ls.at[7 + k]) for k in (2, 1, 0)]
        load_slope = local(slope_in, slope, ls.at[10])
        greet(peers_of(*where))
        _, gain_mlp = unpack_gains(tiles)
        given = []

        def product(n, k, right):
            def theirs_step(zi, _):
                rows = pl.ds(pl.multiple_of(zi * 320, 320), 320)
                give[n - 1, zi] = dot(turned[k, rows, :], right[:, yours]).astype(low).reshape(2, 2, 80, 640)
                return 0

            lax.fori_loop(0, 4, theirs_step, 0)
            given.append(send(give.at[n - 1], extra.at[n], (es.at[2 + n], er.at[2 + n]), sibling))

            def own_step(zi, _):
                rows = pl.ds(pl.multiple_of(zi * 320, 320), 320)
                sums[n, zi] = dot(turned[k, rows, :], right[:, mine]).astype(low).reshape(2, 2, 80, 640)
                return 0

            lax.fori_loop(0, 4, own_step, 0)

        load_down.wait()
        pump(*range(per))
        load_dy.wait()
        load_wide[0].wait()
        load_slope.wait()

        def active_step(j, _):
            rows = pl.ds(pl.multiple_of(j * SPAN, SPAN), SPAN)
            total = dot(dy[rows, :640], wide[2, 0].reshape(1280, 640), NT)
            total = total + dot(dy[rows, 640:], wide[2, 1].reshape(1280, 640), NT)
            grad_upper[rows, :] = (total * slope[rows, :].astype(f32)).astype(low)
            return 0

        lax.fori_loop(0, 2, active_step, 0)
        load_turned[0].wait()
        product(1, 1, grad_upper)
        load_wide[1].wait()
        load_hid.wait()
        gain_rows[...] = jnp.zeros_like(gain_rows)

        def hidden_step(j, _):
            rows = pl.ds(pl.multiple_of(j * SPAN, SPAN), SPAN)
            grad_norm = dot(grad_upper[rows, :640], wide[1, 0].reshape(1280, 640), NT)
            grad_norm = grad_norm + dot(grad_upper[rows, 640:], wide[1, 1].reshape(1280, 640), NT)
            value = hid[rows, :]
            scale = lax.rsqrt(jnp.mean(value * value, axis=-1, keepdims=True) + 1e-06)
            scaled = grad_norm * gain_mlp
            mean = jnp.mean(scaled * value, axis=-1, keepdims=True)
            gain_rows[0:1] = gain_rows[0:1] + jnp.sum(grad_norm * value * scale, axis=0, keepdims=True)
            result = dy[rows, :].astype(f32) + scale * scaled - value * (scale * scale * scale) * mean
            hid[rows, :] = result
            hid_low[rows, :] = result.astype(low)
            return 0

        lax.fori_loop(0, 2, hidden_step, 0)
        given[0].wait_recv()
        fold(1)
        pump(*range(per, 2 * per))
        load_wide[2].wait()
        moved = []

        def heads_grad(j, half):
            rows = pl.ds(SPAN * j, SPAN)
            total = dot(hid_low[rows, :640], wide[0, 0, pl.ds(2 * half, 2)].reshape(640, 640), NT)
            return total + dot(hid_low[rows, 640:], wide[0, 1, pl.ds(2 * half, 2)].reshape(640, 640), NT)

        for j in range(2):
            stage[j] = heads_grad(j, 1 - c).astype(low)
            moved.append(send(stage.at[j], flat_in.at[2 * j + c], (es.at[j], er.at[j]), sibling))
        for j in range(2):
            flat_in[2 * j + c] = heads_grad(j, c).astype(low)
        load_turned[1].wait()
        product(2, 0, hid_low)
        for copy in moved:
            copy.wait()
        given[1].wait_recv()
        fold(2)
        for copy in given:
            copy.wait_send()

    tokens = (512, 1280)
    pl.run_scoped(
        feed_forward,
        pltpu.VMEM((2, 1280, 512), low),
        pltpu.VMEM(tokens, low),
        pltpu.VMEM(tokens, low),
        pltpu.VMEM((3, 2, 4, 2, 2, 80, 640), low),
        pltpu.VMEM(tokens, low),
        pltpu.VMEM(tokens, low),
        pltpu.VMEM((2, 4, 2, 2, 80, 640), low),
        pltpu.VMEM((2, 256, 640), low),
    )

    def attention(heads, probs, oh, doh, acc, flat, normt, part_send, in_send, in_own):
        def fetch(h, slot):
            return pltpu.make_async_copy(p_in.at[h], probs.at[slot], ps.at[slot])

        load_heads = local(heads_in, heads, ls.at[3])
        fetch(0, 0).start()
        load_oh = local(oh_in, oh, ls.at[4])
        load_normt = local(norm_t, normt, ls.at[5])
        weights = extra
        load_weights = local(weights_in, weights, ls.at[6])
        pump(*range(2 * per, 3 * per))
        load_shown.wait()
        own_layer = local(shown.at[x], out_layer.at[x], ls.at[7])
        back_layer = send(shown.at[1 - x], out_layer.at[x], (ys.at[1], yr.at[1]), across)
        sends.append(back_layer)

        def spread(b, _):
            rows = pl.ds(pl.multiple_of(b * SPAN, SPAN), SPAN)
            for h, one in enumerate(spread_heads(flat_in[b], places.at[0])):
                doh[h, rows, :] = one.astype(low)
            return 0

        lax.fori_loop(0, 4, spread, 0)
        load_heads.wait()
        load_oh.wait()

        def attend(h, _):
            slot = lax.rem(h, 2)

            @pl.when(h < 7)
            def _():
                fetch(h + 1, 1 - slot).start()

            fetch(h, slot).wait()
            for i in range(4):
                n = SPAN * (i + 1)
                rows = slice(SPAN * i, SPAN * i + SPAN)
                grad = doh[h, rows, :]
                delta = jnp.sum(grad.astype(f32) * oh[h, rows, :].astype(f32), axis=-1, keepdims=True)
                share = probs[slot, :, OFFSETS[i] : OFFSETS[i + 1]]
                grad_share = dot(grad, heads[2, h, :n, :], NT)
                grad_score = (share.astype(f32) * (grad_share - delta)).astype(low)
                grad_query = dot(grad_score, heads[1, h, :n, :]) * (80.0**-0.5)
                grad_key = dot(grad_score, heads[0, h, rows, :], TN)
                grad_value = dot(share, grad, TN)
                heads[0, h, rows, :] = grad_query.astype(low)
                if i > 0:
                    acc[0, : n - SPAN] = acc[0, : n - SPAN] + grad_key[: n - SPAN]
                    acc[1, : n - SPAN] = acc[1, : n - SPAN] + grad_value[: n - SPAN]
                acc[0, n - SPAN : n] = grad_key[n - SPAN :]
                acc[1, n - SPAN : n] = grad_value[n - SPAN :]
            heads[1, h] = acc[0].astype(low)
            heads[2, h] = acc[1].astype(low)
            return 0

        lax.fori_loop(0, 5, attend, 0)
        pump()
        lax.fori_loop(5, 8, attend, 0)
        load_normt.wait()

        def product(t, n):
            def join(b, _):
                rows = pl.ds(pl.multiple_of(b * SPAN, SPAN), SPAN)
                pairs = [jnp.concatenate([heads[t, 2 * g, rows, :], heads[t, 2 * g + 1, rows, :]], axis=1) for g in range(4)]
                if t == 2:
                    flat[t, rows, :] = join_heads(pairs, places.at[0]).astype(low)
                    return 0
                total = 0.0
                for move, table in ((0, cos_ref), (1, sin_ref)):
                    twice = jnp.concatenate([table[rows, :], table[rows, :]], axis=1)
                    turned = [(pair.astype(f32) * twice).astype(low) for pair in pairs]
                    total = total + join_heads(turned, places.at[move])
                flat[t, rows, :] = total.astype(low)
                return 0

            lax.fori_loop(0, 4, join, 0)

            def step(zi, _):
                rows = pl.ds(pl.multiple_of(zi * 320, 320), 320)
                sums[n % SLOTS, zi] = dot(normt[rows, :], flat[t]).astype(low).reshape(2, 2, 80, 640)
                return 0

            lax.fori_loop(0, 4, step, 0)

        product(2, 3)
        pump(*range(3 * per, 4 * per))
        product(1, 4)
        pump(*range(4 * per, 5 * per))
        product(0, 5)
        pump(*range(5 * per, 6 * per))
        load_weights.wait()

        def norm_grad(block):
            rows = pl.ds(pl.multiple_of(block * SPAN, SPAN), SPAN)
            total = dot(flat[0, rows, :], weights[0].reshape(1280, 640), NT)
            for t in (1, 2):
                total = total + dot(flat[t, rows, :], weights[t].reshape(1280, 640), NT)
            return total

        def theirs_step(j, _):
            part_send[j] = norm_grad(2 * j + 1 - c).astype(low)
            return 0

        lax.fori_loop(0, 2, theirs_step, 0)
        swapped = [send(part_send.at[j], part_recv.at[j], (qs.at[j], qr.at[j]), sibling) for j in range(2)]
        gain_attn, _ = unpack_gains(tiles)
        load_x.wait()
        for copy in swapped:
            copy.wait_recv()

        def input_grad(j):
            grad_norm = norm_grad(2 * j + c) + part_recv[j].astype(f32)
            value = xs_own[j].astype(f32)
            scale = lax.rsqrt(jnp.mean(value * value, axis=-1, keepdims=True) + 1e-06)
            scaled = grad_norm * gain_attn
            mean = jnp.mean(scaled * value, axis=-1, keepdims=True)
            gain_rows[1:2] = gain_rows[1:2] + jnp.sum(grad_norm * value * scale, axis=0, keepdims=True)
            rows = pl.ds(pl.multiple_of(j * SPAN, SPAN), SPAN)
            return hid[rows, :] + scale * scaled - value * (scale * scale * scale) * mean

        in_send[...] = input_grad(1 - x).astype(low)
        back = send(in_send, in_recv, (ys.at[0], yr.at[0]), across)
        in_own[...] = input_grad(x)
        own_input = local(in_own, out_near, os.at[0])
        both = gain_rows[0:2]
        for p in range(16):
            tot[p // 4, (p // 2) % 2, p % 2, 0:2, 0:80] = both[:, 80 * p : 80 * p + 80]
        hop = [send(tot, trecv.at[0], (gs.at[0], gr.at[0]), sibling)]
        pump()
        for copy in hop:
            copy.wait()
        tot[...] = tot[...] + trecv[0]
        hop = [send(tot.at[:, :, 1 - x], trecv.at[1, :, :, 0], (gs.at[1], gr.at[1]), device(z, y, 1 - x, c))]
        sends.extend(hop)
        pump()
        for copy in hop:
            copy.wait_recv()
        tot[:, :, x] = tot[:, :, x] + trecv[1, :, :, 0]
        hop = [send(tot.at[:, 1 - y, x], trecv.at[2, :, 0, 0], (gs.at[2], gr.at[2]), device(z, 1 - y, x, c))]
        sends.extend(hop)
        back.wait_recv()
        far_input = local(in_recv, out_far, os.at[1])
        pump()
        for copy in hop:
            copy.wait_recv()
        tot[:, y, x] = tot[:, y, x] + trecv[2, :, 0, 0]
        hop = []
        for k in (1, 2, 3):
            other = lax.rem(z + k, 4)
            hop.append(send(tot.at[other, y, x], trecv.at[3, k, 0, 0], (gs.at[2 + k], gr.at[2 + k]), device(other, y, x, c)))
        sends.extend(hop)
        while active:
            pump()
        for copy in hop:
            copy.wait_recv()
        summed = tot[z, y, x] + trecv[3, 1, 0, 0] + trecv[3, 2, 0, 0] + trecv[3, 3, 0, 0]
        chosen = jnp.where(c == 0, summed[:, :40], summed[:, 40:80])
        o_gm[...] = chosen[0:1]
        o_ga[...] = chosen[1:2]
        own_input.wait()
        far_input.wait()
        own_layer.wait()
        back_layer.wait_recv()
        back.wait_send()
        for copy in swapped + sends + [copy for _, copy in crossing]:
            copy.wait_send()

    pl.run_scoped(
        attention,
        pltpu.VMEM((3, 8, 1024, 128), low),
        pltpu.VMEM((2, 256, 2560), low),
        pltpu.VMEM((8, 1024, 128), low),
        pltpu.VMEM((8, 1024, 128), low),
        pltpu.VMEM((2, 1024, 128), f32),
        pltpu.VMEM((3, 1024, 640), low),
        pltpu.VMEM((1280, 1024), low),
        pltpu.VMEM((2, 256, 1280), low),
        pltpu.VMEM((256, 1280), low),
        pltpu.VMEM((256, 1280), f32),
    )


def backward_part(layer, hidden, slope, turned, down, dy, wide, weights, tiles, x_own, norm_t, heads, p, oh, cosine, sine, places):
    dma = pltpu.SemaphoreType.DMA
    low, f32 = jnp.bfloat16, jnp.float32
    shape = jax.ShapeDtypeStruct
    vmem, anywhere = pl.BlockSpec(memory_space=pltpu.VMEM), pl.BlockSpec(memory_space=pl.ANY)
    row = shape((40, 1280), f32)
    bufs = [pltpu.VMEM((6,) + v, low) for piece in BACK_PIECES for v in scatter_buffers(piece, 640).values()]
    n = 6 * len(BACK_PIECES)
    return pl.pallas_call(
        backward_kernel,
        name="backward_scatter",
        out_shape=(shape((2, 256, 1280), low), shape((256, 1280), f32), shape((256, 1280), low)) + (row,) * 6 + (shape((1, 40), f32),) * 2,
        in_specs=[anywhere] * 8 + [vmem] + [anywhere] * 5 + [vmem] * 3,
        out_specs=(anywhere,) * 3 + (vmem,) * 8,
        scratch_shapes=[
            pltpu.VMEM((SLOTS, 4, 2, 2, 80, 640), low),
            pltpu.VMEM((3, 4, 2, 2, 80, 640), low),
            pltpu.VMEM((4, 256, 640), low),
            pltpu.VMEM((2, 256, 1280), low),
            pltpu.VMEM((512, 1280), f32),
            pltpu.VMEM((2, 256, 1280), low),
            pltpu.VMEM((2, 256, 1280), low),
            pltpu.VMEM((256, 1280), low),
            pltpu.VMEM((6, 80, 640), f32),
            pltpu.VMEM((6, 40, 640), f32),
            pltpu.VMEM((4, 2, 2, 8, 128), f32),
            pltpu.VMEM((4, 4, 2, 2, 8, 128), f32),
            pltpu.VMEM((8, 1280), f32),
            dma((11,)), dma((5,)), dma((5,)), dma((n, 10)), dma((n, 10)), dma((6,)), dma((6,)), dma((6,)), dma((6,)),
            dma((2,)), dma((2,)), dma((2,)), dma((2,)), dma((2,)), dma((2,)),
        ] + bufs,
        compiler_params=pltpu.CompilerParams(
            collective_id=1, has_side_effects=True, vmem_limit_bytes=62 << 20
        ),
    )(layer, hidden.reshape(512, 1280), slope.reshape(512, 1280), turned, down, dy.reshape(512, 1280), wide, weights, tiles,
      x_own, norm_t, heads, p, oh, cosine, sine, places)


def last_kernel(*refs):
    given, made, held = refs[:11], refs[11:21], refs[21:32]
    wide, ins, outs = refs[32:]
    x = lax.axis_index("seq") // 2
    arrivals = [pltpu.make_async_copy(given[i], held[i], ins.at[i]) for i in range(11)]
    for copy in arrivals:
        copy.start()
    leaving = [pltpu.make_async_copy(held[0], made[0], outs.at[0]), pltpu.make_async_copy(held[1], made[1].at[x], outs.at[1])]
    leaving += [pltpu.make_async_copy(held[i], made[i - 1], outs.at[i]) for i in range(3, 11)]
    arrivals[2].wait()
    wide[...] = held[2][...].astype(jnp.float32)
    far = pltpu.make_async_copy(wide, made[1].at[1 - x], outs.at[2])
    far.start()
    for copy, after in zip(arrivals[:2] + arrivals[3:], leaving):
        copy.wait()
        after.start()
    for copy in leaving + [far]:
        copy.wait()


def last_part(layer, near, far, *others):
    shape = jax.ShapeDtypeStruct
    anywhere = pl.BlockSpec(memory_space=pl.ANY)
    given = (layer, near, far) + others
    made = (shape(layer.shape, layer.dtype), shape(layer.shape, near.dtype)) + tuple(shape(o.shape, o.dtype) for o in others)
    return pl.pallas_call(
        last_kernel,
        name="lay_out",
        out_shape=made,
        in_specs=[anywhere] * len(given),
        out_specs=(anywhere,) * len(made),
        scratch_shapes=[pltpu.VMEM(g.shape, g.dtype) for g in given]
        + [pltpu.VMEM(near.shape, near.dtype), pltpu.SemaphoreType.DMA((11,)), pltpu.SemaphoreType.DMA((11,))],
        compiler_params=pltpu.CompilerParams(vmem_limit_bytes=60 << 20),
    )(*given)


def body(
    inputs,
    w_query,
    w_key,
    w_value,
    w_out,
    w_up,
    w_down,
    gain_attn,
    gain_mlp,
    pad_patches,
    cotangent,
):
    contexts, patches, model_width = inputs.shape
    head_count = HEADS
    head_size = HEAD_DIM
    seq_count = lax.axis_size("seq")
    seq_rank = lax.axis_index("seq")
    token_rows = contexts * patches
    shape_heads = (contexts, patches, head_count, head_size)
    shape_flat = (contexts, patches, model_width)
    shards = (w_query, w_key, w_value, w_out, w_up, w_down, gain_attn, gain_mlp)
    gathered = (
        lax.all_gather(shards[0], ("dp", "seq"), axis=0, tiled=True),
        lax.all_gather(shards[1], ("dp", "seq"), axis=0, tiled=True),
        lax.all_gather(shards[2], ("dp", "seq"), axis=0, tiled=True),
        lax.all_gather(shards[3], ("dp", "seq"), axis=0, tiled=True),
        lax.all_gather(shards[4], ("dp", "seq"), axis=0, tiled=True),
        lax.all_gather(shards[5], ("dp", "seq"), axis=0, tiled=True),
        lax.all_gather(shards[6], ("dp", "seq"), axis=0, tiled=True),
        lax.all_gather(shards[7], ("dp", "seq"), axis=0, tiled=True),
    )
    full_q, full_k, full_v, full_o, full_up, full_down, full_ga, full_gm = gathered
    positions = seq_rank * patches + jnp.arange(patches, dtype=jnp.int32)
    cosine, sine = rope_tables(positions, head_size // 2)
    inputs_f = inputs.astype(jnp.float32).reshape(token_rows, model_width)
    gain_one = full_ga.astype(jnp.float32)
    scale_one = rms_scale(inputs_f)
    flat_attn = (inputs_f * scale_one * gain_one).astype(jnp.bfloat16)
    query_lin = jnp.dot(flat_attn, full_q, preferred_element_type=jnp.float32).reshape(shape_heads)
    key_lin = jnp.dot(flat_attn, full_k, preferred_element_type=jnp.float32).reshape(shape_heads)
    value_flat = jnp.dot(flat_attn, full_v, preferred_element_type=jnp.float32).astype(jnp.bfloat16)
    queries = rotate_pairs(query_lin, cosine, sine).astype(jnp.bfloat16)
    key_flat = rotate_pairs(key_lin, cosine, sine).astype(jnp.bfloat16)
    own_blocks = (key_flat.reshape(shape_flat), value_flat.reshape(shape_flat))
    kept = []
    sources = []
    current = own_blocks
    for offset in range(seq_count):
        if offset > 0:
            current = shifted((current[0], current[1]), "seq", 1)
        kept.append(current)
        sources.append(seq_rank - offset)
    stats = []
    for block_pair, source_idx in zip(kept, sources):
        stats.append(
            block_forward(
                queries,
                block_pair[0].reshape(shape_heads),
                block_pair[1].reshape(shape_heads),
                source_idx,
                positions,
                pad_patches,
                patches,
            )
        )
    peaks = jnp.stack([entry[0] for entry in stats])
    masses = jnp.stack([entry[1] for entry in stats])
    partials = jnp.stack([entry[2] for entry in stats])
    summit = jnp.max(peaks, axis=0)
    weights_blk = jnp.exp(peaks - summit[None])
    total = jnp.sum(weights_blk * masses, axis=0)
    attended = (
        jnp.sum(jnp.swapaxes(weights_blk, 2, 3)[..., None] * partials, axis=0)
        / jnp.swapaxes(total, 1, 2)[..., None]
    )
    attn_low = attended.astype(jnp.bfloat16).reshape(token_rows, model_width)
    branch = jnp.dot(attn_low, full_o, preferred_element_type=jnp.float32)
    hidden = inputs_f + branch
    gain_two = full_gm.astype(jnp.float32)
    scale_two = rms_scale(hidden)
    norm_mlp = (hidden * scale_two * gain_two).astype(jnp.bfloat16)
    upper = jnp.dot(norm_mlp, full_up, preferred_element_type=jnp.float32)
    active = jax.nn.silu(upper).astype(jnp.bfloat16)
    mlp_out = jnp.dot(active, full_down, preferred_element_type=jnp.float32)
    layer_out = (hidden + mlp_out).astype(jnp.bfloat16).reshape(shape_flat)
    back_q, back_k, back_v, back_o, back_up, back_down, back_ga, back_gm = gathered
    cot_low = cotangent.reshape(token_rows, model_width)
    cot_full = cot_low.astype(jnp.float32)
    grad_downw = jnp.dot(active.T, cot_low, preferred_element_type=jnp.float32)
    grad_active = jnp.dot(cot_low, back_down.T, preferred_element_type=jnp.float32)
    sigmoid_up = jax.nn.sigmoid(upper)
    grad_upper = (grad_active * sigmoid_up * (1.0 + upper * (1.0 - sigmoid_up))).astype(
        jnp.bfloat16
    )
    grad_upw = jnp.dot(norm_mlp.T, grad_upper, preferred_element_type=jnp.float32)
    grad_norm_mlp = jnp.dot(grad_upper, back_up.T, preferred_element_type=jnp.float32)
    grad_from_mlp, grad_gain_two = rms_back(
        hidden, scale_two, back_gm.astype(jnp.float32), grad_norm_mlp
    )
    grad_hidden = cot_full + grad_from_mlp
    hid_low = grad_hidden.astype(jnp.bfloat16)
    grad_outw = jnp.dot(attn_low.T, hid_low, preferred_element_type=jnp.float32)
    grad_attn = jnp.dot(hid_low, back_o.T, preferred_element_type=jnp.float32).astype(jnp.bfloat16)
    grad_attn_f = grad_attn.astype(jnp.float32).reshape(shape_heads)
    delta = jnp.swapaxes(jnp.sum(grad_attn_f * attended, axis=-1), 1, 2)
    grad_queries = jnp.zeros(shape_heads, jnp.float32)
    carried = (jnp.zeros(shape_flat, jnp.float32), jnp.zeros(shape_flat, jnp.float32))
    for offset in reversed(range(seq_count)):
        block_pair = kept[offset]
        part_q, part_k, part_v = block_backward(
            queries,
            block_pair[0].reshape(shape_heads),
            block_pair[1].reshape(shape_heads),
            sources[offset],
            positions,
            pad_patches,
            patches,
            summit,
            total,
            delta,
            grad_attn_f,
        )
        grad_queries = grad_queries + part_q
        carried = (carried[0] + part_k.reshape(shape_flat), carried[1] + part_v.reshape(shape_flat))
        if offset > 0:
            carried = (
                shifted(carried[0].astype(jnp.bfloat16), "seq", -1).astype(jnp.float32),
                shifted(carried[1].astype(jnp.bfloat16), "seq", -1).astype(jnp.float32),
            )
    grad_keys, grad_values = carried
    scale_factor = head_size ** (-0.5)
    grad_qlin = (
        rotate_back(grad_queries * scale_factor, cosine, sine)
        .astype(jnp.bfloat16)
        .reshape(token_rows, model_width)
    )
    grad_klin = (
        rotate_back(grad_keys.reshape(shape_heads) * scale_factor, cosine, sine)
        .astype(jnp.bfloat16)
        .reshape(token_rows, model_width)
    )
    grad_vlin = grad_values.astype(jnp.bfloat16).reshape(token_rows, model_width)
    grad_qw = jnp.dot(flat_attn.T, grad_qlin, preferred_element_type=jnp.float32)
    grad_kw = jnp.dot(flat_attn.T, grad_klin, preferred_element_type=jnp.float32)
    grad_vw = jnp.dot(flat_attn.T, grad_vlin, preferred_element_type=jnp.float32)
    grad_norm_attn = jnp.dot(grad_qlin, back_q.T, preferred_element_type=jnp.float32)
    grad_norm_attn = grad_norm_attn + jnp.dot(
        grad_klin, back_k.T, preferred_element_type=jnp.float32
    )
    grad_norm_attn = grad_norm_attn + jnp.dot(
        grad_vlin, back_v.T, preferred_element_type=jnp.float32
    )
    grad_from_attn, grad_gain_one = rms_back(
        inputs_f, scale_one, back_ga.astype(jnp.float32), grad_norm_attn
    )
    grad_input = (grad_hidden + grad_from_attn).reshape(shape_flat)
    totals = (
        lax.psum_scatter(grad_qw, ("dp", "seq"), scatter_dimension=0, tiled=True),
        lax.psum_scatter(grad_kw, ("dp", "seq"), scatter_dimension=0, tiled=True),
        lax.psum_scatter(grad_vw, ("dp", "seq"), scatter_dimension=0, tiled=True),
        lax.psum_scatter(grad_outw, ("dp", "seq"), scatter_dimension=0, tiled=True),
        lax.psum_scatter(grad_upw, ("dp", "seq"), scatter_dimension=0, tiled=True),
        lax.psum_scatter(grad_downw, ("dp", "seq"), scatter_dimension=0, tiled=True),
        lax.psum_scatter(grad_gain_one, ("dp", "seq"), scatter_dimension=0, tiled=True),
        lax.psum_scatter(grad_gain_two, ("dp", "seq"), scatter_dimension=0, tiled=True),
    )
    return (
        layer_out,
        grad_input,
        totals[0],
        totals[1],
        totals[2],
        totals[3],
        totals[4],
        totals[5],
        totals[6],
        totals[7],
    )


def tables(length):
    places = np.arange(length, dtype=np.float32)[:, None]
    freqs = np.float32(10000.0) ** (-np.arange(40, dtype=np.float32) / np.float32(40))
    angles = places * freqs[None]
    wide = ((0, 0), (0, 48))
    moves = np.zeros((2, 4, 256, 256), np.float32)
    for g in range(4):
        for head in range(2):
            for entry in range(80):
                base = 80 * (2 * g + head) - 128 * g
                other = entry + 40 if entry < 40 else entry - 40
                moves[0, g, base + entry, 128 * head + entry] = 1.0
                moves[1, g, base + other, 128 * head + entry] = -1.0 if entry < 40 else 1.0
    cosine, sine = (np.pad(np.tile(f(angles), (1, 2)), wide) for f in (np.cos, np.sin))
    return jnp.asarray(cosine), jnp.asarray(sine), jnp.asarray(moves, jnp.bfloat16)


def fast_body(
    inputs, w_query, w_key, w_value, w_out, w_up, w_down, gain_attn, gain_mlp, pad_patches, cotangent
):
    moves = tables(1024)
    tile = jnp.pad(jnp.stack([gain_attn, gain_mlp]).astype(jnp.float32), ((0, 6), (0, 88)))
    weights, wide, tiles, x_own, dy_own, norm_t, heads, p, oh, hidden, layer, slope, turned, down = forward_part(
        inputs, cotangent, (w_query, w_key, w_value, w_out, w_up, w_down), tile, pad_patches, *moves
    )
    results = last_part(*backward_part(
        layer, hidden, slope, turned, down, dy_own, wide, weights, tiles, x_own, norm_t, heads, p, oh, *moves
    ))
    return results[:8] + (results[8].reshape(40), results[9].reshape(40))


def solution(mesh):
    placed = (
        P("dp", "seq", None),
        P(("dp", "seq"), None),
        P(("dp", "seq"), None),
        P(("dp", "seq"), None),
        P(("dp", "seq"), None),
        P(("dp", "seq"), None),
        P(("dp", "seq"), None),
        P(("dp", "seq")),
        P(("dp", "seq")),
        P("dp"),
        P("dp", "seq", None),
    )
    return jax.shard_map(
        fast_body if dict(mesh.shape) == {"dp": 8, "seq": 4} else body,
        mesh=mesh,
        in_specs=placed,
        out_specs=(
            P("dp", "seq", None),
            P("dp", "seq", None),
            P(("dp", "seq"), None),
            P(("dp", "seq"), None),
            P(("dp", "seq"), None),
            P(("dp", "seq"), None),
            P(("dp", "seq"), None),
            P(("dp", "seq"), None),
            P(("dp", "seq")),
            P(("dp", "seq")),
        ),
        check_vma=False,
    )
```
